768 devices in a mesh: gx: 8 (over y_lo, x), gy: 12 (over z), gz: 8 (over y_hi, core).
Axes of the slice: x: 4, y: 8 (y_hi: 4, y_lo: 2; y = y_hi * 2 + y_lo), z: 12, core: 2. Of those that a mesh axis runs over, the one named last changes fastest.
Arguments:
- adjoint_start: float32 [6, 64, 256, 1536], P(None, 'gz', 'gx', 'gy'), may hold values from -6 to 6
- eddy_visc: float32 [64, 256, 1536], P('gz', 'gx', 'gy'), may hold values from 0.4 to 1.2
- diag_coef: float32 [64, 256, 1536], P('gz', 'gx', 'gy'), may hold values from 6 to 8
- coupling: float32 [6, 6], replicated, may hold values from -5 to 5
- metric_terms: float32 [3, 6, 64, 256, 1536], P(None, None, 'gz', 'gx', 'gy'), may hold values from -0.3125 to 0.3125
- sample_cells: int32 [2048], replicated, may hold values from 0 to 393215
- sample_weights: float32 [2048], replicated, may hold values from -6 to 6
- face_codes: int32 [6], replicated, may hold values from 0 to 2
Outputs:
- adjoint_field: float32 [6, 64, 256, 1536], P(None, 'gz', 'gx', 'gy')
- height_grad: float32 [256, 1536], P('gx', ('gy', 'gz'))
The draws below stay inside these ranges and needn't reach their ends.
Inputs may be any that keep to these rules, and one draw needn't show every extreme that they name: `sample_cells`: each entry is x * 1536 + y for a sample column (x, y); a column may be sampled more than once. `face_codes`: faces in the order streamwise low, streamwise high, spanwise low, spanwise high, bottom, top; 0 fixed zero, 1 zero gradient, 2 mirrored with opposite sign.
All inputs are finite; a program needn't handle non-finite values.
Results may differ from the reference program's by a relative error of at most 0.00011.
Values sent between devices are 32-bit elements; how exact they have to be, the bound alone decides.
No kernel may reach another device: no remote copies, remote signals or barrier semaphores. Data moves between devices by JAX's collectives and lax.ppermute only.
A program may use at most 64 MiB of HBM per device.

```python
import math
import jax
import jax.numpy as jnp
from jax import lax

FIELDS = 6
NSAMP = 2048
NX = 256
NY = 1536
NZ = 64
HUB = 16


def with_ends(entries, rng, smallest, largest):
    place = [jax.random.randint(jax.random.fold_in(rng, axis), (), 0, length) for axis, length in enumerate(entries.shape)]
    longest = entries.shape.index(max(entries.shape))
    beside = place[:longest] + [(place[longest] + 1) % entries.shape[longest]] + place[longest + 1:]
    return entries.at[tuple(place)].set(smallest).at[tuple(beside)].set(largest)


def steps_of(stream_key, extent, shards, smallest, largest):
    def one(axis_at, blocks):
        steps = jax.random.uniform(jax.random.fold_in(jax.random.fold_in(stream_key, 6), axis_at), (blocks,), jnp.float32, smallest / len(shards), largest / len(shards))
        return jnp.repeat(jnp.exp(steps), extent[axis_at] // blocks).reshape((-1,) + (1,) * (len(extent) - axis_at - 1))

    factor_of = one(*shards[0])
    for cut in shards[1:]:
        factor_of = factor_of * one(*cut)
    return factor_of


def scatter_about(own_key, shape, spread, bound, split=(), kind=jnp.bfloat16):
    drawn = jax.random.normal(own_key, shape, jnp.float32) * spread
    if len(split) > 0:
        drawn = steps_of(own_key, shape, split, -0.22, 0.18) * drawn
    return jnp.clip(drawn, min=-bound, max=bound).astype(kind)


def setup_inputs(seed: int = 0) -> dict:
    seeds = jax.random.split(jax.random.key(seed), 9)
    adjoint_start = scatter_about(seeds[0], (FIELDS, NZ, NX, NY), 1.0, 6.0, ((1, 8), (2, 8), (3, 12)), jnp.float32)
    eddy_visc = jnp.clip(jnp.exp(math.log(1.2) - 1.0986123 * jax.random.uniform(seeds[1], (NZ, NX, NY), jnp.float32) ** steps_of(seeds[1], (NZ, NX, NY), ((0, 8), (1, 8), (2, 12)), -0.2, 0.2)), 0.4, 1.2)
    diag_coef = jnp.clip(6.0 + 2.0 * jax.random.uniform(seeds[2], (NZ, NX, NY), jnp.float32) ** steps_of(seeds[2], (NZ, NX, NY), ((0, 8), (1, 8), (2, 12)), -0.2, 0.2), 6.0, 8.0)
    coupling = scatter_about(seeds[3], (FIELDS, FIELDS), 1.0, 5.0, (), jnp.float32)
    metric_terms = scatter_about(seeds[4], (3, FIELDS, NZ, NX, NY), (FIELDS * NZ) ** -0.5, 0.3125, ((2, 8), (3, 8), (4, 12)), jnp.float32)
    sample_cells = with_ends(jax.random.randint(seeds[5], (NSAMP,), 0, NX * NY), jax.random.fold_in(seeds[5], 1), 0, (NX * NY) - 1).astype(jnp.int32)
    sample_weights = scatter_about(seeds[6], (NSAMP,), 2.0, 6.0, (), jnp.float32)
    face_codes = with_ends(jax.random.randint(seeds[7], (6,), 0, 3), jax.random.fold_in(seeds[7], 1), 0, 2).astype(jnp.int32)
    return dict(adjoint_start=adjoint_start, eddy_visc=eddy_visc, diag_coef=diag_coef, coupling=coupling, metric_terms=metric_terms, sample_cells=sample_cells, sample_weights=sample_weights, face_codes=face_codes)


relax_rate = 0.9


def face_factors(face_codes):
    return jnp.where(face_codes == 1, 1.0, jnp.where(face_codes == 2, -1.0, 0.0)).astype(jnp.float32)


def pad_faces(fluxes, factors):
    for along, low_face, high_face in ((2, 0, 1), (3, 2, 3), (1, 4, 5)):
        length = fluxes.shape[along]
        lower_face = factors[low_face] * lax.slice_in_dim(fluxes, 0, 1, axis=along)
        upper_face = factors[high_face] * lax.slice_in_dim(fluxes, length - 1, length, axis=along)
        fluxes = jnp.concatenate([lower_face, fluxes, upper_face], axis=along)
    return fluxes


def neighbor_sum(padded):
    total = padded[:, 2:, 1:-1, 1:-1] + padded[:, :-2, 1:-1, 1:-1]
    total = total + padded[:, 1:-1, 2:, 1:-1] + padded[:, 1:-1, :-2, 1:-1]
    total = total + padded[:, 1:-1, 1:-1, 2:] + padded[:, 1:-1, 1:-1, :-2]
    return total


def relax(adjoint, diag, source, beside, coupling):
    coupled = jnp.einsum("ef,ezxy->fzxy", coupling, adjoint, precision=lax.Precision.HIGHEST)
    remainder = source - (diag[None] * adjoint + coupled - beside)
    return adjoint + relax_rate * remainder / diag[None]


def reference(adjoint_start, eddy_visc, diag_coef, coupling, metric_terms, sample_cells, sample_weights, face_codes):
    factors = face_factors(face_codes)
    col_x = sample_cells // NY
    col_y = sample_cells % NY
    source = jnp.zeros((FIELDS, NZ, NX, NY), jnp.float32).at[0, HUB, col_x, col_y].add(sample_weights)
    adjoint = adjoint_start
    for sweep_no in range(2):
        fluxes = eddy_visc[None] * adjoint
        beside = neighbor_sum(pad_faces(fluxes, factors))
        adjoint = relax(adjoint, diag_coef, source, beside, coupling)
    level_frac = (jnp.arange(NZ, dtype=jnp.float32) + 0.5) / NZ
    level_weights = 1.0 - 0.5 * level_frac
    sums_list = []
    for term_no in range(3):
        column_terms = jnp.sum(metric_terms[term_no] * adjoint, axis=0)
        sums_list.append(jnp.tensordot(level_weights, column_terms, axes=1, precision=lax.Precision.HIGHEST))
    slope_xp = jnp.pad(sums_list[1], ((1, 1), (0, 0)))
    slope_yp = jnp.pad(sums_list[2], ((0, 0), (1, 1)))
    height_grad = sums_list[0] - 0.5 * (slope_xp[2:] - slope_xp[:-2]) - 0.5 * (slope_yp[:, 2:] - slope_yp[:, :-2])
    return adjoint, height_grad
```

```python
import functools

import jax
import jax.numpy as jnp
from jax import lax
from jax.experimental import pallas as pl
from jax.experimental.pallas import tpu as pltpu
from jax.sharding import PartitionSpec as P

relax_rate = 0.9
keep_rate = 0.1

FIELDS = 6
LEV = 8
ROWS = 32
COLS = 128
EXT = 40
EDDY, RATE, STRIP = 6, 7, 8
SLOT = 16

VM = pl.BlockSpec(memory_space=pltpu.VMEM)
SM = pl.BlockSpec(memory_space=pltpu.SMEM)
PARAMS = pltpu.CompilerParams(vmem_limit_bytes=32 * 1024 * 1024)


def roll(v, shift, axis):
    return pltpu.roll(v, shift % v.shape[axis], axis)


def iota(shape, axis):
    return lax.broadcasted_iota(jnp.int32, shape, axis)


def f32(*shape):
    return jax.ShapeDtypeStruct(shape, jnp.float32)


def pack_y(adj, eddy, diag, metric, own, to_right, to_left):
    lane = iota((8, COLS), 1)
    slot, j = lane // SLOT, lane % SLOT
    quad, jj = j // 4, j % 4

    def level(z, _):
        zg, zq = z // 4, z % 4
        for t in range(ROWS // 8):
            rows = pl.ds(8 * t, 8)
            c = jnp.zeros((8, COLS), jnp.float32)
            for p in range(8):
                if p < FIELDS:
                    v = adj[p, z, rows, :]
                elif p == EDDY:
                    v = eddy[z, rows, :]
                else:
                    v = relax_rate / diag[z, rows, :]
                c = jnp.where((slot == p) & (j >= 1) & (j <= 6), roll(v, SLOT * p + 4, 1), c)
                if p < FIELDS:
                    m = metric[0, p, z, rows, :]
                    c = jnp.where((slot == p) & (j >= 8) & (j <= 9), roll(m, SLOT * p + 9, 1), c)
            c8 = roll(c, 8, 1)
            own[z, rows, :] = jnp.where(j < 8, c, jnp.where(j >= 9, c8, 0.0))
            at = 4 * zq
            right = jnp.where(jj == 0, pltpu.roll(c, (at + 120) % 128, 1), pltpu.roll(c, at, 1))
            left = jnp.where(jj == 3, pltpu.roll(c, (at + 122) % 128, 1), pltpu.roll(c, (at + 124) % 128, 1))
            here = quad == zq
            to_right[zg, rows, :] = jnp.where(here, right, to_right[zg, rows, :])
            to_left[zg, rows, :] = jnp.where(here, left, to_left[zg, rows, :])
        return 0

    to_right[...] = jnp.zeros_like(to_right)
    to_left[...] = jnp.zeros_like(to_left)
    lax.fori_loop(0, LEV, level, 0)


def make_source(total_y, idx, cells, weights, src, acc):
    start_x, start_y = idx[0] * ROWS, idx[1] * COLS
    r = iota((48, COLS), 0)
    row_x = jnp.where(r < EXT - 5, r, r - EXT) + start_x
    row_x = jnp.where(r < EXT, row_x, -1)
    l = iota((2 * COLS, COLS), 0)
    j = l - COLS
    col_y = jnp.where((j >= 1) & (j <= 6), j - 4, j + (COLS - 12))
    col_y = jnp.where(l < COLS, l, col_y) + start_y
    col_y = jnp.where((l < COLS) | ((j >= 1) & (j <= 6)) | ((j >= 9) & (j <= 14)), col_y, -1)
    acc[...] = jnp.zeros_like(acc)

    def chunk(k, _):
        c = cells[pl.ds(k, 1), :]
        w = weights[pl.ds(k, 1), :]
        x = ((c.astype(jnp.float32) + 0.5) * (1.0 / total_y)).astype(jnp.int32)
        y = c - x * total_y
        high = w.astype(jnp.bfloat16).astype(jnp.float32)
        mid = (w - high).astype(jnp.bfloat16).astype(jnp.float32)
        low = w - high - mid
        hit = row_x == x
        parts = [jnp.where(hit, v, 0.0).astype(jnp.bfloat16) for v in (low, mid, high)]
        one = jnp.where(col_y == y, 1.0, 0.0).astype(jnp.bfloat16)
        acc[...] += lax.dot_general(
            jnp.concatenate(parts, 0), one, (((1,), (1,)), ((), ())), preferred_element_type=jnp.float32
        )
        return 0

    lax.fori_loop(0, 16, chunk, 0)
    total = acc[0:EXT, :] + acc[48 : 48 + EXT, :] + acc[96 : 96 + EXT, :]
    src[0] = total[:, :COLS]
    src[1] = total[:, COLS:]


def pack_x(own, from_left, from_right, adj, eddy, diag, metric, strip, to_low, to_high):
    j = iota((ROWS, COLS), 1) % SLOT

    def level(z, _):
        zg, at = z // 4, 4 * (z % 4)
        low = pltpu.roll(from_left[zg], (128 - at) % 128, 1)
        high = pltpu.roll(from_right[zg], (140 - at) % 128, 1)
        s = jnp.where(j < 4, low, jnp.where(j >= 12, high, own[z]))
        strip[z] = s
        for msg, a, near in ((to_low, 0, 0), (to_high, ROWS - 3, ROWS - 1)):
            for p in range(FIELDS):
                msg[z, pl.ds(3 * p, 3), :] = adj[p, z, a : a + 3, :]
                msg[z, pl.ds(26 + p, 1), :] = metric[0, p, z, near : near + 1, :]
            msg[z, 18:21, :] = eddy[z, a : a + 3, :]
            b = a if a == 0 else a + 1
            msg[z, 21:23, :] = relax_rate / diag[z, b : b + 2, :]
            msg[z, 23:26, :] = s[a : a + 3, :]
        return 0

    lax.fori_loop(0, LEV, level, 0)


def spread(s, plane):
    m = jnp.where(iota(s.shape, 1) // SLOT == plane, s, 0.0)
    m = m + roll(m, SLOT, 1)
    m = m + roll(m, 2 * SLOT, 1)
    return m + roll(m, 4 * SLOT, 1)


def face(codes, i):
    return jnp.where(codes[i] == 1, 1.0, jnp.where(codes[i] == 2, -1.0, 0.0)).astype(jnp.float32)


class Edges:
    def __init__(self, idx, codes):
        self.low_x, self.high_x = idx[0] == 0, idx[0] == idx[3] - 1
        self.low_y, self.high_y = idx[1] == 0, idx[1] == idx[4] - 1
        self.low_z, self.high_z = idx[2] == 0, idx[2] == idx[5] - 1
        self.factors = [face(codes, i) for i in range(6)]
        self.row = iota((8, COLS), 0)
        self.j = iota((EXT, COLS), 1) % SLOT

    def rows(self, v):
        t4 = v[32:40]
        t4 = jnp.where((self.row == 7) & self.low_x, self.factors[0] * roll(v[0:8], 7, 0), t4)
        t4 = jnp.where((self.row == 0) & self.high_x, self.factors[1] * roll(v[24:32], 1, 0), t4)
        return jnp.concatenate([v[0:32], t4], 0)

    def lanes(self, v):
        low = jnp.where((self.j == 3) & self.low_y, self.factors[2] * roll(v, -1, 1), v)
        return jnp.where((self.j == 12) & self.high_y, self.factors[3] * roll(v, 1, 1), low)

    def flux(self, p, v):
        if p == FIELDS:
            v = self.lanes(v)
        return self.rows(v)


def put_coupling(coup, mix):
    slot = iota((1, COLS), 1) // SLOT
    for d in range(8):
        v = jnp.zeros((1, COLS), jnp.float32)
        for f in range(FIELDS):
            e = (f + d) % 8
            if e < FIELDS:
                v = jnp.where(slot == f, coup[e, f], v)
        mix[d : d + 1, :] = v


def sweep(center, below, above, value, rate, strip_rate, coup, mix, src, flag, store):
    lane = iota((EXT, COLS), 1)
    strip_flux = center(FIELDS)
    for f in range(FIELDS):
        v = center(f)
        left = jnp.where(lane == 0, roll(strip_flux, -(SLOT * f + 3), 1), roll(v, 1, 1))
        right = jnp.where(lane == COLS - 1, roll(strip_flux, COLS - 1 - (SLOT * f + 12), 1), roll(v, -1, 1))
        beside = above(f) + below(f) + roll(v, -1, 0) + roll(v, 1, 0) + right + left
        coupled = coup[0, f] * value(0)
        for e in range(1, FIELDS):
            coupled = coupled + coup[e, f] * value(e)
        rest = beside - coupled
        if f == 0:
            rest = rest + flag * src[0]
        store(f, keep_rate * value(f) + rate * rest)
    v = strip_flux
    beside = above(FIELDS) + below(FIELDS) + roll(v, -1, 0) + roll(v, 1, 0) + roll(v, -1, 1) + roll(v, 1, 1)
    a = value(FIELDS)
    coupled = a * mix[0:1, :]
    for d in range(1, 8):
        coupled = coupled + roll(a, -SLOT * d, 1) * mix[d : d + 1, :]
    store(FIELDS, keep_rate * a + strip_rate * (beside - coupled + flag * src[1]))


def level_sums(z, start_z, total_z, field, strip, metric, metric_row, x, sums, out, zo):
    w = 1.0 - 0.5 * (((start_z + z).astype(jnp.float32) + 0.5) / total_z)
    s0 = s2 = s1 = halo = None
    for f in range(FIELDS):
        a = field(f)
        own = a[:ROWS]
        out[f, zo] = own
        terms = [metric[k, f, z] * own for k in range(3)] + [metric_row[f, z] * a[ROWS:]]
        if f == 0:
            s0, s1, s2, halo = terms
        else:
            s0, s1, s2, halo = s0 + terms[0], s1 + terms[1], s2 + terms[2], halo + terms[3]
    s = x[z, STRIP, :ROWS, :]
    j = iota((ROWS, COLS), 1) % SLOT
    m = jnp.where(j == 3, roll(s, 3, 1), jnp.where(j == 12, roll(s, -3, 1), 0.0))
    sums[0, :ROWS] += w * s0
    sums[1, :ROWS] += w * s1
    sums[1, ROWS:] += w * halo
    sums[2, :ROWS] += w * s2
    sums[3, :ROWS] += w * (m * strip[:ROWS])


def pack_z(idx, codes, strip, from_low, from_high, adj, eddy, diag, x, metric_row, msg_a, msg_b):
    def level(z, _):
        lo, hi = from_low.at[z], from_high.at[z]
        for p in range(9):
            at = 3 * p
            if p < FIELDS:
                v = adj[p, z]
            elif p == EDDY:
                v = eddy[z]
            elif p == RATE:
                v = relax_rate / diag[z]
            else:
                v = strip[z]
                at = 23
            x[z, p, :ROWS, :] = v
            x[z, p, ROWS:, :] = jnp.zeros((8, COLS), jnp.float32)
            if p == RATE:
                x[z, p, 32:34, :] = hi[21:23, :]
                x[z, p, 38:40, :] = lo[21:23, :]
            else:
                x[z, p, 32:35, :] = hi[at : at + 3, :]
                x[z, p, 37:40, :] = lo[at : at + 3, :]
        for f in range(FIELDS):
            metric_row[f, z] = jnp.zeros((8, COLS), jnp.float32)
            metric_row[f, z, 0:1, :] = hi[26 + f : 27 + f, :]
            metric_row[f, z, 7:8, :] = lo[26 + f : 27 + f, :]
        return 0

    lax.fori_loop(0, LEV, level, 0)
    edges = Edges(idx, codes)
    even = idx[2] % 2 == 0
    for msg, top in ((msg_a, even), (msg_b, jnp.logical_not(even))):
        near = jnp.where(top, LEV - 1, 0)
        next_ = jnp.where(top, LEV - 2, 1)
        for p in range(9):
            msg[p] = x[near, p]
        e = x[next_, EDDY]
        for f in range(FIELDS):
            msg[9 + f] = edges.flux(f, x[next_, f] * e)
        s = x[next_, STRIP]
        msg[15] = edges.flux(FIELDS, s * spread(s, EDDY))


def inner_levels(idx, codes, coup, x, metric, metric_row, src, f0, a1, f1, out, sums, mix, a2):
    edges = Edges(idx, codes)
    start_z, total_z = idx[2] * LEV, (idx[5] * LEV).astype(jnp.float32)
    put_coupling(coup, mix)

    def fluxes(z, _):
        e = x[z, EDDY]
        for f in range(FIELDS):
            f0[z, f] = edges.flux(f, x[z, f] * e)
        s = x[z, STRIP]
        f0[z, FIELDS] = edges.flux(FIELDS, s * spread(s, EDDY))
        return 0

    lax.fori_loop(0, LEV, fluxes, 0)

    def first(z, _):
        e = x[z, EDDY]
        s = x[z, STRIP]
        se = spread(s, EDDY)

        def store(p, v):
            a1[z - 1, p] = v
            f1[z - 1, p] = edges.flux(p, v * (se if p == FIELDS else e))

        sweep(
            lambda p: f0[z, p],
            lambda p: f0[z - 1, p],
            lambda p: f0[z + 1, p],
            lambda p: x[z, STRIP if p == FIELDS else p],
            x[z, RATE],
            spread(s, RATE),
            coup,
            mix,
            src,
            0.0,
            store,
        )
        return 0

    lax.fori_loop(1, LEV - 1, first, 0)
    sums[...] = jnp.zeros_like(sums)

    def second(z, _):
        def store(p, v):
            a2[p] = v

        sweep(
            lambda p: f1[z - 1, p],
            lambda p: f1[z - 2, p],
            lambda p: f1[z, p],
            lambda p: a1[z - 1, p],
            x[z, RATE],
            spread(x[z, STRIP], RATE),
            coup,
            mix,
            src,
            0.0,
            store,
        )
        level_sums(z, start_z, total_z, lambda f: a2[f], a2[FIELDS], metric, metric_row, x, sums, out, z - 2)
        return 0

    lax.fori_loop(2, LEV - 2, second, 0)


def outer_levels(
    idx, codes, coup, x, from_a, from_b, metric, metric_row, src, f0, a1, f1, inner_out, inner_sums,
    out, share, sums, mix, a2, halo, fh, ah, gh, an, gn,
):
    edges = Edges(idx, codes)
    start_z, total_z = idx[2] * LEV, (idx[5] * LEV).astype(jnp.float32)
    hub = idx[5] * LEV // 4 - start_z
    put_coupling(coup, mix)
    sums[...] = inner_sums[...]
    halo[0] = from_a[...]
    halo[1] = from_b[...]
    for f in range(FIELDS):
        for z in range(2, LEV - 2):
            out[f, z] = inner_out[f, z - 2]
    even = idx[2] % 2 == 0

    def flag_of(z):
        return jnp.where(z == hub, 1.0, 0.0).astype(jnp.float32)

    def side(n, _):
        top = jnp.logical_xor(even, n == 1)
        near = jnp.where(top, LEV - 1, 0)
        next_ = jnp.where(top, LEV - 2, 1)
        third = jnp.where(top, LEV - 3, 2)
        over = jnp.where(top, LEV, -1)
        ghost = jnp.where(top, edges.high_z, edges.low_z)
        factor = jnp.where(top, edges.factors[5], edges.factors[4])
        e = halo[n, EDDY]
        s = halo[n, STRIP]
        se = spread(s, EDDY)
        for p in range(FIELDS + 1):
            v = s * se if p == FIELDS else halo[n, p] * e
            fh[p] = jnp.where(ghost, factor * f0[near, p], edges.flux(p, v))

        def store_near(p, v):
            an[p] = v
            e = spread(x[near, STRIP], EDDY) if p == FIELDS else x[near, EDDY]
            gn[p] = edges.flux(p, v * e)

        sweep(
            lambda p: f0[near, p],
            lambda p: fh[p],
            lambda p: f0[next_, p],
            lambda p: x[near, STRIP if p == FIELDS else p],
            x[near, RATE],
            spread(x[near, STRIP], RATE),
            coup,
            mix,
            src,
            flag_of(near),
            store_near,
        )

        def store_over(p, v):
            gh[p] = jnp.where(ghost, factor * gn[p], edges.flux(p, v * (se if p == FIELDS else e)))

        sweep(
            lambda p: fh[p],
            lambda p: halo[n, 9 + p],
            lambda p: f0[near, p],
            lambda p: halo[n, STRIP if p == FIELDS else p],
            halo[n, RATE],
            spread(s, RATE),
            coup,
            mix,
            src,
            flag_of(over),
            store_over,
        )

        def store_last(p, v):
            a2[p] = v

        def last(z, *levels):
            sweep(
                *levels, x[z, RATE], spread(x[z, STRIP], RATE), coup, mix, src, flag_of(z), store_last
            )
            level_sums(z, start_z, total_z, lambda f: a2[f], a2[FIELDS], metric, metric_row, x, sums, out, z)

        last(near, lambda p: gn[p], lambda p: gh[p], lambda p: f1[next_ - 1, p], lambda p: an[p])
        last(next_, lambda p: f1[next_ - 1, p], lambda p: gn[p], lambda p: f1[third - 1, p], lambda p: a1[next_ - 1, p])
        return 0

    lax.fori_loop(0, 2, side, 0)
    s1 = sums[1]
    stream = roll(s1, -1, 0)[:ROWS] - roll(s1, 1, 0)[:ROWS]
    t = sums[3, :ROWS]
    t = t + roll(t, 4 * SLOT, 1)
    t = t + roll(t, 2 * SLOT, 1)
    t = t + roll(t, SLOT, 1)
    s2 = sums[2, :ROWS]
    lane = iota((ROWS, COLS), 1)
    right = jnp.where(lane == COLS - 1, roll(t, 3, 1), roll(s2, -1, 1))
    left = jnp.where(lane == 0, roll(t, -3, 1), roll(s2, 1, 1))
    share[...] = (sums[0, :ROWS] - 0.5 * stream - 0.5 * (right - left)).T


def add_shares(parts, out):
    width = out.shape[1]
    total = parts[0:width, :]
    for i in range(1, COLS // width):
        total = total + parts[width * i : width * (i + 1), :]
    out[...] = total.T


def call(body, outs, ins, scratch=(), flops=1000000):
    return pl.pallas_call(
        body,
        out_shape=outs,
        in_specs=ins,
        out_specs=jax.tree.map(lambda _: VM, outs),
        scratch_shapes=list(scratch),
        compiler_params=PARAMS,
        cost_estimate=pl.CostEstimate(flops=flops, bytes_accessed=1 << 20, transcendentals=0),
    )


def local(adjoint_start, eddy_visc, diag_coef, coupling, metric_terms, sample_cells, sample_weights, face_codes):
    index = [lax.axis_index(a) for a in ("gx", "gy", "gz")]
    count = [lax.axis_size(a) for a in ("gx", "gy", "gz")]
    idx = jnp.stack(index + [jnp.int32(c) for c in count]).astype(jnp.int32)

    def shift(v, axis, step):
        n = lax.axis_size(axis)
        return lax.ppermute(v, axis, [(i, i + step) for i in range(n) if 0 <= i + step < n])

    def trade(v, axis, first):
        n = lax.axis_size(axis)
        pairs = [(i, i + 1) for i in range(first, n - 1, 2)]
        return lax.ppermute(v, axis, pairs + [(b, a) for a, b in pairs])

    def buf(*shape):
        return pltpu.VMEM(shape, jnp.float32)

    own, to_right, to_left = call(
        pack_y,
        (f32(LEV, ROWS, COLS), f32(2, ROWS, COLS), f32(2, ROWS, COLS)),
        [VM] * 4,
    )(adjoint_start, eddy_visc, diag_coef, metric_terms[2:3])
    from_left = shift(to_right, "gy", 1)
    from_right = shift(to_left, "gy", -1)
    src = call(functools.partial(make_source, COLS * count[1]), f32(2, EXT, COLS), [SM, VM, VM], [buf(144, 2 * COLS)])(
        idx, sample_cells.reshape(16, 128), sample_weights.reshape(16, 128)
    )
    strip, to_low, to_high = call(
        pack_x,
        (f32(LEV, ROWS, COLS), f32(LEV, ROWS, COLS), f32(LEV, ROWS, COLS)),
        [VM] * 7,
    )(own, from_left, from_right, adjoint_start, eddy_visc, diag_coef, metric_terms[1:2])
    from_low = shift(to_high, "gx", 1)
    from_high = shift(to_low, "gx", -1)
    x, metric_row, msg_a, msg_b = call(
        pack_z,
        (f32(LEV, 9, EXT, COLS), f32(FIELDS, LEV, 8, COLS), f32(16, EXT, COLS), f32(16, EXT, COLS)),
        [SM, SM] + [VM] * 6,
    )(idx, face_codes, strip, from_low, from_high, adjoint_start, eddy_visc, diag_coef)
    from_b = trade(msg_b, "gz", 1)
    from_a = trade(msg_a, "gz", 0)
    f0, a1, f1, inner_out, inner_sums = call(
        inner_levels,
        (
            f32(LEV, 7, EXT, COLS),
            f32(LEV - 2, 7, EXT, COLS),
            f32(LEV - 2, 7, EXT, COLS),
            f32(FIELDS, LEV - 4, ROWS, COLS),
            f32(4, EXT, COLS),
        ),
        [SM, SM, SM] + [VM] * 4,
        [buf(8, COLS), buf(7, EXT, COLS)],
    )(idx, face_codes, coupling, x, metric_terms, metric_row, src)
    adjoint, share = call(
        outer_levels,
        (f32(FIELDS, LEV, ROWS, COLS), f32(COLS, ROWS)),
        [SM, SM, SM] + [VM] * 11,
        [buf(4, EXT, COLS), buf(8, COLS), buf(7, EXT, COLS), buf(2, 16, EXT, COLS)] + [buf(7, EXT, COLS)] * 5,
    )(
        idx, face_codes, coupling, x, from_a, from_b, metric_terms, metric_row, src, f0, a1, f1, inner_out, inner_sums
    )
    parts = lax.all_to_all(share, "gz", 0, 0, tiled=True)
    height_grad = call(add_shares, f32(ROWS, COLS // count[2]), [VM])(parts)
    return (adjoint, height_grad)


def solution(mesh):
    return jax.shard_map(
        local,
        mesh=mesh,
        in_specs=(
            P(None, "gz", "gx", "gy"),
            P("gz", "gx", "gy"),
            P("gz", "gx", "gy"),
            P(),
            P(None, None, "gz", "gx", "gy"),
            P(),
            P(),
            P(),
        ),
        out_specs=(P(None, "gz", "gx", "gy"), P("gx", ("gy", "gz"))),
        check_vma=False,
    )
```

```python
import functools

import jax
import jax.numpy as jnp
from jax import lax
from jax.experimental import pallas as pl
from jax.experimental.pallas import tpu as pltpu
from jax.sharding import PartitionSpec as P

relax_rate = 0.9
keep_rate = 0.1

FIELDS = 6
LEV = 8
ROWS = 32
COLS = 128
EXT = 40
EDDY, RATE, STRIP = 6, 7, 8
SLOT = 16

VM = pl.BlockSpec(memory_space=pltpu.VMEM)
SM = pl.BlockSpec(memory_space=pltpu.SMEM)
HB = pl.BlockSpec(memory_space=pltpu.HBM)
PARAMS = pltpu.CompilerParams(vmem_limit_bytes=16 * 1024 * 1024)


def roll(v, shift, axis):
    return pltpu.roll(v, shift % v.shape[axis], axis)


def iota(shape, axis):
    return lax.broadcasted_iota(jnp.int32, shape, axis)


def f32(*shape):
    return jax.ShapeDtypeStruct(shape, jnp.float32)


def pack_y(adj, eddy, diag, metric, *rest):
    own, to_right, to_left, adj_buf, eddy_buf, diag_buf, metric_buf, sems = rest[-8:]
    half = LEV // 2
    copies = []
    for h in range(2):
        at = pl.ds(h * half, half)
        pairs = (
            (adj.at[:, at], adj_buf.at[:, at]),
            (eddy.at[at], eddy_buf.at[at]),
            (diag.at[at], diag_buf.at[at]),
            (metric.at[2, :, at], metric_buf.at[:, at]),
        )
        copies.append([pltpu.make_async_copy(a, b, sems.at[h, i]) for i, (a, b) in enumerate(pairs)])
    for c in copies[0] + copies[1]:
        c.start()
    lane = iota((8, COLS), 1)
    slot, j = lane // SLOT, lane % SLOT
    quad, jj = j // 4, j % 4
    edge_at = [(slot == p) & (j >= 1) & (j <= 6) for p in range(8)]
    metric_at = [(slot == p) & (j >= 8) & (j <= 9) for p in range(FIELDS)]
    for zg in range(2):
        for c in copies[zg]:
            c.wait()
        for t in range(ROWS // 8):
            rows = pl.ds(8 * t, 8)
            right = left = jnp.zeros((8, COLS), jnp.float32)
            for zq in range(4):
                z = 4 * zg + zq
                c = jnp.zeros((8, COLS), jnp.float32)
                for p in range(8):
                    if p < FIELDS:
                        v = adj_buf[p, z, rows, :]
                    elif p == EDDY:
                        v = eddy_buf[z, rows, :]
                    else:
                        v = relax_rate / diag_buf[z, rows, :]
                    c = jnp.where(edge_at[p], roll(v, SLOT * p + 4, 1), c)
                    if p < FIELDS:
                        c = jnp.where(metric_at[p], roll(metric_buf[p, z, rows, :], SLOT * p + 9, 1), c)
                own[z, rows, :] = jnp.where(j < 8, c, jnp.where(j >= 9, roll(c, 8, 1), 0.0))
                at = 4 * zq
                here = quad == zq
                right = jnp.where(here, jnp.where(jj == 0, roll(c, at - 8, 1), roll(c, at, 1)), right)
                left = jnp.where(here, jnp.where(jj == 3, roll(c, at - 6, 1), roll(c, at - 4, 1)), left)
            to_right[zg, rows, :] = right
            to_left[zg, rows, :] = left


def make_source(total_y, idx, cells, weights, src):
    start_x, start_y = idx[0] * ROWS, idx[1] * COLS
    r = iota((48, COLS), 0)
    row_x = jnp.where(r < EXT - 5, r, r - EXT) + start_x
    row_x = jnp.where(r < EXT, row_x, -1)
    l = iota((2 * COLS, COLS), 0)
    j = l - COLS
    col_y = jnp.where((j >= 1) & (j <= 6), j - 4, j + (COLS - 12))
    col_y = jnp.where(l < COLS, l, col_y) + start_y
    col_y = jnp.where((l < COLS) | ((j >= 1) & (j <= 6)) | ((j >= 9) & (j <= 14)), col_y, -1)
    acc = jnp.zeros((144, 2 * COLS), jnp.float32)
    for k in range(0, 16, 2):
        left, one = [], []
        for q in (k, k + 1):
            c = cells[q : q + 1, :]
            w = weights[q : q + 1, :]
            x = ((c.astype(jnp.float32) + 0.5) * (1.0 / total_y)).astype(jnp.int32)
            y = c - x * total_y
            high = w.astype(jnp.bfloat16).astype(jnp.float32)
            mid = (w - high).astype(jnp.bfloat16).astype(jnp.float32)
            low = w - high - mid
            hit = row_x == x
            left.append(jnp.concatenate([jnp.where(hit, v, 0.0).astype(jnp.bfloat16) for v in (low, mid, high)], 0))
            one.append(jnp.where(col_y == y, 1.0, 0.0).astype(jnp.bfloat16))
        acc = acc + lax.dot_general(
            jnp.concatenate(left, 1),
            jnp.concatenate(one, 1),
            (((1,), (1,)), ((), ())),
            preferred_element_type=jnp.float32,
        )
    total = acc[0:EXT, :] + acc[48 : 48 + EXT, :] + acc[96 : 96 + EXT, :]
    src[0] = total[:, :COLS]
    src[1] = total[:, COLS:]


HIGH_AT = [0, 3, 6, 9, 12, 15, 18, 21, 23]
LOW_AT = [6 + a for a in HIGH_AT]
HIGH_METRIC, LOW_METRIC = 26, 0


def pack_x(src, own, from_left, from_right, adj, eddy, diag, metric, strip, to_low, to_high):
    j = iota((ROWS, COLS), 1) % SLOT
    for z in range(LEV):
        zg, at = z // 4, 4 * (z % 4)
        low = roll(from_left[zg], -at, 1)
        high = roll(from_right[zg], 12 - at, 1)
        s = jnp.where(j < 4, low, jnp.where(j >= 12, high, own[z]))
        strip[z] = s
        sides = ((to_low, 0, 0, 0, HIGH_AT, HIGH_METRIC), (to_high, ROWS - 3, ROWS - 2, ROWS - 1, LOW_AT, LOW_METRIC))
        for msg, a, b, near, at, metric_at in sides:
            for p in range(FIELDS):
                msg[z, at[p] : at[p] + 3, :] = adj[p, z, a : a + 3, :]
                msg[z, metric_at + p : metric_at + p + 1, :] = metric[1, p, z, near : near + 1, :]
            msg[z, at[EDDY] : at[EDDY] + 3, :] = eddy[z, a : a + 3, :]
            msg[z, at[RATE] : at[RATE] + 2, :] = relax_rate / diag[z, b : b + 2, :]
            msg[z, at[STRIP] : at[STRIP] + 3, :] = s[a : a + 3, :]


def lanes_of(v, plane):
    return jnp.take_along_axis(v, iota(v.shape, 1) % SLOT + SLOT * plane, axis=1)


def face(codes, i):
    return jnp.where(codes[i] == 1, 1.0, jnp.where(codes[i] == 2, -1.0, 0.0)).astype(jnp.float32)


class Edges:
    def __init__(self, info):
        self.low_x, self.high_x = info[0] == 0, info[0] == info[3] - 1
        self.low_y, self.high_y = info[1] == 0, info[1] == info[4] - 1
        self.low_z, self.high_z = info[2] == 0, info[2] == info[5] - 1
        self.factors = [face(info, 6 + i) for i in range(6)]
        row, j = iota((8, COLS), 0), iota((EXT, COLS), 1) % SLOT
        self.row_low, self.row_high = (row == 7) & self.low_x, (row == 0) & self.high_x
        self.j = j
        self.ghost_low, self.ghost_high = (j == 3) & self.low_y, (j == 12) & self.high_y
        self.own_low, self.own_high = (j == 4) & self.low_y, (j == 11) & self.high_y

    def flux(self, v):
        t4 = v[32:40]
        t4 = jnp.where(self.row_low, self.factors[0] * roll(v[0:8], 7, 0), t4)
        t4 = jnp.where(self.row_high, self.factors[1] * roll(v[24:32], 1, 0), t4)
        return jnp.concatenate([v[0:32], t4], 0)


def put_coupling(coup, mix):
    slot = iota((1, COLS), 1) // SLOT
    for e in range(FIELDS):
        v = jnp.zeros((1, COLS), jnp.float32)
        for f in range(FIELDS):
            v = jnp.where(slot == f, coup[e, f], v)
        mix[e : e + 1, :] = v


def sweep(edges, center, vertical, value, rate, strip_rate, coup, mix, store, src=None, flag=None):
    lane = iota((EXT, COLS), 1)
    f2, f3 = edges.factors[2], edges.factors[3]
    v = center(FIELDS)
    up, down = roll(v, 1, 1), roll(v, -1, 1)
    fixed = jnp.where(edges.ghost_low, f2 * down, jnp.where(edges.ghost_high, f3 * up, v))
    both = jnp.where(edges.j == 3, fixed, roll(fixed, -10, 1))
    beside = vertical(FIELDS) + roll(v, -1, 0) + roll(v, 1, 0)
    beside = beside + jnp.where(edges.own_low, f2 * v, up) + jnp.where(edges.own_high, f3 * v, down)
    a = value(FIELDS)
    coupled = lanes_of(a, 0) * mix[0:1, :]
    for e in range(1, FIELDS):
        coupled = coupled + lanes_of(a, e) * mix[e : e + 1, :]
    rest = beside - coupled
    if src is not None:
        rest = rest + flag * src[1]
    store(FIELDS, keep_rate * a + strip_rate * rest)
    for f in range(FIELDS):
        v = center(f)
        end = roll(both, -(SLOT * f + 3), 1)
        left = jnp.where(lane == 0, end, roll(v, 1, 1))
        right = jnp.where(lane == COLS - 1, end, roll(v, -1, 1))
        beside = vertical(f) + roll(v, -1, 0) + roll(v, 1, 0) + right + left
        coupled = coup[0, f] * value(0)
        for e in range(1, FIELDS):
            coupled = coupled + coup[e, f] * value(e)
        rest = beside - coupled
        if f == 0 and src is not None:
            rest = rest + flag * src[0]
        store(f, keep_rate * value(f) + rate * rest)


def level_sums(z, info, field, edge_strip, strip, metric, metric_row, sums, out, zo):
    total_z = (info[5] * LEV).astype(jnp.float32)
    w = 1.0 - 0.5 * (((info[2] * LEV + z).astype(jnp.float32) + 0.5) / total_z)
    totals = None
    for f in range(FIELDS):
        a = field(f)
        own = a[:ROWS]
        out[f, zo] = own
        terms = [metric[k, f, z] * own for k in range(3)] + [metric_row[f, z] * a[ROWS:]]
        totals = terms if f == 0 else [s + t for s, t in zip(totals, terms)]
    s = strip[z, :ROWS]
    j = iota((ROWS, COLS), 1) % SLOT
    m = jnp.where(j == 3, roll(s, 3, 1), jnp.where(j == 12, roll(s, -3, 1), 0.0))
    sums[0, :ROWS] += w * totals[0]
    sums[1, :ROWS] += w * totals[1]
    sums[1, ROWS:] += w * totals[3]
    sums[2, :ROWS] += w * totals[2]
    sums[3, :ROWS] += w * (m * edge_strip[:ROWS])


def pack_z(info, strip, from_low, from_high, adj, eddy, diag, halo, metric_row, msg_a, msg_b):
    row = iota((8, COLS), 0)
    for z in range(LEV):
        for p in range(9):
            at = 2 if p == RATE else 3
            above = from_high[z, HIGH_AT[p] : HIGH_AT[p] + 8, :]
            start = LOW_AT[p] - (8 - at)
            halo[z, p] = jnp.where(row < 4, above, from_low[z, start : start + 8, :])
        for f in range(FIELDS):
            above = jnp.broadcast_to(from_high[z, HIGH_METRIC + f : HIGH_METRIC + f + 1, :], (8, COLS))
            below = jnp.broadcast_to(from_low[z, LOW_METRIC + f : LOW_METRIC + f + 1, :], (8, COLS))
            metric_row[f, z] = jnp.where(row < 4, above, below)
    edges = Edges(info)
    even = info[2] % 2 == 0

    def plane(z, p):
        own = adj[p, z] if p < FIELDS else eddy[z] if p == EDDY else relax_rate / diag[z] if p == RATE else strip[z]
        return jnp.concatenate([own, halo[z, p]], 0)

    for msg, top in ((msg_a, even), (msg_b, jnp.logical_not(even))):
        near = jnp.where(top, LEV - 1, 0)
        next_ = jnp.where(top, LEV - 2, 1)
        for p in range(9):
            msg[p] = plane(near, p)
        e = plane(next_, EDDY)
        for f in range(FIELDS):
            msg[9 + f] = edges.flux(plane(next_, f) * e)
        s = plane(next_, STRIP)
        msg[15] = edges.flux(s * lanes_of(s, EDDY))


def inner_levels(
    info, coup, adj, eddy, diag, strip, halo, metric, metric_row, src,
    f0, near1, next2, f1, rates, edge_eddy, edge_rate, out, sums, mix, a1, a2,
):
    edges = Edges(info)
    put_coupling(coup, mix)
    hub = info[5] * LEV // 4 - info[2] * LEV
    flag = jnp.where(hub == 0, 1.0, 0.0).astype(jnp.float32)

    def value(z, p):
        own = adj[p, z] if p < FIELDS else strip[z]
        return jnp.concatenate([own, halo[z, STRIP if p == FIELDS else p]], 0)

    def eddies(z):
        return jnp.concatenate([eddy[z], halo[z, EDDY]], 0)

    for z in range(LEV):
        rates[z] = jnp.concatenate([relax_rate / diag[z], halo[z, RATE]], 0)
        s = value(z, FIELDS)
        edge_eddy[z] = lanes_of(s, EDDY)
        edge_rate[z] = lanes_of(s, RATE)
        e = eddies(z)
        for f in range(FIELDS):
            f0[z, f] = edges.flux(value(z, f) * e)
        f0[z, FIELDS] = edges.flux(s * edge_eddy[z])

    def around(array, z):
        return lambda p: array[z - 1, p] + array[z + 1, p]

    def first(z, vertical, store, **more):
        sweep(edges, lambda p: f0[z, p], vertical, lambda p: value(z, p), rates[z], edge_rate[z], coup, mix, store, **more)

    def store_near(i):
        def store(p, v):
            near1[i, p] = v

        return store

    def store_inner(z):
        def store(p, v):
            a1[z, p] = v
            f1[z, p] = edges.flux(v * (edge_eddy[z] if p == FIELDS else eddies(z)))

        return store

    first(0, lambda p: f0[1, p], store_near(0), src=src, flag=flag)
    first(LEV - 1, lambda p: f0[LEV - 2, p], store_near(1))
    for z in range(1, LEV - 1):
        first(z, around(f0, z), store_inner(z))
    sums[...] = jnp.zeros_like(sums)

    def second(z, vertical, store):
        sweep(edges, lambda p: f1[z, p], vertical, lambda p: a1[z, p], rates[z], edge_rate[z], coup, mix, store)

    def store_next(i):
        def store(p, v):
            next2[i, p] = v

        return store

    def store_last(z):
        def store(p, v):
            a2[z, p] = v

        return store

    second(1, lambda p: f1[2, p], store_next(0))
    second(LEV - 2, lambda p: f1[LEV - 3, p], store_next(1))
    for z in range(2, LEV - 2):
        second(z, around(f1, z), store_last(z))
        level_sums(z, info, lambda f: a2[z, f], a2[z, FIELDS], strip, metric, metric_row, sums, out, z - 2)


def outer_levels(
    info, coup, eddy, strip, halo_rows, from_a, from_b, metric, metric_row, src,
    f0, near1, next2, f1, rates, edge_eddy, edge_rate, inner_out, inner_sums,
    out, share, sums, mix, fh, ah, gh, an, gn, a2,
):
    edges = Edges(info)
    hub = info[5] * LEV // 4 - info[2] * LEV
    put_coupling(coup, mix)
    sums[...] = inner_sums[...]
    for f in range(FIELDS):
        for z in range(2, LEV - 2):
            out[f, z] = inner_out[f, z - 2]
    even = info[2] % 2 == 0

    def flag_of(z):
        return jnp.where(z == hub, 1.0, 0.0).astype(jnp.float32)

    for n, msg in enumerate((from_a, from_b)):
        top = even if n == 0 else jnp.logical_not(even)
        i = jnp.where(top, 1, 0)
        near = jnp.where(top, LEV - 1, 0)
        next_ = jnp.where(top, LEV - 2, 1)
        over = jnp.where(top, LEV, -1)
        ghost = jnp.where(top, edges.high_z, edges.low_z)
        factor = jnp.where(top, edges.factors[5], edges.factors[4])
        eddy_over = msg[EDDY]
        s = msg[STRIP]
        edge_eddy_over = lanes_of(s, EDDY)
        eddy_near = jnp.concatenate([eddy[near], halo_rows[near, EDDY]], 0)
        for p in range(FIELDS + 1):
            v = s * edge_eddy_over if p == FIELDS else msg[p] * eddy_over
            v = jnp.where(ghost, factor * f0[near, p], edges.flux(v))
            fh[n, p] = v
            r, e = (edge_rate[near], edge_eddy[near]) if p == FIELDS else (rates[near], eddy_near)
            v = near1[i, p] + r * v
            an[n, p] = v
            gn[n, p] = edges.flux(v * e)

        def store_over(p, v):
            v = edges.flux(v * (edge_eddy_over if p == FIELDS else eddy_over))
            gh[n, p] = jnp.where(ghost, factor * gn[n, p], v)

        sweep(
            edges,
            lambda p: fh[n, p],
            lambda p: msg[9 + p] + f0[near, p],
            lambda p: msg[STRIP if p == FIELDS else p],
            msg[RATE],
            lanes_of(s, RATE),
            coup,
            mix,
            store_over,
            src,
            flag_of(over),
        )

        def after(p):
            r = edge_rate[next_] if p == FIELDS else rates[next_]
            return next2[i, p] + r * gn[n, p]

        level_sums(next_, info, after, after(FIELDS), strip, metric, metric_row, sums, out, next_)

        def store_last(p, v):
            a2[n, p] = v

        sweep(
            edges,
            lambda p: gn[n, p],
            lambda p: gh[n, p] + f1[next_, p],
            lambda p: an[n, p],
            rates[near],
            edge_rate[near],
            coup,
            mix,
            store_last,
            src,
            flag_of(near),
        )
        level_sums(near, info, lambda f: a2[n, f], a2[n, FIELDS], strip, metric, metric_row, sums, out, near)

    s1 = sums[1]
    stream = roll(s1, -1, 0)[:ROWS] - roll(s1, 1, 0)[:ROWS]
    t = sums[3, :ROWS]
    t = t + roll(t, 4 * SLOT, 1)
    t = t + roll(t, 2 * SLOT, 1)
    t = t + roll(t, SLOT, 1)
    s2 = sums[2, :ROWS]
    lane = iota((ROWS, COLS), 1)
    right = jnp.where(lane == COLS - 1, roll(t, 3, 1), roll(s2, -1, 1))
    left = jnp.where(lane == 0, roll(t, -3, 1), roll(s2, 1, 1))
    total = sums[0, :ROWS] - 0.5 * stream - 0.5 * (right - left)
    turned = jnp.concatenate([total, jnp.zeros((COLS - ROWS, COLS), jnp.float32)], 0).T
    count, width = share.shape[0], COLS // share.shape[0]
    group = iota((8, COLS), 1) // ROWS
    for k in range(count):
        v = turned[width * k : width * k + 8]
        for q in range(1, width // 8):
            v = jnp.where(group == q, roll(turned[width * k + 8 * q : width * k + 8 * q + 8], ROWS * q, 1), v)
        share[k] = v


def add_shares(parts, out):
    total = parts[0]
    for i in range(1, parts.shape[0]):
        total = total + parts[i]
    for q in range(out.shape[0] // 8):
        out[8 * q : 8 * q + 8, :] = roll(total, -ROWS * q, 1)[:, :ROWS]


def call(body, outs, ins, scratch=(), flops=1000000):
    return pl.pallas_call(
        body,
        out_shape=outs,
        in_specs=ins,
        out_specs=jax.tree.map(lambda _: VM, outs),
        scratch_shapes=list(scratch),
        compiler_params=PARAMS,
        cost_estimate=pl.CostEstimate(flops=flops, bytes_accessed=1 << 20, transcendentals=0),
    )


def local(adjoint_start, eddy_visc, diag_coef, coupling, metric_terms, sample_cells, sample_weights, face_codes):
    index = [lax.axis_index(a) for a in ("gx", "gy", "gz")]
    count = [lax.axis_size(a) for a in ("gx", "gy", "gz")]
    place = jnp.stack(index + [jnp.int32(c) for c in count]).astype(jnp.int32)
    info = jnp.concatenate([place, face_codes])
    cells, weights = sample_cells.reshape(16, 128), sample_weights.reshape(16, 128)

    def shift(v, axis, step):
        n = lax.axis_size(axis)
        return lax.ppermute(v, axis, [(i, i + step) for i in range(n) if 0 <= i + step < n])

    def trade(v, axis, first):
        n = lax.axis_size(axis)
        pairs = [(i, i + 1) for i in range(first, n - 1, 2)]
        return lax.ppermute(v, axis, pairs + [(b, a) for a, b in pairs])

    def buf(*shape):
        return pltpu.VMEM(shape, jnp.float32)

    level = (LEV, ROWS, COLS)
    own, to_right, to_left = call(
        pack_y,
        (f32(*level), f32(2, ROWS, COLS), f32(2, ROWS, COLS)),
        [HB] * 4 + [VM, VM, SM],
        [buf(FIELDS, *level), buf(*level), buf(*level), buf(FIELDS, *level), pltpu.SemaphoreType.DMA((2, 4))],
    )(adjoint_start, eddy_visc, diag_coef, metric_terms, cells, weights, coupling)
    from_left = shift(to_right, "gy", 1)
    from_right = shift(to_left, "gy", -1)
    src = call(functools.partial(make_source, COLS * count[1]), f32(2, EXT, COLS), [SM, VM, VM])(info, cells, weights)
    strip, to_low, to_high = call(pack_x, (f32(*level),) * 3, [VM] * 8)(
        src, own, from_left, from_right, adjoint_start, eddy_visc, diag_coef, metric_terms
    )
    from_low = shift(to_high, "gx", 1)
    from_high = shift(to_low, "gx", -1)
    halo, metric_row, msg_a, msg_b = call(
        pack_z,
        (f32(LEV, 9, 8, COLS), f32(FIELDS, LEV, 8, COLS), f32(16, EXT, COLS), f32(16, EXT, COLS)),
        [SM] + [VM] * 6,
    )(info, strip, from_low, from_high, adjoint_start, eddy_visc, diag_coef)
    from_b = trade(msg_b, "gz", 1)
    from_a = trade(msg_a, "gz", 0)
    ext = (EXT, COLS)
    *inner, inner_out, inner_sums = call(
        inner_levels,
        (
            f32(LEV, 7, *ext),
            f32(2, 7, *ext),
            f32(2, 7, *ext),
            f32(LEV, 7, *ext),
            f32(LEV, *ext),
            f32(LEV, *ext),
            f32(LEV, *ext),
            f32(FIELDS, LEV - 4, ROWS, COLS),
            f32(4, *ext),
        ),
        [SM, SM] + [VM] * 8,
        [buf(8, COLS), buf(LEV, 7, *ext), buf(LEV, 7, *ext)],
    )(info, coupling, adjoint_start, eddy_visc, diag_coef, strip, halo, metric_terms, metric_row, src)
    adjoint, share = call(
        outer_levels,
        (f32(FIELDS, *level), f32(count[2], 8, COLS)),
        [SM, SM] + [VM] * 17,
        [buf(4, *ext), buf(8, COLS)] + [buf(2, 7, *ext)] * 6,
    )(info, coupling, eddy_visc, strip, halo, from_a, from_b, metric_terms, metric_row, src, *inner, inner_out, inner_sums)
    parts = lax.all_to_all(share, "gz", 0, 0, tiled=True)
    height_grad = call(add_shares, f32(COLS // count[2], ROWS), [VM])(parts).T
    return (adjoint, height_grad)


def solution(mesh):
    return jax.shard_map(
        local,
        mesh=mesh,
        in_specs=(
            P(None, "gz", "gx", "gy"),
            P("gz", "gx", "gy"),
            P("gz", "gx", "gy"),
            P(),
            P(None, None, "gz", "gx", "gy"),
            P(),
            P(),
            P(),
        ),
        out_specs=(P(None, "gz", "gx", "gy"), P("gx", ("gy", "gz"))),
        check_vma=False,
    )
```

```python
import functools

import jax
import jax.numpy as jnp
from jax import lax
from jax.experimental import pallas as pl
from jax.experimental.pallas import tpu as pltpu
from jax.sharding import PartitionSpec as P

relax_rate = 0.9
keep_rate = 0.1

FIELDS = 6
LEV = 8
ROWS = 32
COLS = 128
EXT = 40
EDDY, RATE, STRIP = 6, 7, 8
SLOT = 16

VM = pl.BlockSpec(memory_space=pltpu.VMEM)
SM = pl.BlockSpec(memory_space=pltpu.SMEM)


def roll(v, shift, axis):
    return pltpu.roll(v, shift % v.shape[axis], axis)


def iota(shape, axis):
    return lax.broadcasted_iota(jnp.int32, shape, axis)


def f32(*shape):
    return jax.ShapeDtypeStruct(shape, jnp.float32)


def pack_y(adj, eddy, diag, metric, own, to_right, to_left):
    lane = iota((8, COLS), 1)
    slot, j = lane // SLOT, lane % SLOT
    quad, jj = j // 4, j % 4
    edge_at = [(slot == p) & (j >= 1) & (j <= 6) for p in range(8)]
    metric_at = [(slot == p) & (j >= 8) & (j <= 9) for p in range(FIELDS)]
    for zg in range(2):
        for t in range(ROWS // 8):
            rows = pl.ds(8 * t, 8)
            right = left = jnp.zeros((8, COLS), jnp.float32)
            for zq in range(4):
                z = 4 * zg + zq
                c = jnp.zeros((8, COLS), jnp.float32)
                for p in range(8):
                    if p < FIELDS:
                        v = adj[p, z, rows, :]
                    elif p == EDDY:
                        v = eddy[z, rows, :]
                    else:
                        v = relax_rate / diag[z, rows, :]
                    c = jnp.where(edge_at[p], roll(v, SLOT * p + 4, 1), c)
                    if p < FIELDS:
                        c = jnp.where(metric_at[p], roll(metric[0, p, z, rows, :], SLOT * p + 9, 1), c)
                own[z, rows, :] = jnp.where(j < 8, c, jnp.where(j >= 9, roll(c, 8, 1), 0.0))
                at = 4 * zq
                here = quad == zq
                right = jnp.where(here, jnp.where(jj == 0, roll(c, at - 8, 1), roll(c, at, 1)), right)
                left = jnp.where(here, jnp.where(jj == 3, roll(c, at - 6, 1), roll(c, at - 4, 1)), left)
            to_right[zg, rows, :] = right
            to_left[zg, rows, :] = left


MIX, PAIR = 8, 16


def make_source(total_y, idx, codes, coup, cells, weights, src, table):
    slot = iota((1, COLS), 1) // SLOT
    for i in range(6):
        factor = jnp.where(codes[i] == 1, 1.0, jnp.where(codes[i] == 2, -1.0, 0.0)).astype(jnp.float32)
        table[i : i + 1, :] = jnp.full((1, COLS), factor)
    for e in range(FIELDS):
        v = jnp.zeros((1, COLS), jnp.float32)
        for f in range(FIELDS):
            v = jnp.where(slot == f, coup[e, f], v)
            at = PAIR + FIELDS * e + f
            table[at : at + 1, :] = jnp.full((1, COLS), coup[e, f])
        table[MIX + e : MIX + e + 1, :] = v
    start_x, start_y = idx[0] * ROWS, idx[1] * COLS
    r = iota((48, COLS), 0)
    row_x = jnp.where(r < EXT - 5, r, r - EXT) + start_x
    row_x = jnp.where(r < EXT, row_x, -1)
    l = iota((2 * COLS, COLS), 0)
    j = l - COLS
    col_y = jnp.where((j >= 1) & (j <= 6), j - 4, j + (COLS - 12))
    col_y = jnp.where(l < COLS, l, col_y) + start_y
    col_y = jnp.where((l < COLS) | ((j >= 1) & (j <= 6)) | ((j >= 9) & (j <= 14)), col_y, -1)
    acc = jnp.zeros((144, 2 * COLS), jnp.float32)
    for k in range(0, 16, 2):
        left, one = [], []
        for q in (k, k + 1):
            c = cells[q : q + 1, :]
            w = weights[q : q + 1, :]
            x = ((c.astype(jnp.float32) + 0.5) * (1.0 / total_y)).astype(jnp.int32)
            y = c - x * total_y
            high = w.astype(jnp.bfloat16).astype(jnp.float32)
            mid = (w - high).astype(jnp.bfloat16).astype(jnp.float32)
            low = w - high - mid
            hit = row_x == x
            left.append(jnp.concatenate([jnp.where(hit, v, 0.0).astype(jnp.bfloat16) for v in (low, mid, high)], 0))
            one.append(jnp.where(col_y == y, 1.0, 0.0).astype(jnp.bfloat16))
        acc = acc + lax.dot_general(
            jnp.concatenate(left, 1),
            jnp.concatenate(one, 1),
            (((1,), (1,)), ((), ())),
            preferred_element_type=jnp.float32,
        )
    total = acc[0:EXT, :] + acc[48 : 48 + EXT, :] + acc[96 : 96 + EXT, :]
    src[0] = total[:, :COLS]
    src[1] = total[:, COLS:]


HIGH_AT = [0, 3, 6, 9, 12, 15, 18, 21, 23]
LOW_AT = [6 + a for a in HIGH_AT]
HIGH_METRIC, LOW_METRIC = 26, 0


def pack_x(src, own, from_left, from_right, adj, eddy, diag, metric, strip, to_low, to_high):
    j = iota((ROWS, COLS), 1) % SLOT
    for z in range(LEV):
        zg, at = z // 4, 4 * (z % 4)
        low = roll(from_left[zg], -at, 1)
        high = roll(from_right[zg], 12 - at, 1)
        s = jnp.where(j < 4, low, jnp.where(j >= 12, high, own[z]))
        strip[z] = s
        sides = ((to_low, 0, 0, 0, HIGH_AT, HIGH_METRIC), (to_high, ROWS - 3, ROWS - 2, ROWS - 1, LOW_AT, LOW_METRIC))
        for msg, a, b, near, at, metric_at in sides:
            for p in range(FIELDS):
                msg[z, at[p] : at[p] + 3, :] = adj[p, z, a : a + 3, :]
                msg[z, metric_at + p : metric_at + p + 1, :] = metric[1, p, z, near : near + 1, :]
            msg[z, at[EDDY] : at[EDDY] + 3, :] = eddy[z, a : a + 3, :]
            msg[z, at[RATE] : at[RATE] + 2, :] = relax_rate / diag[z, b : b + 2, :]
            msg[z, at[STRIP] : at[STRIP] + 3, :] = s[a : a + 3, :]


def lanes_of(v, plane):
    return jnp.take_along_axis(v, iota(v.shape, 1) % SLOT + SLOT * plane, axis=1)


class Edges:
    def __init__(self, info, table):
        self.low_x, self.high_x = info[0] == 0, info[0] == info[3] - 1
        self.low_y, self.high_y = info[1] == 0, info[1] == info[4] - 1
        self.low_z, self.high_z = info[2] == 0, info[2] == info[5] - 1
        self.factors = [table[i : i + 1, :] for i in range(6)]
        row, j = iota((8, COLS), 0), iota((EXT, COLS), 1) % SLOT
        self.row_low, self.row_high = (row == 7) & self.low_x, (row == 0) & self.high_x
        self.j = j
        self.ghost_low, self.ghost_high = (j == 3) & self.low_y, (j == 12) & self.high_y
        self.own_low, self.own_high = (j == 4) & self.low_y, (j == 11) & self.high_y

    def flux(self, v):
        t4 = v[32:40]
        t4 = jnp.where(self.row_low, self.factors[0] * roll(v[0:8], 7, 0), t4)
        t4 = jnp.where(self.row_high, self.factors[1] * roll(v[24:32], 1, 0), t4)
        return jnp.concatenate([v[0:32], t4], 0)


def sweep(edges, center, vertical, value, rate, strip_rate, table, store, src=None, flag=None):
    lane = iota((EXT, COLS), 1)

    def pair(e, f):
        at = PAIR + FIELDS * e + f
        return table[at : at + 1, :]

    f2, f3 = edges.factors[2], edges.factors[3]
    v = center(FIELDS)
    up, down = roll(v, 1, 1), roll(v, -1, 1)
    fixed = jnp.where(edges.ghost_low, f2 * down, jnp.where(edges.ghost_high, f3 * up, v))
    both = jnp.where(edges.j == 3, fixed, roll(fixed, -10, 1))
    beside = vertical(FIELDS) + roll(v, -1, 0) + roll(v, 1, 0)
    beside = beside + jnp.where(edges.own_low, f2 * v, up) + jnp.where(edges.own_high, f3 * v, down)
    a = value(FIELDS)
    coupled = lanes_of(a, 0) * table[MIX : MIX + 1, :]
    for e in range(1, FIELDS):
        coupled = coupled + lanes_of(a, e) * table[MIX + e : MIX + e + 1, :]
    rest = beside - coupled
    if src is not None:
        rest = rest + flag * src[1]
    store(FIELDS, keep_rate * a + strip_rate * rest)
    for f in range(FIELDS):
        v = center(f)
        end = roll(both, -(SLOT * f + 3), 1)
        left = jnp.where(lane == 0, end, roll(v, 1, 1))
        right = jnp.where(lane == COLS - 1, end, roll(v, -1, 1))
        beside = vertical(f) + roll(v, -1, 0) + roll(v, 1, 0) + right + left
        coupled = pair(0, f) * value(0)
        for e in range(1, FIELDS):
            coupled = coupled + pair(e, f) * value(e)
        rest = beside - coupled
        if f == 0 and src is not None:
            rest = rest + flag * src[0]
        store(f, keep_rate * value(f) + rate * rest)


def level_sums(z, info, field, edge_strip, strip, metric, metric_row, sums, out, zo):
    total_z = (info[5] * LEV).astype(jnp.float32)
    w = 1.0 - 0.5 * (((info[2] * LEV + z).astype(jnp.float32) + 0.5) / total_z)
    totals = None
    for f in range(FIELDS):
        a = field(f)
        own = a[:ROWS]
        out[f, zo] = own
        terms = [metric[k, f, z] * own for k in range(3)] + [metric_row[f, z] * a[ROWS:]]
        totals = terms if f == 0 else [s + t for s, t in zip(totals, terms)]
    s = strip[z, :ROWS]
    j = iota((ROWS, COLS), 1) % SLOT
    m = jnp.where(j == 3, roll(s, 3, 1), jnp.where(j == 12, roll(s, -3, 1), 0.0))
    sums[0, :ROWS] += w * totals[0]
    sums[1, :ROWS] += w * totals[1]
    sums[1, ROWS:] += w * totals[3]
    sums[2, :ROWS] += w * totals[2]
    sums[3, :ROWS] += w * (m * edge_strip[:ROWS])


def halo_tile(from_low, from_high, z, p):
    at = 2 if p == RATE else 3
    start = LOW_AT[p] - (8 - at)
    above, below = from_high[z, pl.ds(HIGH_AT[p], 8), :], from_low[z, pl.ds(start, 8), :]
    return jnp.where(iota((8, COLS), 0) < 4, above, below)


def pack_z(far, info, table, strip, from_low, from_high, adj, eddy, diag, msg):
    edges = Edges(info, table)
    top = (info[2] % 2 == 0) != far

    def plane(z, p):
        own = adj[p, z] if p < FIELDS else eddy[z] if p == EDDY else relax_rate / diag[z] if p == RATE else strip[z]
        return jnp.concatenate([own, halo_tile(from_low, from_high, z, p)], 0)

    near = jnp.where(top, LEV - 1, 0)
    next_ = jnp.where(top, LEV - 2, 1)
    for p in range(9):
        msg[p] = plane(near, p)
    e = plane(next_, EDDY)
    for f in range(FIELDS):
        msg[9 + f] = edges.flux(plane(next_, f) * e)
    s = plane(next_, STRIP)
    msg[15] = edges.flux(s * lanes_of(s, EDDY))


def inner_levels(
    info, table, adj, eddy, diag, strip, from_low, from_high, metric, src,
    f0, near1, next2, f1, rates, edge_eddy, edge_rate, out, sums, halo, metric_row, a1, a2,
):
    edges = Edges(info, table)
    row = iota((8, COLS), 0)
    for z in range(LEV):
        for p in range(9):
            halo[z, p] = halo_tile(from_low, from_high, z, p)
        for f in range(FIELDS):
            above = jnp.broadcast_to(from_high[z, HIGH_METRIC + f : HIGH_METRIC + f + 1, :], (8, COLS))
            below = jnp.broadcast_to(from_low[z, LOW_METRIC + f : LOW_METRIC + f + 1, :], (8, COLS))
            metric_row[f, z] = jnp.where(row < 4, above, below)
    hub = info[5] * LEV // 4 - info[2] * LEV
    flag = jnp.where(hub == 0, 1.0, 0.0).astype(jnp.float32)

    def value(z, p):
        own = adj[p, z] if p < FIELDS else strip[z]
        return jnp.concatenate([own, halo[z, STRIP if p == FIELDS else p]], 0)

    def eddies(z):
        return jnp.concatenate([eddy[z], halo[z, EDDY]], 0)

    for z in range(LEV):
        rates[z] = jnp.concatenate([relax_rate / diag[z], halo[z, RATE]], 0)
        s = value(z, FIELDS)
        edge_eddy[z] = lanes_of(s, EDDY)
        edge_rate[z] = lanes_of(s, RATE)
        e = eddies(z)
        for f in range(FIELDS):
            f0[z, f] = edges.flux(value(z, f) * e)
        f0[z, FIELDS] = edges.flux(s * edge_eddy[z])

    def around(array, z):
        return lambda p: array[z - 1, p] + array[z + 1, p]

    def first(z, vertical, store, **more):
        sweep(edges, lambda p: f0[z, p], vertical, lambda p: value(z, p), rates[z], edge_rate[z], table, store, **more)

    def store_near(i):
        def store(p, v):
            near1[i, p] = v

        return store

    def store_inner(z):
        def store(p, v):
            a1[z, p] = v
            f1[z, p] = edges.flux(v * (edge_eddy[z] if p == FIELDS else eddies(z)))

        return store

    first(0, lambda p: f0[1, p], store_near(0), src=src, flag=flag)
    first(LEV - 1, lambda p: f0[LEV - 2, p], store_near(1))
    for z in range(1, LEV - 1):
        first(z, around(f0, z), store_inner(z))
    sums[...] = jnp.zeros_like(sums)

    def second(z, vertical, store):
        sweep(edges, lambda p: f1[z, p], vertical, lambda p: a1[z, p], rates[z], edge_rate[z], table, store)

    def store_next(i):
        def store(p, v):
            next2[i, p] = v

        return store

    def store_last(z):
        def store(p, v):
            a2[z, p] = v

        return store

    second(1, lambda p: f1[2, p], store_next(0))
    second(LEV - 2, lambda p: f1[LEV - 3, p], store_next(1))
    for z in range(2, LEV - 2):
        second(z, around(f1, z), store_last(z))
        level_sums(z, info, lambda f: a2[z, f], a2[z, FIELDS], strip, metric, metric_row, sums, out, z - 2)


def outer_levels(
    info, table, eddy, strip, from_b, from_a, metric, src,
    f0, near1, next2, f1, rates, edge_eddy, edge_rate, inner_out, inner_sums, halo_rows, metric_row,
    out, share, sums, fh, gh, an, gn, a2,
):
    edges = Edges(info, table)
    hub = info[5] * LEV // 4 - info[2] * LEV
    sums[...] = inner_sums[...]
    for f in range(FIELDS):
        for z in range(2, LEV - 2):
            out[f, z] = inner_out[f, z - 2]
    even = info[2] % 2 == 0

    def flag_of(z):
        return jnp.where(z == hub, 1.0, 0.0).astype(jnp.float32)

    for n, msg in enumerate((from_a, from_b)):
        top = even if n == 0 else jnp.logical_not(even)
        i = jnp.where(top, 1, 0)
        near = jnp.where(top, LEV - 1, 0)
        next_ = jnp.where(top, LEV - 2, 1)
        over = jnp.where(top, LEV, -1)
        ghost = jnp.where(top, edges.high_z, edges.low_z)
        factor = jnp.where(top, edges.factors[5], edges.factors[4])
        eddy_over = msg[EDDY]
        s = msg[STRIP]
        edge_eddy_over = lanes_of(s, EDDY)
        eddy_near = jnp.concatenate([eddy[near], halo_rows[near, EDDY]], 0)
        for p in range(FIELDS + 1):
            v = s * edge_eddy_over if p == FIELDS else msg[p] * eddy_over
            v = jnp.where(ghost, factor * f0[near, p], edges.flux(v))
            fh[n, p] = v
            r, e = (edge_rate[near], edge_eddy[near]) if p == FIELDS else (rates[near], eddy_near)
            v = near1[i, p] + r * v
            an[n, p] = v
            gn[n, p] = edges.flux(v * e)

        def store_over(p, v):
            v = edges.flux(v * (edge_eddy_over if p == FIELDS else eddy_over))
            gh[n, p] = jnp.where(ghost, factor * gn[n, p], v)

        sweep(
            edges,
            lambda p: fh[n, p],
            lambda p: msg[9 + p] + f0[near, p],
            lambda p: msg[STRIP if p == FIELDS else p],
            msg[RATE],
            lanes_of(s, RATE),
            table,
            store_over,
            src,
            flag_of(over),
        )

        def after(p):
            r = edge_rate[next_] if p == FIELDS else rates[next_]
            return next2[i, p] + r * gn[n, p]

        level_sums(next_, info, after, after(FIELDS), strip, metric, metric_row, sums, out, next_)

        def store_last(p, v):
            a2[n, p] = v

        sweep(
            edges,
            lambda p: gn[n, p],
            lambda p: gh[n, p] + f1[next_, p],
            lambda p: an[n, p],
            rates[near],
            edge_rate[near],
            table,
            store_last,
            src,
            flag_of(near),
        )
        level_sums(near, info, lambda f: a2[n, f], a2[n, FIELDS], strip, metric, metric_row, sums, out, near)

    s1 = sums[1]
    stream = roll(s1, -1, 0)[:ROWS] - roll(s1, 1, 0)[:ROWS]
    t = sums[3, :ROWS]
    t = t + roll(t, 4 * SLOT, 1)
    t = t + roll(t, 2 * SLOT, 1)
    t = t + roll(t, SLOT, 1)
    s2 = sums[2, :ROWS]
    lane = iota((ROWS, COLS), 1)
    right = jnp.where(lane == COLS - 1, roll(t, 3, 1), roll(s2, -1, 1))
    left = jnp.where(lane == 0, roll(t, -3, 1), roll(s2, 1, 1))
    total = sums[0, :ROWS] - 0.5 * stream - 0.5 * (right - left)
    turned = jnp.concatenate([total, jnp.zeros((COLS - ROWS, COLS), jnp.float32)], 0).T
    count, width = share.shape[0], COLS // share.shape[0]
    group = iota((8, COLS), 1) // ROWS
    for k in range(count):
        v = turned[width * k : width * k + 8]
        for q in range(1, width // 8):
            v = jnp.where(group == q, roll(turned[width * k + 8 * q : width * k + 8 * q + 8], ROWS * q, 1), v)
        share[k] = v


def add_shares(parts, out):
    total = parts[0]
    for i in range(1, parts.shape[0]):
        total = total + parts[i]
    for q in range(out.shape[0] // 8):
        out[8 * q : 8 * q + 8, :] = roll(total, -ROWS * q, 1)[:, :ROWS]


def call(body, outs, ins, scratch=()):
    return pl.pallas_call(
        body,
        out_shape=outs,
        in_specs=ins,
        out_specs=jax.tree.map(lambda _: VM, outs),
        scratch_shapes=list(scratch),
        compiler_params=pltpu.CompilerParams(vmem_limit_bytes=16 << 20),
        cost_estimate=pl.CostEstimate(flops=1000000, bytes_accessed=1 << 20, transcendentals=0),
    )


def local(adjoint_start, eddy_visc, diag_coef, coupling, metric_terms, sample_cells, sample_weights, face_codes):
    index = [lax.axis_index(a) for a in ("gx", "gy", "gz")]
    count = [lax.axis_size(a) for a in ("gx", "gy", "gz")]
    info = jnp.stack(index + [jnp.int32(c) for c in count]).astype(jnp.int32)
    cells, weights = sample_cells.reshape(16, 128), sample_weights.reshape(16, 128)

    def shift(v, axis, step):
        n = lax.axis_size(axis)
        return lax.ppermute(v, axis, [(i, i + step) for i in range(n) if 0 <= i + step < n])

    def trade(v, axis, first):
        n = lax.axis_size(axis)
        pairs = [(i, i + 1) for i in range(first, n - 1, 2)]
        return lax.ppermute(v, axis, pairs + [(b, a) for a, b in pairs])

    def buf(*shape):
        return pltpu.VMEM(shape, jnp.float32)

    level = (LEV, ROWS, COLS)
    own, to_right, to_left = call(
        pack_y,
        (f32(*level), f32(2, ROWS, COLS), f32(2, ROWS, COLS)),
        [VM] * 4,
    )(adjoint_start, eddy_visc, diag_coef, metric_terms[2:3])
    from_left = shift(to_right, "gy", 1)
    from_right = shift(to_left, "gy", -1)
    src, table = call(
        functools.partial(make_source, COLS * count[1]), (f32(2, EXT, COLS), f32(56, COLS)), [SM] * 3 + [VM] * 2
    )(info, face_codes, coupling, cells, weights)
    strip, to_low, to_high = call(pack_x, (f32(*level),) * 3, [VM] * 8)(
        src, own, from_left, from_right, adjoint_start, eddy_visc, diag_coef, metric_terms
    )
    from_low = shift(to_high, "gx", 1)
    from_high = shift(to_low, "gx", -1)
    received = (from_low, from_high, adjoint_start, eddy_visc, diag_coef)
    msg_b, msg_a = [
        call(functools.partial(pack_z, far), f32(16, EXT, COLS), [SM] + [VM] * 7)(info, table, strip, *received)
        for far in (True, False)
    ]
    from_b = trade(msg_b, "gz", 1)
    from_a = trade(msg_a, "gz", 0)
    ext = (EXT, COLS)
    inner = call(
        inner_levels,
        (
            f32(LEV, 7, *ext),
            f32(2, 7, *ext),
            f32(2, 7, *ext),
            f32(LEV, 7, *ext),
            f32(LEV, *ext),
            f32(LEV, *ext),
            f32(LEV, *ext),
            f32(FIELDS, LEV - 4, ROWS, COLS),
            f32(4, *ext),
            f32(LEV, 9, 8, COLS),
            f32(FIELDS, LEV, 8, COLS),
        ),
        [SM] + [VM] * 9,
        [buf(LEV, 7, *ext), buf(LEV, 7, *ext)],
    )(info, table, adjoint_start, eddy_visc, diag_coef, strip, from_low, from_high, metric_terms, src)
    adjoint, share = call(
        outer_levels,
        (f32(FIELDS, *level), f32(count[2], 8, COLS)),
        [SM] + [VM] * 18,
        [buf(4, *ext)] + [buf(2, 7, *ext)] * 5,
    )(info, table, eddy_visc, strip, from_b, from_a, metric_terms, src, *inner)
    parts = lax.all_to_all(share, "gz", 0, 0, tiled=True)
    height_grad = call(add_shares, f32(COLS // count[2], ROWS), [VM])(parts).T
    return (adjoint, height_grad)


def solution(mesh):
    return jax.shard_map(
        local,
        mesh=mesh,
        in_specs=(
            P(None, "gz", "gx", "gy"),
            P("gz", "gx", "gy"),
            P("gz", "gx", "gy"),
            P(),
            P(None, None, "gz", "gx", "gy"),
            P(),
            P(),
            P(),
        ),
        out_specs=(P(None, "gz", "gx", "gy"), P("gx", ("gy", "gz"))),
        check_vma=False,
    )
```

```python
import functools

import jax
import jax.numpy as jnp
from jax import lax
from jax.experimental import pallas as pl
from jax.experimental.pallas import tpu as pltpu
from jax.sharding import PartitionSpec as P

relax_rate = 0.9
keep_rate = 0.1

FIELDS = 6
LEV = 8
ROWS = 32
COLS = 128
EXT = 40
EDDY, RATE, STRIP = 6, 7, 8
SLOT = 16

VM = pl.BlockSpec(memory_space=pltpu.VMEM)
SM = pl.BlockSpec(memory_space=pltpu.SMEM)


def roll(v, shift, axis):
    return pltpu.roll(v, shift % v.shape[axis], axis)


def iota(shape, axis):
    return lax.broadcasted_iota(jnp.int32, shape, axis)


def f32(*shape):
    return jax.ShapeDtypeStruct(shape, jnp.float32)


def pipeline(tasks):
    held = None
    for begin, end in tasks:
        started = begin()
        if held is not None:
            held[0](held[1])
        held = (end, started)
    held[0](held[1])


def pack_y(adj, eddy, diag, metric, own, to_right, to_left, packed):
    shape = (4, 8, COLS)
    lane = iota(shape, 2)
    slot, j = lane // SLOT, lane % SLOT
    quad, jj = j // 4, j % 4

    def block(zg, t):
        return pl.ds(4 * zg, 4), pl.ds(8 * t, 8)

    def gather(zg, t):
        zs, rows = block(zg, t)

        def planes(p):
            if p >= 8:
                return roll(metric[0, p - 8, zs, rows, :], SLOT * (p - 8) + 9, 2)
            v = adj[p, zs, rows, :] if p < FIELDS else eddy[zs, rows, :] if p == EDDY else relax_rate / diag[zs, rows, :]
            return roll(v, SLOT * p + 4, 2)

        def choose(p, v, c):
            if p >= 8:
                return jnp.where((slot == p - 8) & (j >= 8) & (j <= 9), v, c)
            return jnp.where((slot == p) & (j >= 1) & (j <= 6), v, c)

        c = jnp.zeros(shape, jnp.float32)
        ahead = [planes(0), planes(1), planes(2)]
        for p in range(14):
            if p + 3 < 14:
                ahead.append(planes(p + 3))
            c = choose(p, ahead[p], c)
        packed[zs, rows, :] = c

    def send(zg, t):
        zs, rows = block(zg, t)
        c = packed[zs, rows, :]
        c8 = roll(c, 8, 2)
        right = left = jnp.zeros((8, COLS), jnp.float32)
        moved = []
        for zq in range(4):
            at = 4 * zq
            moved.append([roll(c[zq], at + by, 1) for by in (-8, 0, -6, -4)])
        own[zs, rows, :] = jnp.where(j < 8, c, jnp.where(j >= 9, c8, 0.0))
        for zq in range(4):
            r0, r1, l0, l1 = moved[zq]
            here = quad[0] == zq
            right = jnp.where(here, jnp.where(jj[0] == 0, r0, r1), right)
            left = jnp.where(here, jnp.where(jj[0] == 3, l0, l1), left)
        to_right[zg, rows, :] = right
        to_left[zg, rows, :] = left

    blocks = [(zg, t) for zg in range(2) for t in range(ROWS // 8)]
    for zg, t in blocks:
        gather(zg, t)
    for zg, t in blocks:
        send(zg, t)


MIX, PAIR = 8, 16


def make_source(total_y, idx, codes, coup, cells, weights, after, src, table):
    slot = iota((1, COLS), 1) // SLOT
    for i in range(6):
        factor = jnp.where(codes[i] == 1, 1.0, jnp.where(codes[i] == 2, -1.0, 0.0)).astype(jnp.float32)
        table[i : i + 1, :] = jnp.full((1, COLS), factor)
    for e in range(FIELDS):
        v = jnp.zeros((1, COLS), jnp.float32)
        for f in range(FIELDS):
            v = jnp.where(slot == f, coup[e, f], v)
            at = PAIR + FIELDS * e + f
            table[at : at + 1, :] = jnp.full((1, COLS), coup[e, f])
        table[MIX + e : MIX + e + 1, :] = v
    start_x, start_y = idx[0] * ROWS, idx[1] * COLS
    r = iota((48, COLS), 0)
    row_x = jnp.where(r < EXT - 5, r, r - EXT) + start_x
    row_x = jnp.where(r < EXT, row_x, -1)
    l = iota((2 * COLS, COLS), 0)
    j = l - COLS
    col_y = jnp.where((j >= 1) & (j <= 6), j - 4, j + (COLS - 12))
    col_y = jnp.where(l < COLS, l, col_y) + start_y
    col_y = jnp.where((l < COLS) | ((j >= 1) & (j <= 6)) | ((j >= 9) & (j <= 14)), col_y, -1)
    acc = jnp.zeros((144, 2 * COLS), jnp.float32)
    for k in range(0, 16, 2):
        left, one = [], []
        for q in (k, k + 1):
            c = cells[q : q + 1, :]
            w = weights[q : q + 1, :]
            x = ((c.astype(jnp.float32) + 0.5) * (1.0 / total_y)).astype(jnp.int32)
            y = c - x * total_y
            high = w.astype(jnp.bfloat16).astype(jnp.float32)
            mid = (w - high).astype(jnp.bfloat16).astype(jnp.float32)
            low = w - high - mid
            hit = row_x == x
            left.append(jnp.concatenate([jnp.where(hit, v, 0.0).astype(jnp.bfloat16) for v in (low, mid, high)], 0))
            one.append(jnp.where(col_y == y, 1.0, 0.0).astype(jnp.bfloat16))
        acc = acc + lax.dot_general(
            jnp.concatenate(left, 1),
            jnp.concatenate(one, 1),
            (((1,), (1,)), ((), ())),
            preferred_element_type=jnp.float32,
        )
    total = acc[0:EXT, :] + acc[48 : 48 + EXT, :] + acc[96 : 96 + EXT, :]
    src[0] = total[:, :COLS]
    src[1] = total[:, COLS:]


HIGH_AT = [0, 3, 6, 9, 12, 15, 18, 21, 23]
LOW_AT = [6 + a for a in HIGH_AT]
HIGH_METRIC, LOW_METRIC = 26, 0


def pack_x(own, from_left, from_right, adj, eddy, diag, metric, strip, to_low, to_high):
    j = iota((ROWS, COLS), 1) % SLOT
    for z in range(LEV):
        zg, at = z // 4, 4 * (z % 4)
        low = roll(from_left[zg], -at, 1)
        high = roll(from_right[zg], 12 - at, 1)
        s = jnp.where(j < 4, low, jnp.where(j >= 12, high, own[z]))
        strip[z] = s
        sides = ((to_low, 0, 0, 0, HIGH_AT, HIGH_METRIC), (to_high, ROWS - 3, ROWS - 2, ROWS - 1, LOW_AT, LOW_METRIC))
        for msg, a, b, near, at, metric_at in sides:
            for p in range(FIELDS):
                msg[z, at[p] : at[p] + 3, :] = adj[p, z, a : a + 3, :]
                msg[z, metric_at + p : metric_at + p + 1, :] = metric[1, p, z, near : near + 1, :]
            msg[z, at[EDDY] : at[EDDY] + 3, :] = eddy[z, a : a + 3, :]
            msg[z, at[RATE] : at[RATE] + 2, :] = relax_rate / diag[z, b : b + 2, :]
            msg[z, at[STRIP] : at[STRIP] + 3, :] = s[a : a + 3, :]


def lanes_of(v, plane):
    return jnp.take_along_axis(v, iota(v.shape, 1) % SLOT + SLOT * plane, axis=1)


class Edges:
    def __init__(self, info, table):
        self.low_x, self.high_x = info[0] == 0, info[0] == info[3] - 1
        self.low_y, self.high_y = info[1] == 0, info[1] == info[4] - 1
        self.low_z, self.high_z = info[2] == 0, info[2] == info[5] - 1
        self.factors = [table[i : i + 1, :] for i in range(6)]
        row, j = iota((8, COLS), 0), iota((EXT, COLS), 1) % SLOT
        self.row_low, self.row_high = (row == 7) & self.low_x, (row == 0) & self.high_x
        self.j = j
        self.ghost_low, self.ghost_high = (j == 3) & self.low_y, (j == 12) & self.high_y
        self.own_low, self.own_high = (j == 4) & self.low_y, (j == 11) & self.high_y

    def flux(self, v):
        t4 = v[32:40]
        t4 = jnp.where(self.row_low, self.factors[0] * roll(v[0:8], 7, 0), t4)
        t4 = jnp.where(self.row_high, self.factors[1] * roll(v[24:32], 1, 0), t4)
        return jnp.concatenate([v[0:32], t4], 0)


class Level:
    def __init__(self, center, vertical, value, rate, edge_rate, ends, lateral, store, src=None, flag=None):
        self.center, self.vertical, self.value = center, vertical, value
        self.rate, self.edge_rate, self.ends, self.lateral = rate, edge_rate, ends, lateral
        self.store, self.src, self.flag = store, src, flag


def prepare(edges, strips, ends, lateral):
    f2, f3 = edges.factors[2], edges.factors[3]

    def task(at, strip):
        def end(moved):
            v, up, down = moved
            ends[at] = jnp.where(edges.ghost_low, f2 * down, jnp.where(edges.ghost_high, f3 * up, v))
            lateral[at] = jnp.where(edges.own_low, f2 * v, up) + jnp.where(edges.own_high, f3 * v, down)

        def begin():
            v = strip()
            return v, roll(v, 1, 1), roll(v, -1, 1)

        return begin, end

    def turn(at, _):
        def begin():
            v = ends[at]
            return v, roll(v, -10, 1)

        def end(moved):
            ends[at] = jnp.where(edges.j == 3, *moved)

        return begin, end

    pipeline([task(*s) for s in strips])
    pipeline([turn(*s) for s in strips])


def sweep(levels, table):
    lane = iota((EXT, COLS), 1)
    half = FIELDS // 2

    def pair(e, f):
        at = PAIR + FIELDS * e + f
        return table[at : at + 1, :]

    def field(level, f):
        def begin():
            v = level.center(f)
            return v, roll(level.ends(), -(SLOT * f + 3), 1), roll(v, 1, 1), roll(v, -1, 1)

        def end(moved):
            v, edge, left, right = moved
            left = jnp.where(lane == 0, edge, left)
            right = jnp.where(lane == COLS - 1, edge, right)
            beside = level.vertical(f) + roll(v, -1, 0) + roll(v, 1, 0) + right + left
            coupled = pair(0, f) * level.value(0)
            for e in range(1, FIELDS):
                coupled = coupled + pair(e, f) * level.value(e)
            rest = beside - coupled
            if f == 0 and level.src is not None:
                rest = rest + level.flag * level.src[0]
            level.store(f, keep_rate * level.value(f) + level.rate() * rest)

        return begin, end

    def strip(level):
        sums = []

        def mixed(first):
            def begin():
                a = level.value(FIELDS)
                return [lanes_of(a, e) for e in range(first, first + half)]

            def end(moved):
                terms = [v * table[MIX + first + i : MIX + first + i + 1, :] for i, v in enumerate(moved)]
                sums.append(terms[0] + terms[1] + terms[2])

            return begin, end

        def end(_):
            v = level.center(FIELDS)
            rest = level.vertical(FIELDS) + roll(v, -1, 0) + roll(v, 1, 0) + level.lateral() - (sums[0] + sums[1])
            if level.src is not None:
                rest = rest + level.flag * level.src[1]
            level.store(FIELDS, keep_rate * level.value(FIELDS) + level.edge_rate() * rest)

        return [mixed(0), mixed(half), (lambda: None, end)]

    pipeline([task for level in levels for task in strip(level) + [field(level, f) for f in range(FIELDS)]])


def level_sums(z, info, field, edge_strip, strip, metric, metric_row, sums, out, zo):
    total_z = (info[5] * LEV).astype(jnp.float32)
    w = 1.0 - 0.5 * (((info[2] * LEV + z).astype(jnp.float32) + 0.5) / total_z)
    totals = None
    for f in range(FIELDS):
        a = field(f)
        own = a[:ROWS]
        out[f, zo] = own
        terms = [metric[k, f, z] * own for k in range(3)] + [metric_row[f, z] * a[ROWS:]]
        totals = terms if f == 0 else [s + t for s, t in zip(totals, terms)]
    s = strip[z, :ROWS]
    j = iota((ROWS, COLS), 1) % SLOT
    m = jnp.where(j == 3, roll(s, 3, 1), jnp.where(j == 12, roll(s, -3, 1), 0.0))
    sums[0, :ROWS] += w * totals[0]
    sums[1, :ROWS] += w * totals[1]
    sums[1, ROWS:] += w * totals[3]
    sums[2, :ROWS] += w * totals[2]
    sums[3, :ROWS] += w * (m * edge_strip[:ROWS])


def halo_tile(from_low, from_high, z, p):
    at = 2 if p == RATE else 3
    start = LOW_AT[p] - (8 - at)
    above, below = from_high[z, pl.ds(HIGH_AT[p], 8), :], from_low[z, pl.ds(start, 8), :]
    return jnp.where(iota((8, COLS), 0) < 4, above, below)


def pack_z(far, info, table, strip, from_low, from_high, adj, eddy, diag, msg):
    edges = Edges(info, table)
    top = (info[2] % 2 == 0) != far

    def plane(z, p):
        own = adj[p, z] if p < FIELDS else eddy[z] if p == EDDY else relax_rate / diag[z] if p == RATE else strip[z]
        return jnp.concatenate([own, halo_tile(from_low, from_high, z, p)], 0)

    near = jnp.where(top, LEV - 1, 0)
    next_ = jnp.where(top, LEV - 2, 1)
    for p in range(9):
        msg[p] = plane(near, p)
    e = plane(next_, EDDY)
    for f in range(FIELDS):
        msg[9 + f] = edges.flux(plane(next_, f) * e)
    s = plane(next_, STRIP)
    msg[15] = edges.flux(s * lanes_of(s, EDDY))


def inner_levels(
    info, table, adj, eddy, diag, strip, from_low, from_high, metric, src,
    f0, near1, next2, f1, rates, edge_eddy, edge_rate, out, sums, halo, metric_row, a1, a2, ends, lateral,
):
    edges = Edges(info, table)
    row = iota((8, COLS), 0)
    for z in range(LEV):
        for p in range(9):
            halo[z, p] = halo_tile(from_low, from_high, z, p)
        for f in range(FIELDS):
            above = jnp.broadcast_to(from_high[z, HIGH_METRIC + f : HIGH_METRIC + f + 1, :], (8, COLS))
            below = jnp.broadcast_to(from_low[z, LOW_METRIC + f : LOW_METRIC + f + 1, :], (8, COLS))
            metric_row[f, z] = jnp.where(row < 4, above, below)
    hub = info[5] * LEV // 4 - info[2] * LEV
    flag = jnp.where(hub == 0, 1.0, 0.0).astype(jnp.float32)

    def value(z, p):
        own = adj[p, z] if p < FIELDS else strip[z]
        return jnp.concatenate([own, halo[z, STRIP if p == FIELDS else p]], 0)

    def eddies(z):
        return jnp.concatenate([eddy[z], halo[z, EDDY]], 0)

    for z in range(LEV):
        rates[z] = jnp.concatenate([relax_rate / diag[z], halo[z, RATE]], 0)
        s = value(z, FIELDS)
        edge_eddy[z] = lanes_of(s, EDDY)
        edge_rate[z] = lanes_of(s, RATE)
    for z in range(LEV):
        e = eddies(z)
        for f in range(FIELDS):
            f0[z, f] = edges.flux(value(z, f) * e)
        f0[z, FIELDS] = edges.flux(value(z, FIELDS) * edge_eddy[z])

    def strips_of(array, zs):
        return [(z, lambda z=z: array[z, FIELDS]) for z in zs]

    def level(z, flux, value, vertical, store, **more):
        return Level(
            lambda p: flux[z, p],
            vertical,
            lambda p: value(z, p),
            lambda: rates[z],
            lambda: edge_rate[z],
            lambda: ends[z],
            lambda: lateral[z],
            store,
            **more,
        )

    def store_first(z):
        def store(p, v):
            if z in (0, LEV - 1):
                near1[z // (LEV - 1), p] = v
            else:
                a1[z, p] = v
                f1[z, p] = edges.flux(v * (edge_eddy[z] if p == FIELDS else eddies(z)))

        return store

    def store_second(z):
        def store(p, v):
            if z in (1, LEV - 2):
                next2[z // (LEV - 2), p] = v
            else:
                a2[z, p] = v

        return store

    def around(array, z, low, high):
        if z == low:
            return lambda p: array[z + 1, p]
        if z == high:
            return lambda p: array[z - 1, p]
        return lambda p: array[z - 1, p] + array[z + 1, p]

    prepare(edges, strips_of(f0, range(LEV)), ends, lateral)
    sweep(
        [
            level(z, f0, value, around(f0, z, 0, LEV - 1), store_first(z), **({"src": src, "flag": flag} if z == 0 else {}))
            for z in range(LEV)
        ],
        table,
    )
    inside = range(1, LEV - 1)
    prepare(edges, strips_of(f1, inside), ends, lateral)
    sweep([level(z, f1, lambda z, p: a1[z, p], around(f1, z, 1, LEV - 2), store_second(z)) for z in inside], table)
    sums[...] = jnp.zeros_like(sums)
    for z in range(2, LEV - 2):
        level_sums(z, info, lambda f: a2[z, f], a2[z, FIELDS], strip, metric, metric_row, sums, out, z - 2)


def outer_levels(
    info, table, eddy, strip, from_b, from_a, metric, src,
    f0, near1, next2, f1, rates, edge_eddy, edge_rate, inner_out, inner_sums, halo_rows, metric_row,
    out, share, sums, fh, gh, an, gn, a2, edge_over, ends, lateral,
):
    edges = Edges(info, table)
    hub = info[5] * LEV // 4 - info[2] * LEV
    sums[...] = inner_sums[...]
    for f in range(FIELDS):
        for z in range(2, LEV - 2):
            out[f, z] = inner_out[f, z - 2]
    even = info[2] % 2 == 0

    def flag_of(z):
        return jnp.where(z == hub, 1.0, 0.0).astype(jnp.float32)

    def side(n, msg):
        top = even if n == 0 else jnp.logical_not(even)
        near, next_ = jnp.where(top, LEV - 1, 0), jnp.where(top, LEV - 2, 1)
        ghost = jnp.where(top, edges.high_z, edges.low_z)
        factor = jnp.where(top, edges.factors[5], edges.factors[4])
        return n, msg, jnp.where(top, 1, 0), near, next_, jnp.where(top, LEV, -1), ghost, factor

    sides = [side(0, from_a), side(1, from_b)]
    for n, msg, *_ in sides:
        edge_over[n, 0] = lanes_of(msg[STRIP], EDDY)
        edge_over[n, 1] = lanes_of(msg[STRIP], RATE)
    for n, msg, i, near, next_, over, ghost, factor in sides:
        eddy_near = jnp.concatenate([eddy[near], halo_rows[near, EDDY]], 0)
        for p in (FIELDS, *range(FIELDS)):
            v = msg[STRIP] * edge_over[n, 0] if p == FIELDS else msg[p] * msg[EDDY]
            v = jnp.where(ghost, factor * f0[near, p], edges.flux(v))
            fh[n, p] = v
            r, e = (edge_rate[near], edge_eddy[near]) if p == FIELDS else (rates[near], eddy_near)
            v = near1[i, p] + r * v
            an[n, p] = v
            gn[n, p] = edges.flux(v * e)
    prepare(edges, [(n, lambda n=n: fh[n, FIELDS]) for n in range(2)], ends, lateral)
    prepare(edges, [(2 + n, lambda n=n: gn[n, FIELDS]) for n in range(2)], ends, lateral)

    def over_level(n, msg, i, near, next_, over, ghost, factor):
        def store(p, v):
            v = edges.flux(v * (edge_over[n, 0] if p == FIELDS else msg[EDDY]))
            gh[n, p] = jnp.where(ghost, factor * gn[n, p], v)

        return Level(
            lambda p: fh[n, p],
            lambda p: msg[9 + p] + f0[near, p],
            lambda p: msg[STRIP if p == FIELDS else p],
            lambda: msg[RATE],
            lambda: edge_over[n, 1],
            lambda: ends[n],
            lambda: lateral[n],
            store,
            src,
            flag_of(over),
        )

    def near_level(n, msg, i, near, next_, over, ghost, factor):
        def store(p, v):
            a2[n, p] = v

        return Level(
            lambda p: gn[n, p],
            lambda p: gh[n, p] + f1[next_, p],
            lambda p: an[n, p],
            lambda: rates[near],
            lambda: edge_rate[near],
            lambda: ends[2 + n],
            lambda: lateral[2 + n],
            store,
            src,
            flag_of(near),
        )

    sweep([over_level(*s) for s in sides], table)
    for n, msg, i, near, next_, over, ghost, factor in sides:

        def after(p):
            return next2[i, p] + (edge_rate[next_] if p == FIELDS else rates[next_]) * gn[n, p]

        level_sums(next_, info, after, after(FIELDS), strip, metric, metric_row, sums, out, next_)
    sweep([near_level(*s) for s in sides], table)
    for n, msg, i, near, *_ in sides:
        level_sums(near, info, lambda f: a2[n, f], a2[n, FIELDS], strip, metric, metric_row, sums, out, near)

    s1 = sums[1]
    stream = roll(s1, -1, 0)[:ROWS] - roll(s1, 1, 0)[:ROWS]
    t = sums[3, :ROWS]
    s2 = sums[2, :ROWS]
    lane = iota((ROWS, COLS), 1)
    right, left = roll(s2, -1, 1), roll(s2, 1, 1)
    high = [roll(t, COLS - 1 - (SLOT * f + 12), 1) for f in range(FIELDS)]
    low = [roll(t, -(SLOT * f + 3), 1) for f in range(FIELDS)]
    right = jnp.where(lane == COLS - 1, (high[0] + high[1] + high[2]) + (high[3] + high[4] + high[5]), right)
    left = jnp.where(lane == 0, (low[0] + low[1] + low[2]) + (low[3] + low[4] + low[5]), left)
    total = sums[0, :ROWS] - 0.5 * stream - 0.5 * (right - left)
    turned = jnp.concatenate([total, jnp.zeros((COLS - ROWS, COLS), jnp.float32)], 0).T
    for k in range(share.shape[0]):
        share[k] = turned[share.shape[1] * k : share.shape[1] * (k + 1)]


def add_shares(parts, out):
    total = parts[0]
    for i in range(1, parts.shape[0]):
        total = total + parts[i]
    out[...] = total[:, :ROWS]


def call(body, outs, ins, scratch=()):
    return pl.pallas_call(
        body,
        out_shape=outs,
        in_specs=ins,
        out_specs=jax.tree.map(lambda _: VM, outs),
        scratch_shapes=list(scratch),
        compiler_params=pltpu.CompilerParams(vmem_limit_bytes=16 << 20),
        cost_estimate=pl.CostEstimate(flops=1000000, bytes_accessed=1 << 20, transcendentals=0),
    )


def local(adjoint_start, eddy_visc, diag_coef, coupling, metric_terms, sample_cells, sample_weights, face_codes):
    index = [lax.axis_index(a) for a in ("gx", "gy", "gz")]
    count = [lax.axis_size(a) for a in ("gx", "gy", "gz")]
    info = jnp.stack(index + [jnp.int32(c) for c in count]).astype(jnp.int32)
    cells, weights = sample_cells.reshape(16, 128), sample_weights.reshape(16, 128)

    def shift(v, axis, step):
        n = lax.axis_size(axis)
        return lax.ppermute(v, axis, [(i, i + step) for i in range(n) if 0 <= i + step < n])

    def trade(v, axis, first):
        n = lax.axis_size(axis)
        pairs = [(i, i + 1) for i in range(first, n - 1, 2)]
        return lax.ppermute(v, axis, pairs + [(b, a) for a, b in pairs])

    def buf(*shape):
        return pltpu.VMEM(shape, jnp.float32)

    level = (LEV, ROWS, COLS)
    own, to_right, to_left = call(
        pack_y,
        (f32(*level), f32(2, ROWS, COLS), f32(2, ROWS, COLS)),
        [VM] * 4,
        [buf(*level)],
    )(adjoint_start, eddy_visc, diag_coef, metric_terms[2:3])
    from_left = shift(to_right, "gy", 1)
    from_right = shift(to_left, "gy", -1)
    strip, to_low, to_high = call(pack_x, (f32(*level),) * 3, [VM] * 7)(
        own, from_left, from_right, adjoint_start, eddy_visc, diag_coef, metric_terms
    )
    from_low = shift(to_high, "gx", 1)
    from_high = shift(to_low, "gx", -1)
    src, table = call(
        functools.partial(make_source, COLS * count[1]), (f32(2, EXT, COLS), f32(56, COLS)), [SM] * 3 + [VM] * 3
    )(info, face_codes, coupling, cells, weights, strip)
    received = (from_low, from_high, adjoint_start, eddy_visc, diag_coef)
    msg_b, msg_a = [
        call(functools.partial(pack_z, far), f32(16, EXT, COLS), [SM] + [VM] * 7)(info, table, strip, *received)
        for far in (True, False)
    ]
    from_b = trade(msg_b, "gz", 1)
    from_a = trade(msg_a, "gz", 0)
    ext = (EXT, COLS)
    inner = call(
        inner_levels,
        (
            f32(LEV, 7, *ext),
            f32(2, 7, *ext),
            f32(2, 7, *ext),
            f32(LEV, 7, *ext),
            f32(LEV, *ext),
            f32(LEV, *ext),
            f32(LEV, *ext),
            f32(FIELDS, LEV - 4, ROWS, COLS),
            f32(4, *ext),
            f32(LEV, 9, 8, COLS),
            f32(FIELDS, LEV, 8, COLS),
        ),
        [SM] + [VM] * 9,
        [buf(LEV, 7, *ext), buf(LEV, 7, *ext), buf(LEV, *ext), buf(LEV, *ext)],
    )(info, table, adjoint_start, eddy_visc, diag_coef, strip, from_low, from_high, metric_terms, src)
    adjoint, share = call(
        outer_levels,
        (f32(FIELDS, *level), f32(count[2], COLS // count[2], COLS)),
        [SM] + [VM] * 18,
        [buf(4, *ext)] + [buf(2, 7, *ext)] * 5 + [buf(2, 2, *ext), buf(4, *ext), buf(4, *ext)],
    )(info, table, eddy_visc, strip, from_b, from_a, metric_terms, src, *inner)
    parts = lax.all_to_all(share, "gz", 0, 0, tiled=True)
    height_grad = call(add_shares, f32(COLS // count[2], ROWS), [VM])(parts).T
    return (adjoint, height_grad)


def solution(mesh):
    return jax.shard_map(
        local,
        mesh=mesh,
        in_specs=(
            P(None, "gz", "gx", "gy"),
            P("gz", "gx", "gy"),
            P("gz", "gx", "gy"),
            P(),
            P(None, None, "gz", "gx", "gy"),
            P(),
            P(),
            P(),
        ),
        out_specs=(P(None, "gz", "gx", "gy"), P("gx", ("gy", "gz"))),
        check_vma=False,
    )
```

```python
import functools

import jax
import jax.numpy as jnp
from jax import lax
from jax.experimental import pallas as pl
from jax.experimental.pallas import tpu as pltpu
from jax.sharding import PartitionSpec as P

relax_rate = 0.9
keep_rate = 0.1

FIELDS = 6
LEV = 8
ROWS = 32
COLS = 128
EXT = 40
EDDY, RATE, STRIP = 6, 7, 8
SLOT = 16

VM = pl.BlockSpec(memory_space=pltpu.VMEM)
SM = pl.BlockSpec(memory_space=pltpu.SMEM)


def roll(v, shift, axis):
    return pltpu.roll(v, shift % v.shape[axis], axis)


def iota(shape, axis):
    return lax.broadcasted_iota(jnp.int32, shape, axis)


def f32(*shape):
    return jax.ShapeDtypeStruct(shape, jnp.float32)


def pipeline(tasks):
    held = None
    for begin, end in tasks:
        started = begin()
        if held is not None:
            held[0](held[1])
        held = (end, started)
    held[0](held[1])


class Either:
    def __init__(self, condition, first, second):
        self.condition, self.first, self.second = condition, first, second

    def __getitem__(self, at):
        return jnp.where(self.condition, self.first[at], self.second[at])


def two_sides(even, from_a, from_b):
    return Either(even, from_b, from_a), Either(even, from_a, from_b)


def pack_y(adj, eddy, diag, metric, own, msg_a, msg_b, packed):
    even = lax.axis_index("gy") % 2 == 0
    shape = (4, 8, COLS)
    lane = iota(shape, 2)
    slot, j = lane // SLOT, lane % SLOT
    quad, jj = j // 4, j % 4

    def block(zg, t):
        return pl.ds(4 * zg, 4), pl.ds(8 * t, 8)

    def gather(zg, t):
        zs, rows = block(zg, t)

        def planes(p):
            if p >= 8:
                return roll(metric[0, p - 8, zs, rows, :], SLOT * (p - 8) + 9, 2)
            v = adj[p, zs, rows, :] if p < FIELDS else eddy[zs, rows, :] if p == EDDY else relax_rate / diag[zs, rows, :]
            return roll(v, SLOT * p + 4, 2)

        def choose(p, v, c):
            if p >= 8:
                return jnp.where((slot == p - 8) & (j >= 8) & (j <= 9), v, c)
            return jnp.where((slot == p) & (j >= 1) & (j <= 6), v, c)

        c = jnp.zeros(shape, jnp.float32)
        ahead = [planes(0), planes(1), planes(2)]
        for p in range(14):
            if p + 3 < 14:
                ahead.append(planes(p + 3))
            c = choose(p, ahead[p], c)
        packed[zs, rows, :] = c

    def send(zg, t):
        zs, rows = block(zg, t)
        c = packed[zs, rows, :]
        c8 = roll(c, 8, 2)
        right = left = jnp.zeros((8, COLS), jnp.float32)
        moved = []
        for zq in range(4):
            at = 4 * zq
            moved.append([roll(c[zq], at + by, 1) for by in (-8, 0, -6, -4)])
        own[zs, rows, :] = jnp.where(j < 8, c, jnp.where(j >= 9, c8, 0.0))
        for zq in range(4):
            r0, r1, l0, l1 = moved[zq]
            here = quad[0] == zq
            right = jnp.where(here, jnp.where(jj[0] == 0, r0, r1), right)
            left = jnp.where(here, jnp.where(jj[0] == 3, l0, l1), left)
        msg_a[zg, rows, :] = jnp.where(even, right, left)
        msg_b[zg, rows, :] = jnp.where(even, left, right)

    blocks = [(zg, t) for zg in range(2) for t in range(ROWS // 8)]
    for zg, t in blocks:
        gather(zg, t)
    for zg, t in blocks:
        send(zg, t)


MIX, PAIR = 8, 16


def make_source(total_y, idx, codes, coup, cells, weights, after, src, table):
    slot = iota((1, COLS), 1) // SLOT
    for i in range(6):
        factor = jnp.where(codes[i] == 1, 1.0, jnp.where(codes[i] == 2, -1.0, 0.0)).astype(jnp.float32)
        table[i : i + 1, :] = jnp.full((1, COLS), factor)
    for e in range(FIELDS):
        v = jnp.zeros((1, COLS), jnp.float32)
        for f in range(FIELDS):
            v = jnp.where(slot == f, coup[e, f], v)
            at = PAIR + FIELDS * e + f
            table[at : at + 1, :] = jnp.full((1, COLS), coup[e, f])
        table[MIX + e : MIX + e + 1, :] = v
    start_x, start_y = idx[0] * ROWS, idx[1] * COLS
    r = iota((48, COLS), 0)
    row_x = jnp.where(r < EXT - 5, r, r - EXT) + start_x
    row_x = jnp.where(r < EXT, row_x, -1)
    l = iota((2 * COLS, COLS), 0)
    j = l - COLS
    col_y = jnp.where((j >= 1) & (j <= 6), j - 4, j + (COLS - 12))
    col_y = jnp.where(l < COLS, l, col_y) + start_y
    col_y = jnp.where((l < COLS) | ((j >= 1) & (j <= 6)) | ((j >= 9) & (j <= 14)), col_y, -1)
    acc = jnp.zeros((144, 2 * COLS), jnp.float32)
    for k in range(0, 16, 2):
        left, one = [], []
        for q in (k, k + 1):
            c = cells[q : q + 1, :]
            w = weights[q : q + 1, :]
            x = ((c.astype(jnp.float32) + 0.5) * (1.0 / total_y)).astype(jnp.int32)
            y = c - x * total_y
            high = w.astype(jnp.bfloat16).astype(jnp.float32)
            mid = (w - high).astype(jnp.bfloat16).astype(jnp.float32)
            low = w - high - mid
            hit = row_x == x
            left.append(jnp.concatenate([jnp.where(hit, v, 0.0).astype(jnp.bfloat16) for v in (low, mid, high)], 0))
            one.append(jnp.where(col_y == y, 1.0, 0.0).astype(jnp.bfloat16))
        acc = acc + lax.dot_general(
            jnp.concatenate(left, 1),
            jnp.concatenate(one, 1),
            (((1,), (1,)), ((), ())),
            preferred_element_type=jnp.float32,
        )
    total = acc[0:EXT, :] + acc[48 : 48 + EXT, :] + acc[96 : 96 + EXT, :]
    src[0] = total[:, :COLS]
    src[1] = total[:, COLS:]


HIGH_AT = [0, 3, 6, 9, 12, 15, 18, 21, 23]
LOW_AT = [6 + a for a in HIGH_AT]
HIGH_METRIC, LOW_METRIC = 26, 0


def pack_x(info, own, from_a, from_b, adj, eddy, diag, metric, strip, msg_a, msg_b, to_low, to_high):
    from_left, from_right = two_sides(info[1] % 2 == 0, from_a, from_b)
    even = info[0] % 2 == 0
    j = iota((ROWS, COLS), 1) % SLOT
    for z in range(LEV):
        zg, at = z // 4, 4 * (z % 4)
        low = roll(from_left[zg], -at, 1)
        high = roll(from_right[zg], 12 - at, 1)
        s = jnp.where(j < 4, low, jnp.where(j >= 12, high, own[z]))
        strip[z] = s
        sides = ((to_low, 0, 0, 0, HIGH_AT, HIGH_METRIC), (to_high, ROWS - 3, ROWS - 2, ROWS - 1, LOW_AT, LOW_METRIC))
        for msg, a, b, near, at, metric_at in sides:
            for p in range(FIELDS):
                msg[z, at[p] : at[p] + 3, :] = adj[p, z, a : a + 3, :]
                msg[z, metric_at + p : metric_at + p + 1, :] = metric[1, p, z, near : near + 1, :]
            msg[z, at[EDDY] : at[EDDY] + 3, :] = eddy[z, a : a + 3, :]
            msg[z, at[RATE] : at[RATE] + 2, :] = relax_rate / diag[z, b : b + 2, :]
            msg[z, at[STRIP] : at[STRIP] + 3, :] = s[a : a + 3, :]
    for z in range(LEV):
        low, high = to_low[z], to_high[z]
        msg_a[z] = jnp.where(even, high, low)
        msg_b[z] = jnp.where(even, low, high)


def lanes_of(v, plane):
    return jnp.take_along_axis(v, iota(v.shape, 1) % SLOT + SLOT * plane, axis=1)


class Edges:
    def __init__(self, info, table):
        self.low_x, self.high_x = info[0] == 0, info[0] == info[3] - 1
        self.low_y, self.high_y = info[1] == 0, info[1] == info[4] - 1
        self.low_z, self.high_z = info[2] == 0, info[2] == info[5] - 1
        self.factors = [table[i : i + 1, :] for i in range(6)]
        row, j = iota((8, COLS), 0), iota((EXT, COLS), 1) % SLOT
        self.row_low, self.row_high = (row == 7) & self.low_x, (row == 0) & self.high_x
        self.j = j
        self.ghost_low, self.ghost_high = (j == 3) & self.low_y, (j == 12) & self.high_y
        self.own_low, self.own_high = (j == 4) & self.low_y, (j == 11) & self.high_y

    def flux(self, v):
        t4 = v[32:40]
        t4 = jnp.where(self.row_low, self.factors[0] * roll(v[0:8], 7, 0), t4)
        t4 = jnp.where(self.row_high, self.factors[1] * roll(v[24:32], 1, 0), t4)
        return jnp.concatenate([v[0:32], t4], 0)


class Level:
    def __init__(self, center, vertical, value, rate, edge_rate, ends, lateral, store, src=None, flag=None):
        self.center, self.vertical, self.value = center, vertical, value
        self.rate, self.edge_rate, self.ends, self.lateral = rate, edge_rate, ends, lateral
        self.store, self.src, self.flag = store, src, flag


def prepare(edges, strips, ends, lateral):
    f2, f3 = edges.factors[2], edges.factors[3]

    def task(at, strip):
        def end(moved):
            v, up, down = moved
            ends[at] = jnp.where(edges.ghost_low, f2 * down, jnp.where(edges.ghost_high, f3 * up, v))
            lateral[at] = jnp.where(edges.own_low, f2 * v, up) + jnp.where(edges.own_high, f3 * v, down)

        def begin():
            v = strip()
            return v, roll(v, 1, 1), roll(v, -1, 1)

        return begin, end

    def turn(at, _):
        def begin():
            v = ends[at]
            return v, roll(v, -10, 1)

        def end(moved):
            ends[at] = jnp.where(edges.j == 3, *moved)

        return begin, end

    pipeline([task(*s) for s in strips])
    pipeline([turn(*s) for s in strips])


def sweep(levels, table):
    lane = iota((EXT, COLS), 1)
    half = FIELDS // 2

    def pair(e, f):
        at = PAIR + FIELDS * e + f
        return table[at : at + 1, :]

    def field(level, f):
        def begin():
            v = level.center(f)
            return v, roll(level.ends(), -(SLOT * f + 3), 1), roll(v, 1, 1), roll(v, -1, 1)

        def end(moved):
            v, edge, left, right = moved
            left = jnp.where(lane == 0, edge, left)
            right = jnp.where(lane == COLS - 1, edge, right)
            beside = level.vertical(f) + roll(v, -1, 0) + roll(v, 1, 0) + right + left
            coupled = pair(0, f) * level.value(0)
            for e in range(1, FIELDS):
                coupled = coupled + pair(e, f) * level.value(e)
            rest = beside - coupled
            if f == 0 and level.src is not None:
                rest = rest + level.flag * level.src[0]
            level.store(f, keep_rate * level.value(f) + level.rate() * rest)

        return begin, end

    def strip(level):
        sums = []

        def mixed(first):
            def begin():
                a = level.value(FIELDS)
                return [lanes_of(a, e) for e in range(first, first + half)]

            def end(moved):
                terms = [v * table[MIX + first + i : MIX + first + i + 1, :] for i, v in enumerate(moved)]
                sums.append(terms[0] + terms[1] + terms[2])

            return begin, end

        def end(_):
            v = level.center(FIELDS)
            rest = level.vertical(FIELDS) + roll(v, -1, 0) + roll(v, 1, 0) + level.lateral() - (sums[0] + sums[1])
            if level.src is not None:
                rest = rest + level.flag * level.src[1]
            level.store(FIELDS, keep_rate * level.value(FIELDS) + level.edge_rate() * rest)

        return [mixed(0), mixed(half), (lambda: None, end)]

    pipeline([task for level in levels for task in strip(level) + [field(level, f) for f in range(FIELDS)]])


def level_sums(z, info, field, edge_strip, strip, metric, metric_row, sums, out, zo):
    total_z = (info[5] * LEV).astype(jnp.float32)
    w = 1.0 - 0.5 * (((info[2] * LEV + z).astype(jnp.float32) + 0.5) / total_z)
    totals = None
    for f in range(FIELDS):
        a = field(f)
        own = a[:ROWS]
        out[f, zo] = own
        terms = [metric[k, f, z] * own for k in range(3)] + [metric_row[f, z] * a[ROWS:]]
        totals = terms if f == 0 else [s + t for s, t in zip(totals, terms)]
    s = strip[z, :ROWS]
    j = iota((ROWS, COLS), 1) % SLOT
    m = jnp.where(j == 3, roll(s, 3, 1), jnp.where(j == 12, roll(s, -3, 1), 0.0))
    sums[0, :ROWS] += w * totals[0]
    sums[1, :ROWS] += w * totals[1]
    sums[1, ROWS:] += w * totals[3]
    sums[2, :ROWS] += w * totals[2]
    sums[3, :ROWS] += w * (m * edge_strip[:ROWS])


def halo_tile(from_low, from_high, z, p):
    at = 2 if p == RATE else 3
    start = LOW_AT[p] - (8 - at)
    above, below = from_high[z, pl.ds(HIGH_AT[p], 8), :], from_low[z, pl.ds(start, 8), :]
    return jnp.where(iota((8, COLS), 0) < 4, above, below)


def pack_z(far, info, table, strip, from_a, from_b, adj, eddy, diag, msg):
    from_low, from_high = two_sides(info[0] % 2 == 0, from_a, from_b)
    edges = Edges(info, table)
    top = (info[2] % 2 == 0) != far

    def plane(z, p):
        own = adj[p, z] if p < FIELDS else eddy[z] if p == EDDY else relax_rate / diag[z] if p == RATE else strip[z]
        return jnp.concatenate([own, halo_tile(from_low, from_high, z, p)], 0)

    near = jnp.where(top, LEV - 1, 0)
    next_ = jnp.where(top, LEV - 2, 1)
    for p in range(9):
        msg[p] = plane(near, p)
    e = plane(next_, EDDY)
    for f in range(FIELDS):
        msg[9 + f] = edges.flux(plane(next_, f) * e)
    s = plane(next_, STRIP)
    msg[15] = edges.flux(s * lanes_of(s, EDDY))


def inner_levels(
    info, table, adj, eddy, diag, strip, from_a, from_b, metric, src,
    f0, near1, next2, f1, rates, edge_eddy, edge_rate, out, sums, halo, metric_row, a1, a2, ends, lateral,
):
    from_low, from_high = two_sides(info[0] % 2 == 0, from_a, from_b)
    edges = Edges(info, table)
    row = iota((8, COLS), 0)
    for z in range(LEV):
        for p in range(9):
            halo[z, p] = halo_tile(from_low, from_high, z, p)
        for f in range(FIELDS):
            above = jnp.broadcast_to(from_high[z, HIGH_METRIC + f : HIGH_METRIC + f + 1, :], (8, COLS))
            below = jnp.broadcast_to(from_low[z, LOW_METRIC + f : LOW_METRIC + f + 1, :], (8, COLS))
            metric_row[f, z] = jnp.where(row < 4, above, below)
    hub = info[5] * LEV // 4 - info[2] * LEV
    flag = jnp.where(hub == 0, 1.0, 0.0).astype(jnp.float32)

    def value(z, p):
        own = adj[p, z] if p < FIELDS else strip[z]
        return jnp.concatenate([own, halo[z, STRIP if p == FIELDS else p]], 0)

    def eddies(z):
        return jnp.concatenate([eddy[z], halo[z, EDDY]], 0)

    for z in range(LEV):
        rates[z] = jnp.concatenate([relax_rate / diag[z], halo[z, RATE]], 0)
        s = value(z, FIELDS)
        edge_eddy[z] = lanes_of(s, EDDY)
        edge_rate[z] = lanes_of(s, RATE)
    for z in range(LEV):
        e = eddies(z)
        for f in range(FIELDS):
            f0[z, f] = edges.flux(value(z, f) * e)
        f0[z, FIELDS] = edges.flux(value(z, FIELDS) * edge_eddy[z])

    def strips_of(array, zs):
        return [(z, lambda z=z: array[z, FIELDS]) for z in zs]

    def level(z, flux, value, vertical, store, **more):
        return Level(
            lambda p: flux[z, p],
            vertical,
            lambda p: value(z, p),
            lambda: rates[z],
            lambda: edge_rate[z],
            lambda: ends[z],
            lambda: lateral[z],
            store,
            **more,
        )

    def store_first(z):
        def store(p, v):
            if z in (0, LEV - 1):
                near1[z // (LEV - 1), p] = v
            else:
                a1[z, p] = v
                f1[z, p] = edges.flux(v * (edge_eddy[z] if p == FIELDS else eddies(z)))

        return store

    def store_second(z):
        def store(p, v):
            if z in (1, LEV - 2):
                next2[z // (LEV - 2), p] = v
            else:
                a2[z, p] = v

        return store

    def around(array, z, low, high):
        if z == low:
            return lambda p: array[z + 1, p]
        if z == high:
            return lambda p: array[z - 1, p]
        return lambda p: array[z - 1, p] + array[z + 1, p]

    prepare(edges, strips_of(f0, range(LEV)), ends, lateral)
    sweep(
        [
            level(z, f0, value, around(f0, z, 0, LEV - 1), store_first(z), **({"src": src, "flag": flag} if z == 0 else {}))
            for z in range(LEV)
        ],
        table,
    )
    inside = range(1, LEV - 1)
    prepare(edges, strips_of(f1, inside), ends, lateral)
    sweep([level(z, f1, lambda z, p: a1[z, p], around(f1, z, 1, LEV - 2), store_second(z)) for z in inside], table)
    sums[...] = jnp.zeros_like(sums)
    for z in range(2, LEV - 2):
        level_sums(z, info, lambda f: a2[z, f], a2[z, FIELDS], strip, metric, metric_row, sums, out, z - 2)


def outer_levels(
    info, table, eddy, strip, from_b, from_a, metric, src,
    f0, near1, next2, f1, rates, edge_eddy, edge_rate, inner_out, inner_sums, halo_rows, metric_row,
    out, share, sums, fh, gh, an, gn, a2, edge_over, ends, lateral,
):
    edges = Edges(info, table)
    hub = info[5] * LEV // 4 - info[2] * LEV
    sums[...] = inner_sums[...]
    for f in range(FIELDS):
        for z in range(2, LEV - 2):
            out[f, z] = inner_out[f, z - 2]
    even = info[2] % 2 == 0

    def flag_of(z):
        return jnp.where(z == hub, 1.0, 0.0).astype(jnp.float32)

    def side(n, msg):
        top = even if n == 0 else jnp.logical_not(even)
        near, next_ = jnp.where(top, LEV - 1, 0), jnp.where(top, LEV - 2, 1)
        ghost = jnp.where(top, edges.high_z, edges.low_z)
        factor = jnp.where(top, edges.factors[5], edges.factors[4])
        return n, msg, jnp.where(top, 1, 0), near, next_, jnp.where(top, LEV, -1), ghost, factor

    sides = [side(0, from_a), side(1, from_b)]
    for n, msg, *_ in sides:
        edge_over[n, 0] = lanes_of(msg[STRIP], EDDY)
        edge_over[n, 1] = lanes_of(msg[STRIP], RATE)
    for n, msg, i, near, next_, over, ghost, factor in sides:
        eddy_near = jnp.concatenate([eddy[near], halo_rows[near, EDDY]], 0)
        for p in (FIELDS, *range(FIELDS)):
            v = msg[STRIP] * edge_over[n, 0] if p == FIELDS else msg[p] * msg[EDDY]
            v = jnp.where(ghost, factor * f0[near, p], edges.flux(v))
            fh[n, p] = v
            r, e = (edge_rate[near], edge_eddy[near]) if p == FIELDS else (rates[near], eddy_near)
            v = near1[i, p] + r * v
            an[n, p] = v
            gn[n, p] = edges.flux(v * e)
    prepare(edges, [(n, lambda n=n: fh[n, FIELDS]) for n in range(2)], ends, lateral)
    prepare(edges, [(2 + n, lambda n=n: gn[n, FIELDS]) for n in range(2)], ends, lateral)

    def over_level(n, msg, i, near, next_, over, ghost, factor):
        def store(p, v):
            v = edges.flux(v * (edge_over[n, 0] if p == FIELDS else msg[EDDY]))
            gh[n, p] = jnp.where(ghost, factor * gn[n, p], v)

        return Level(
            lambda p: fh[n, p],
            lambda p: msg[9 + p] + f0[near, p],
            lambda p: msg[STRIP if p == FIELDS else p],
            lambda: msg[RATE],
            lambda: edge_over[n, 1],
            lambda: ends[n],
            lambda: lateral[n],
            store,
            src,
            flag_of(over),
        )

    def near_level(n, msg, i, near, next_, over, ghost, factor):
        def store(p, v):
            a2[n, p] = v

        return Level(
            lambda p: gn[n, p],
            lambda p: gh[n, p] + f1[next_, p],
            lambda p: an[n, p],
            lambda: rates[near],
            lambda: edge_rate[near],
            lambda: ends[2 + n],
            lambda: lateral[2 + n],
            store,
            src,
            flag_of(near),
        )

    sweep([over_level(*s) for s in sides], table)
    for n, msg, i, near, next_, over, ghost, factor in sides:

        def after(p):
            return next2[i, p] + (edge_rate[next_] if p == FIELDS else rates[next_]) * gn[n, p]

        level_sums(next_, info, after, after(FIELDS), strip, metric, metric_row, sums, out, next_)
    sweep([near_level(*s) for s in sides], table)
    for n, msg, i, near, *_ in sides:
        level_sums(near, info, lambda f: a2[n, f], a2[n, FIELDS], strip, metric, metric_row, sums, out, near)

    s1 = sums[1]
    stream = roll(s1, -1, 0)[:ROWS] - roll(s1, 1, 0)[:ROWS]
    t = sums[3, :ROWS]
    s2 = sums[2, :ROWS]
    lane = iota((ROWS, COLS), 1)
    right, left = roll(s2, -1, 1), roll(s2, 1, 1)
    high = [roll(t, COLS - 1 - (SLOT * f + 12), 1) for f in range(FIELDS)]
    low = [roll(t, -(SLOT * f + 3), 1) for f in range(FIELDS)]
    right = jnp.where(lane == COLS - 1, (high[0] + high[1] + high[2]) + (high[3] + high[4] + high[5]), right)
    left = jnp.where(lane == 0, (low[0] + low[1] + low[2]) + (low[3] + low[4] + low[5]), left)
    total = sums[0, :ROWS] - 0.5 * stream - 0.5 * (right - left)
    turned = jnp.concatenate([total, jnp.zeros((COLS - ROWS, COLS), jnp.float32)], 0).T
    for k in range(share.shape[0]):
        share[k] = turned[share.shape[1] * k : share.shape[1] * (k + 1)]


def add_shares(parts, out):
    total = parts[0]
    for i in range(1, parts.shape[0]):
        total = total + parts[i]
    out[...] = total[:, :ROWS]


def call(body, outs, ins, scratch=()):
    return pl.pallas_call(
        body,
        out_shape=outs,
        in_specs=ins,
        out_specs=jax.tree.map(lambda _: VM, outs),
        scratch_shapes=list(scratch),
        compiler_params=pltpu.CompilerParams(vmem_limit_bytes=16 << 20),
        cost_estimate=pl.CostEstimate(flops=1000000, bytes_accessed=1 << 20, transcendentals=0),
    )


def local(adjoint_start, eddy_visc, diag_coef, coupling, metric_terms, sample_cells, sample_weights, face_codes):
    index = [lax.axis_index(a) for a in ("gx", "gy", "gz")]
    count = [lax.axis_size(a) for a in ("gx", "gy", "gz")]
    info = jnp.stack(index + [jnp.int32(c) for c in count]).astype(jnp.int32)
    cells, weights = sample_cells.reshape(16, 128), sample_weights.reshape(16, 128)

    def trade(v, axis, first):
        n = lax.axis_size(axis)
        pairs = [(i, i + 1) for i in range(first, n - 1, 2)]
        return lax.ppermute(v, axis, pairs + [(b, a) for a, b in pairs])

    def buf(*shape):
        return pltpu.VMEM(shape, jnp.float32)

    level = (LEV, ROWS, COLS)
    own, msg_a, msg_b = call(
        pack_y,
        (f32(*level), f32(2, ROWS, COLS), f32(2, ROWS, COLS)),
        [VM] * 4,
        [buf(*level)],
    )(adjoint_start, eddy_visc, diag_coef, metric_terms[2:3])
    beside = trade(msg_a, "gy", 0), trade(msg_b, "gy", 1)
    strip, msg_a, msg_b = call(pack_x, (f32(*level),) * 3, [SM] + [VM] * 7, [buf(*level)] * 2)(
        info, own, *beside, adjoint_start, eddy_visc, diag_coef, metric_terms
    )
    beside = trade(msg_a, "gx", 0), trade(msg_b, "gx", 1)
    src, table = call(
        functools.partial(make_source, COLS * count[1]), (f32(2, EXT, COLS), f32(56, COLS)), [SM] * 3 + [VM] * 3
    )(info, face_codes, coupling, cells, weights, strip)
    received = (*beside, adjoint_start, eddy_visc, diag_coef)
    msg_b, msg_a = [
        call(functools.partial(pack_z, far), f32(16, EXT, COLS), [SM] + [VM] * 7)(info, table, strip, *received)
        for far in (True, False)
    ]
    from_b = trade(msg_b, "gz", 1)
    from_a = trade(msg_a, "gz", 0)
    ext = (EXT, COLS)
    inner = call(
        inner_levels,
        (
            f32(LEV, 7, *ext),
            f32(2, 7, *ext),
            f32(2, 7, *ext),
            f32(LEV, 7, *ext),
            f32(LEV, *ext),
            f32(LEV, *ext),
            f32(LEV, *ext),
            f32(FIELDS, LEV - 4, ROWS, COLS),
            f32(4, *ext),
            f32(LEV, 9, 8, COLS),
            f32(FIELDS, LEV, 8, COLS),
        ),
        [SM] + [VM] * 9,
        [buf(LEV, 7, *ext), buf(LEV, 7, *ext), buf(LEV, *ext), buf(LEV, *ext)],
    )(info, table, adjoint_start, eddy_visc, diag_coef, strip, *beside, metric_terms, src)
    adjoint, share = call(
        outer_levels,
        (f32(FIELDS, *level), f32(count[2], COLS // count[2], COLS)),
        [SM] + [VM] * 18,
        [buf(4, *ext)] + [buf(2, 7, *ext)] * 5 + [buf(2, 2, *ext), buf(4, *ext), buf(4, *ext)],
    )(info, table, eddy_visc, strip, from_b, from_a, metric_terms, src, *inner)
    parts = lax.all_to_all(share, "gz", 0, 0, tiled=True)
    height_grad = call(add_shares, f32(COLS // count[2], ROWS), [VM])(parts).T
    return (adjoint, height_grad)


def solution(mesh):
    return jax.shard_map(
        local,
        mesh=mesh,
        in_specs=(
            P(None, "gz", "gx", "gy"),
            P("gz", "gx", "gy"),
            P("gz", "gx", "gy"),
            P(),
            P(None, None, "gz", "gx", "gy"),
            P(),
            P(),
            P(),
        ),
        out_specs=(P(None, "gz", "gx", "gy"), P("gx", ("gy", "gz"))),
        check_vma=False,
    )
```

```python
import functools

import jax
import jax.numpy as jnp
from jax import lax
from jax.experimental import pallas as pl
from jax.experimental.pallas import tpu as pltpu
from jax.sharding import PartitionSpec as P

relax_rate = 0.9
keep_rate = 0.1

FIELDS = 6
LEV = 8
ROWS = 32
COLS = 128
EXT = 40
EDDY, RATE, STRIP = 6, 7, 8
SLOT = 16

VM = pl.BlockSpec(memory_space=pltpu.VMEM)
SM = pl.BlockSpec(memory_space=pltpu.SMEM)


def roll(v, shift, axis):
    return pltpu.roll(v, shift % v.shape[axis], axis)


def iota(shape, axis):
    return lax.broadcasted_iota(jnp.int32, shape, axis)


def f32(*shape):
    return jax.ShapeDtypeStruct(shape, jnp.float32)


def pipeline(tasks):
    held = None
    for begin, end in tasks:
        started = begin()
        if held is not None:
            held[0](held[1])
        held = (end, started)
    held[0](held[1])


def place():
    return [lax.axis_index(a) for a in ("gx", "gy", "gz")] + [lax.axis_size(a) for a in ("gx", "gy", "gz")]


class Either:
    def __init__(self, condition, first, second):
        self.condition, self.first, self.second = condition, first, second

    def __getitem__(self, at):
        return jnp.where(self.condition, self.first[at], self.second[at])


def two_sides(even, from_a, from_b):
    return Either(even, from_b, from_a), Either(even, from_a, from_b)


def pack_y(adj, eddy, diag, metric, own, msg_a, msg_b, packed):
    even = place()[1] % 2 == 0
    shape = (4, 8, COLS)
    lane = iota(shape, 2)
    slot, j = lane // SLOT, lane % SLOT
    quad, jj = j // 4, j % 4

    def block(zg, t):
        return pl.ds(4 * zg, 4), pl.ds(8 * t, 8)

    def gather(zg, t):
        zs, rows = block(zg, t)

        def planes(p):
            if p >= 8:
                return roll(metric[0, p - 8, zs, rows, :], SLOT * (p - 8) + 9, 2)
            v = adj[p, zs, rows, :] if p < FIELDS else eddy[zs, rows, :] if p == EDDY else relax_rate / diag[zs, rows, :]
            return roll(v, SLOT * p + 4, 2)

        def choose(p, v, c):
            if p >= 8:
                return jnp.where((slot == p - 8) & (j >= 8) & (j <= 9), v, c)
            return jnp.where((slot == p) & (j >= 1) & (j <= 6), v, c)

        c = jnp.zeros(shape, jnp.float32)
        ahead = [planes(0), planes(1), planes(2)]
        for p in range(14):
            if p + 3 < 14:
                ahead.append(planes(p + 3))
            c = choose(p, ahead[p], c)
        packed[zs, rows, :] = c

    def send(zg, t):
        zs, rows = block(zg, t)
        c = packed[zs, rows, :]
        c8 = roll(c, 8, 2)
        right = left = jnp.zeros((8, COLS), jnp.float32)
        moved = []
        for zq in range(4):
            at = 4 * zq
            moved.append([roll(c[zq], at + by, 1) for by in (-8, 0, -6, -4)])
        own[zs, rows, :] = jnp.where(j < 8, c, jnp.where(j >= 9, c8, 0.0))
        for zq in range(4):
            r0, r1, l0, l1 = moved[zq]
            here = quad[0] == zq
            right = jnp.where(here, jnp.where(jj[0] == 0, r0, r1), right)
            left = jnp.where(here, jnp.where(jj[0] == 3, l0, l1), left)
        msg_a[zg, rows, :] = jnp.where(even, right, left)
        msg_b[zg, rows, :] = jnp.where(even, left, right)

    blocks = [(zg, t) for zg in range(2) for t in range(ROWS // 8)]
    for zg, t in blocks:
        gather(zg, t)
    for zg, t in blocks:
        send(zg, t)


MIX, PAIR = 8, 16


def make_source(codes, coup, cells, weights, after, src, table):
    slot = iota((1, COLS), 1) // SLOT
    for i in range(6):
        factor = jnp.where(codes[i] == 1, 1.0, jnp.where(codes[i] == 2, -1.0, 0.0)).astype(jnp.float32)
        table[i : i + 1, :] = jnp.full((1, COLS), factor)
    for e in range(FIELDS):
        v = jnp.zeros((1, COLS), jnp.float32)
        for f in range(FIELDS):
            v = jnp.where(slot == f, coup[e, f], v)
            at = PAIR + FIELDS * e + f
            table[at : at + 1, :] = jnp.full((1, COLS), coup[e, f])
        table[MIX + e : MIX + e + 1, :] = v
    info = place()
    start_x, start_y, total_y = info[0] * ROWS, info[1] * COLS, info[4] * COLS
    r = iota((48, COLS), 0)
    row_x = jnp.where(r < EXT - 5, r, r - EXT) + start_x
    row_x = jnp.where(r < EXT, row_x, -1)
    l = iota((2 * COLS, COLS), 0)
    j = l - COLS
    col_y = jnp.where((j >= 1) & (j <= 6), j - 4, j + (COLS - 12))
    col_y = jnp.where(l < COLS, l, col_y) + start_y
    col_y = jnp.where((l < COLS) | ((j >= 1) & (j <= 6)) | ((j >= 9) & (j <= 14)), col_y, -1)
    acc = jnp.zeros((144, 2 * COLS), jnp.float32)
    for k in range(0, 16, 2):
        left, one = [], []
        for q in (k, k + 1):
            c = cells[q : q + 1, :]
            w = weights[q : q + 1, :]
            x = ((c.astype(jnp.float32) + 0.5) * (1.0 / total_y)).astype(jnp.int32)
            y = c - x * total_y
            high = w.astype(jnp.bfloat16).astype(jnp.float32)
            mid = (w - high).astype(jnp.bfloat16).astype(jnp.float32)
            low = w - high - mid
            hit = row_x == x
            left.append(jnp.concatenate([jnp.where(hit, v, 0.0).astype(jnp.bfloat16) for v in (low, mid, high)], 0))
            one.append(jnp.where(col_y == y, 1.0, 0.0).astype(jnp.bfloat16))
        acc = acc + lax.dot_general(
            jnp.concatenate(left, 1),
            jnp.concatenate(one, 1),
            (((1,), (1,)), ((), ())),
            preferred_element_type=jnp.float32,
        )
    total = acc[0:EXT, :] + acc[48 : 48 + EXT, :] + acc[96 : 96 + EXT, :]
    src[0] = total[:, :COLS]
    src[1] = total[:, COLS:]


HIGH_AT = [0, 3, 6, 9, 12, 15, 18, 21, 23]
LOW_AT = [6 + a for a in HIGH_AT]
HIGH_METRIC, LOW_METRIC = 26, 0


def pack_x(own, from_a, from_b, adj, eddy, diag, metric, strip, msg_a, msg_b, to_low, to_high):
    info = place()
    from_left, from_right = two_sides(info[1] % 2 == 0, from_a, from_b)
    even = info[0] % 2 == 0
    j = iota((ROWS, COLS), 1) % SLOT
    for z in range(LEV):
        zg, at = z // 4, 4 * (z % 4)
        low = roll(from_left[zg], -at, 1)
        high = roll(from_right[zg], 12 - at, 1)
        s = jnp.where(j < 4, low, jnp.where(j >= 12, high, own[z]))
        strip[z] = s
        sides = ((to_low, 0, 0, 0, HIGH_AT, HIGH_METRIC), (to_high, ROWS - 3, ROWS - 2, ROWS - 1, LOW_AT, LOW_METRIC))
        for msg, a, b, near, at, metric_at in sides:
            for p in range(FIELDS):
                msg[z, at[p] : at[p] + 3, :] = adj[p, z, a : a + 3, :]
                msg[z, metric_at + p : metric_at + p + 1, :] = metric[1, p, z, near : near + 1, :]
            msg[z, at[EDDY] : at[EDDY] + 3, :] = eddy[z, a : a + 3, :]
            msg[z, at[RATE] : at[RATE] + 2, :] = relax_rate / diag[z, b : b + 2, :]
            msg[z, at[STRIP] : at[STRIP] + 3, :] = s[a : a + 3, :]
    for z in range(LEV):
        low, high = to_low[z], to_high[z]
        msg_a[z] = jnp.where(even, high, low)
        msg_b[z] = jnp.where(even, low, high)


def lanes_of(v, plane):
    return jnp.take_along_axis(v, iota(v.shape, 1) % SLOT + SLOT * plane, axis=1)


class Edges:
    def __init__(self, info, table):
        self.low_x, self.high_x = info[0] == 0, info[0] == info[3] - 1
        self.low_y, self.high_y = info[1] == 0, info[1] == info[4] - 1
        self.low_z, self.high_z = info[2] == 0, info[2] == info[5] - 1
        self.factors = [table[i : i + 1, :] for i in range(6)]
        row, j = iota((8, COLS), 0), iota((EXT, COLS), 1) % SLOT
        self.row_low, self.row_high = (row == 7) & self.low_x, (row == 0) & self.high_x
        self.j = j
        self.ghost_low, self.ghost_high = (j == 3) & self.low_y, (j == 12) & self.high_y
        self.own_low, self.own_high = (j == 4) & self.low_y, (j == 11) & self.high_y

    def flux(self, v):
        t4 = v[32:40]
        t4 = jnp.where(self.row_low, self.factors[0] * roll(v[0:8], 7, 0), t4)
        t4 = jnp.where(self.row_high, self.factors[1] * roll(v[24:32], 1, 0), t4)
        return jnp.concatenate([v[0:32], t4], 0)


class Level:
    def __init__(self, center, vertical, value, rate, edge_rate, ends, lateral, store, src=None, flag=None):
        self.center, self.vertical, self.value = center, vertical, value
        self.rate, self.edge_rate, self.ends, self.lateral = rate, edge_rate, ends, lateral
        self.store, self.src, self.flag = store, src, flag


def prepare(edges, strips, ends, lateral):
    f2, f3 = edges.factors[2], edges.factors[3]

    def task(at, strip):
        def end(moved):
            v, up, down = moved
            ends[at] = jnp.where(edges.ghost_low, f2 * down, jnp.where(edges.ghost_high, f3 * up, v))
            lateral[at] = jnp.where(edges.own_low, f2 * v, up) + jnp.where(edges.own_high, f3 * v, down)

        def begin():
            v = strip()
            return v, roll(v, 1, 1), roll(v, -1, 1)

        return begin, end

    def turn(at, _):
        def begin():
            v = ends[at]
            return v, roll(v, -10, 1)

        def end(moved):
            ends[at] = jnp.where(edges.j == 3, *moved)

        return begin, end

    pipeline([task(*s) for s in strips])
    pipeline([turn(*s) for s in strips])


def sweep(levels, table):
    lane = iota((EXT, COLS), 1)
    half = FIELDS // 2

    def pair(e, f):
        at = PAIR + FIELDS * e + f
        return table[at : at + 1, :]

    def field(level, f):
        def begin():
            v = level.center(f)
            return v, roll(level.ends(), -(SLOT * f + 3), 1), roll(v, 1, 1), roll(v, -1, 1)

        def end(moved):
            v, edge, left, right = moved
            left = jnp.where(lane == 0, edge, left)
            right = jnp.where(lane == COLS - 1, edge, right)
            beside = level.vertical(f) + roll(v, -1, 0) + roll(v, 1, 0) + right + left
            coupled = pair(0, f) * level.value(0)
            for e in range(1, FIELDS):
                coupled = coupled + pair(e, f) * level.value(e)
            rest = beside - coupled
            if f == 0 and level.src is not None:
                rest = rest + level.flag * level.src[0]
            level.store(f, keep_rate * level.value(f) + level.rate() * rest)

        return begin, end

    def strip(level):
        sums = []

        def mixed(first):
            def begin():
                a = level.value(FIELDS)
                return [lanes_of(a, e) for e in range(first, first + half)]

            def end(moved):
                terms = [v * table[MIX + first + i : MIX + first + i + 1, :] for i, v in enumerate(moved)]
                sums.append(terms[0] + terms[1] + terms[2])

            return begin, end

        def end(_):
            v = level.center(FIELDS)
            rest = level.vertical(FIELDS) + roll(v, -1, 0) + roll(v, 1, 0) + level.lateral() - (sums[0] + sums[1])
            if level.src is not None:
                rest = rest + level.flag * level.src[1]
            level.store(FIELDS, keep_rate * level.value(FIELDS) + level.edge_rate() * rest)

        return [mixed(0), mixed(half), (lambda: None, end)]

    pipeline([task for level in levels for task in strip(level) + [field(level, f) for f in range(FIELDS)]])


def level_sums(z, info, field, edge_strip, strip, metric, metric_row, sums, out, zo):
    total_z = info[5] * LEV
    w = 1.0 - 0.5 * ((jnp.int32(info[2] * LEV + z).astype(jnp.float32) + 0.5) / total_z)
    totals = None
    for f in range(FIELDS):
        a = field(f)
        own = a[:ROWS]
        out[f, zo] = own
        terms = [metric[k, f, z] * own for k in range(3)] + [metric_row[f, z] * a[ROWS:]]
        totals = terms if f == 0 else [s + t for s, t in zip(totals, terms)]
    s = strip[z, :ROWS]
    j = iota((ROWS, COLS), 1) % SLOT
    m = jnp.where(j == 3, roll(s, 3, 1), jnp.where(j == 12, roll(s, -3, 1), 0.0))
    sums[0, :ROWS] += w * totals[0]
    sums[1, :ROWS] += w * totals[1]
    sums[1, ROWS:] += w * totals[3]
    sums[2, :ROWS] += w * totals[2]
    sums[3, :ROWS] += w * (m * edge_strip[:ROWS])


def halo_tile(from_low, from_high, z, p):
    at = 2 if p == RATE else 3
    start = LOW_AT[p] - (8 - at)
    above, below = from_high[z, pl.ds(HIGH_AT[p], 8), :], from_low[z, pl.ds(start, 8), :]
    return jnp.where(iota((8, COLS), 0) < 4, above, below)


def pack_z(far, table, strip, from_a, from_b, adj, eddy, diag, msg):
    info = place()
    from_low, from_high = two_sides(info[0] % 2 == 0, from_a, from_b)
    edges = Edges(info, table)
    top = (info[2] % 2 == 0) != far

    def plane(z, p):
        own = adj[p, z] if p < FIELDS else eddy[z] if p == EDDY else relax_rate / diag[z] if p == RATE else strip[z]
        return jnp.concatenate([own, halo_tile(from_low, from_high, z, p)], 0)

    near = jnp.where(top, LEV - 1, 0)
    next_ = jnp.where(top, LEV - 2, 1)
    for p in range(9):
        msg[p] = plane(near, p)
    e = plane(next_, EDDY)
    for f in range(FIELDS):
        msg[9 + f] = edges.flux(plane(next_, f) * e)
    s = plane(next_, STRIP)
    msg[15] = edges.flux(s * lanes_of(s, EDDY))


def inner_levels(
    table, adj, eddy, diag, strip, from_a, from_b, metric, src,
    f0, near1, next2, f1, rates, edge_eddy, edge_rate, out, sums, halo, metric_row, a1, a2, ends, lateral,
):
    info = place()
    from_low, from_high = two_sides(info[0] % 2 == 0, from_a, from_b)
    edges = Edges(info, table)
    row = iota((8, COLS), 0)
    for z in range(LEV):
        for p in range(9):
            halo[z, p] = halo_tile(from_low, from_high, z, p)
        for f in range(FIELDS):
            above = jnp.broadcast_to(from_high[z, HIGH_METRIC + f : HIGH_METRIC + f + 1, :], (8, COLS))
            below = jnp.broadcast_to(from_low[z, LOW_METRIC + f : LOW_METRIC + f + 1, :], (8, COLS))
            metric_row[f, z] = jnp.where(row < 4, above, below)
    hub = info[5] * LEV // 4 - info[2] * LEV
    flag = jnp.where(hub == 0, 1.0, 0.0).astype(jnp.float32)

    def value(z, p):
        own = adj[p, z] if p < FIELDS else strip[z]
        return jnp.concatenate([own, halo[z, STRIP if p == FIELDS else p]], 0)

    def eddies(z):
        return jnp.concatenate([eddy[z], halo[z, EDDY]], 0)

    for z in range(LEV):
        rates[z] = jnp.concatenate([relax_rate / diag[z], halo[z, RATE]], 0)
        s = value(z, FIELDS)
        edge_eddy[z] = lanes_of(s, EDDY)
        edge_rate[z] = lanes_of(s, RATE)
    for z in range(LEV):
        e = eddies(z)
        for f in range(FIELDS):
            f0[z, f] = edges.flux(value(z, f) * e)
        f0[z, FIELDS] = edges.flux(value(z, FIELDS) * edge_eddy[z])

    def strips_of(array, zs):
        return [(z, lambda z=z: array[z, FIELDS]) for z in zs]

    def level(z, flux, value, vertical, store, **more):
        return Level(
            lambda p: flux[z, p],
            vertical,
            lambda p: value(z, p),
            lambda: rates[z],
            lambda: edge_rate[z],
            lambda: ends[z],
            lambda: lateral[z],
            store,
            **more,
        )

    def store_first(z):
        def store(p, v):
            if z in (0, LEV - 1):
                near1[z // (LEV - 1), p] = v
            else:
                a1[z, p] = v
                f1[z, p] = edges.flux(v * (edge_eddy[z] if p == FIELDS else eddies(z)))

        return store

    def store_second(z):
        def store(p, v):
            if z in (1, LEV - 2):
                next2[z // (LEV - 2), p] = v
            else:
                a2[z, p] = v

        return store

    def around(array, z, low, high):
        if z == low:
            return lambda p: array[z + 1, p]
        if z == high:
            return lambda p: array[z - 1, p]
        return lambda p: array[z - 1, p] + array[z + 1, p]

    prepare(edges, strips_of(f0, range(LEV)), ends, lateral)
    sweep(
        [
            level(z, f0, value, around(f0, z, 0, LEV - 1), store_first(z), **({"src": src, "flag": flag} if z == 0 else {}))
            for z in range(LEV)
        ],
        table,
    )
    inside = range(1, LEV - 1)
    prepare(edges, strips_of(f1, inside), ends, lateral)
    sweep([level(z, f1, lambda z, p: a1[z, p], around(f1, z, 1, LEV - 2), store_second(z)) for z in inside], table)
    sums[...] = jnp.zeros_like(sums)
    for z in range(2, LEV - 2):
        level_sums(z, info, lambda f: a2[z, f], a2[z, FIELDS], strip, metric, metric_row, sums, out, z - 2)


def outer_levels(
    table, eddy, strip, from_b, from_a, metric, src,
    f0, near1, next2, f1, rates, edge_eddy, edge_rate, inner_out, inner_sums, halo_rows, metric_row,
    out, share, sums, fh, gh, an, gn, a2, edge_over, ends, lateral,
):
    info = place()
    edges = Edges(info, table)
    hub = info[5] * LEV // 4 - info[2] * LEV
    sums[...] = inner_sums[...]
    for f in range(FIELDS):
        for z in range(2, LEV - 2):
            out[f, z] = inner_out[f, z - 2]
    even = info[2] % 2 == 0

    def flag_of(z):
        return jnp.where(z == hub, 1.0, 0.0).astype(jnp.float32)

    def side(n, msg):
        top = even if n == 0 else jnp.logical_not(even)
        near, next_ = jnp.where(top, LEV - 1, 0), jnp.where(top, LEV - 2, 1)
        ghost = jnp.where(top, edges.high_z, edges.low_z)
        factor = jnp.where(top, edges.factors[5], edges.factors[4])
        return n, msg, jnp.where(top, 1, 0), near, next_, jnp.where(top, LEV, -1), ghost, factor

    sides = [side(0, from_a), side(1, from_b)]
    for n, msg, *_ in sides:
        edge_over[n, 0] = lanes_of(msg[STRIP], EDDY)
        edge_over[n, 1] = lanes_of(msg[STRIP], RATE)
    for n, msg, i, near, next_, over, ghost, factor in sides:
        eddy_near = jnp.concatenate([eddy[near], halo_rows[near, EDDY]], 0)
        for p in (FIELDS, *range(FIELDS)):
            v = msg[STRIP] * edge_over[n, 0] if p == FIELDS else msg[p] * msg[EDDY]
            v = jnp.where(ghost, factor * f0[near, p], edges.flux(v))
            fh[n, p] = v
            r, e = (edge_rate[near], edge_eddy[near]) if p == FIELDS else (rates[near], eddy_near)
            v = near1[i, p] + r * v
            an[n, p] = v
            gn[n, p] = edges.flux(v * e)
    prepare(edges, [(n, lambda n=n: fh[n, FIELDS]) for n in range(2)], ends, lateral)
    prepare(edges, [(2 + n, lambda n=n: gn[n, FIELDS]) for n in range(2)], ends, lateral)

    def over_level(n, msg, i, near, next_, over, ghost, factor):
        def store(p, v):
            v = edges.flux(v * (edge_over[n, 0] if p == FIELDS else msg[EDDY]))
            gh[n, p] = jnp.where(ghost, factor * gn[n, p], v)

        return Level(
            lambda p: fh[n, p],
            lambda p: msg[9 + p] + f0[near, p],
            lambda p: msg[STRIP if p == FIELDS else p],
            lambda: msg[RATE],
            lambda: edge_over[n, 1],
            lambda: ends[n],
            lambda: lateral[n],
            store,
            src,
            flag_of(over),
        )

    def near_level(n, msg, i, near, next_, over, ghost, factor):
        def store(p, v):
            a2[n, p] = v

        return Level(
            lambda p: gn[n, p],
            lambda p: gh[n, p] + f1[next_, p],
            lambda p: an[n, p],
            lambda: rates[near],
            lambda: edge_rate[near],
            lambda: ends[2 + n],
            lambda: lateral[2 + n],
            store,
            src,
            flag_of(near),
        )

    sweep([over_level(*s) for s in sides], table)
    for n, msg, i, near, next_, over, ghost, factor in sides:

        def after(p):
            return next2[i, p] + (edge_rate[next_] if p == FIELDS else rates[next_]) * gn[n, p]

        level_sums(next_, info, after, after(FIELDS), strip, metric, metric_row, sums, out, next_)
    sweep([near_level(*s) for s in sides], table)
    for n, msg, i, near, *_ in sides:
        level_sums(near, info, lambda f: a2[n, f], a2[n, FIELDS], strip, metric, metric_row, sums, out, near)

    s1 = sums[1]
    stream = roll(s1, -1, 0)[:ROWS] - roll(s1, 1, 0)[:ROWS]
    t = sums[3, :ROWS]
    s2 = sums[2, :ROWS]
    lane = iota((ROWS, COLS), 1)
    right, left = roll(s2, -1, 1), roll(s2, 1, 1)
    high = [roll(t, COLS - 1 - (SLOT * f + 12), 1) for f in range(FIELDS)]
    low = [roll(t, -(SLOT * f + 3), 1) for f in range(FIELDS)]
    right = jnp.where(lane == COLS - 1, (high[0] + high[1] + high[2]) + (high[3] + high[4] + high[5]), right)
    left = jnp.where(lane == 0, (low[0] + low[1] + low[2]) + (low[3] + low[4] + low[5]), left)
    total = sums[0, :ROWS] - 0.5 * stream - 0.5 * (right - left)
    turned = jnp.concatenate([total, jnp.zeros((COLS - ROWS, COLS), jnp.float32)], 0).T
    for k in range(share.shape[0]):
        share[k] = turned[share.shape[1] * k : share.shape[1] * (k + 1)]


def add_shares(parts, out):
    total = parts[0]
    for i in range(1, parts.shape[0]):
        total = total + parts[i]
    out[...] = total[:, :ROWS]


def call(body, outs, ins, scratch=()):
    return pl.pallas_call(
        body,
        out_shape=outs,
        in_specs=ins,
        out_specs=jax.tree.map(lambda _: VM, outs),
        scratch_shapes=list(scratch),
        compiler_params=pltpu.CompilerParams(vmem_limit_bytes=16 << 20),
        cost_estimate=pl.CostEstimate(flops=1000000, bytes_accessed=1 << 20, transcendentals=0),
    )


def local(adjoint_start, eddy_visc, diag_coef, coupling, metric_terms, sample_cells, sample_weights, face_codes):
    slices = lax.axis_size("gz")
    cells, weights = sample_cells.reshape(16, 128), sample_weights.reshape(16, 128)

    def trade(v, axis, first):
        n = lax.axis_size(axis)
        pairs = [(i, i + 1) for i in range(first, n - 1, 2)]
        return lax.ppermute(v, axis, pairs + [(b, a) for a, b in pairs])

    def buf(*shape):
        return pltpu.VMEM(shape, jnp.float32)

    level = (LEV, ROWS, COLS)
    own, msg_a, msg_b = call(
        pack_y,
        (f32(*level), f32(2, ROWS, COLS), f32(2, ROWS, COLS)),
        [VM] * 4,
        [buf(*level)],
    )(adjoint_start, eddy_visc, diag_coef, metric_terms[2:3])
    beside = trade(msg_a, "gy", 0), trade(msg_b, "gy", 1)
    strip, msg_a, msg_b = call(pack_x, (f32(*level),) * 3, [VM] * 7, [buf(*level)] * 2)(
        own, *beside, adjoint_start, eddy_visc, diag_coef, metric_terms
    )
    beside = trade(msg_a, "gx", 0), trade(msg_b, "gx", 1)
    src, table = call(
        make_source, (f32(2, EXT, COLS), f32(56, COLS)), [SM] * 2 + [VM] * 3
    )(face_codes, coupling, cells, weights, strip)
    received = (*beside, adjoint_start, eddy_visc, diag_coef)
    msg_b, msg_a = [
        call(functools.partial(pack_z, far), f32(16, EXT, COLS), [VM] * 7)(table, strip, *received)
        for far in (True, False)
    ]
    from_b = trade(msg_b, "gz", 1)
    from_a = trade(msg_a, "gz", 0)
    ext = (EXT, COLS)
    inner = call(
        inner_levels,
        (
            f32(LEV, 7, *ext),
            f32(2, 7, *ext),
            f32(2, 7, *ext),
            f32(LEV, 7, *ext),
            f32(LEV, *ext),
            f32(LEV, *ext),
            f32(LEV, *ext),
            f32(FIELDS, LEV - 4, ROWS, COLS),
            f32(4, *ext),
            f32(LEV, 9, 8, COLS),
            f32(FIELDS, LEV, 8, COLS),
        ),
        [VM] * 9,
        [buf(LEV, 7, *ext), buf(LEV, 7, *ext), buf(LEV, *ext), buf(LEV, *ext)],
    )(table, adjoint_start, eddy_visc, diag_coef, strip, *beside, metric_terms, src)
    adjoint, share = call(
        outer_levels,
        (f32(FIELDS, *level), f32(slices, COLS // slices, COLS)),
        [VM] * 18,
        [buf(4, *ext)] + [buf(2, 7, *ext)] * 5 + [buf(2, 2, *ext), buf(4, *ext), buf(4, *ext)],
    )(table, eddy_visc, strip, from_b, from_a, metric_terms, src, *inner)
    parts = lax.all_to_all(share, "gz", 0, 0, tiled=True)
    height_grad = call(add_shares, f32(COLS // slices, ROWS), [VM])(parts).T
    return (adjoint, height_grad)


def solution(mesh):
    return jax.shard_map(
        local,
        mesh=mesh,
        in_specs=(
            P(None, "gz", "gx", "gy"),
            P("gz", "gx", "gy"),
            P("gz", "gx", "gy"),
            P(),
            P(None, None, "gz", "gx", "gy"),
            P(),
            P(),
            P(),
        ),
        out_specs=(P(None, "gz", "gx", "gy"), P("gx", ("gy", "gz"))),
        check_vma=False,
    )
```

```python
import functools

import jax
import jax.numpy as jnp
from jax import lax
from jax.experimental import pallas as pl
from jax.experimental.pallas import tpu as pltpu
from jax.sharding import PartitionSpec as P

relax_rate = 0.9
keep_rate = 0.1

FIELDS = 6
LEV = 8
ROWS = 32
COLS = 128
EXT = 40
EDDY, RATE, STRIP = 6, 7, 8
SLOT = 16

VM = pl.BlockSpec(memory_space=pltpu.VMEM)
SM = pl.BlockSpec(memory_space=pltpu.SMEM)


def roll(v, shift, axis):
    return pltpu.roll(v, shift % v.shape[axis], axis)


def iota(shape, axis):
    return lax.broadcasted_iota(jnp.int32, shape, axis)


def f32(*shape):
    return jax.ShapeDtypeStruct(shape, jnp.float32)


def pipeline(tasks):
    held = None
    for begin, end in tasks:
        started = begin()
        if held is not None:
            held[0](held[1])
        held = (end, started)
    held[0](held[1])


def place():
    return [lax.axis_index(a) for a in ("gx", "gy", "gz")] + [lax.axis_size(a) for a in ("gx", "gy", "gz")]


class Either:
    def __init__(self, condition, first, second):
        self.condition, self.first, self.second = condition, first, second

    def __getitem__(self, at):
        return jnp.where(self.condition, self.first[at], self.second[at])


def two_sides(even, from_a, from_b):
    return Either(even, from_b, from_a), Either(even, from_a, from_b)


def pack_y(adj, eddy, diag, metric, own, msg_a, msg_b, packed):
    even = place()[1] % 2 == 0
    shape = (4, 8, COLS)
    lane = iota(shape, 2)
    slot, j = lane // SLOT, lane % SLOT
    quad, jj = j // 4, j % 4

    def block(zg, t):
        return pl.ds(4 * zg, 4), pl.ds(8 * t, 8)

    def gather(zg, t):
        zs, rows = block(zg, t)

        def planes(p):
            if p >= 8:
                return roll(metric[0, p - 8, zs, rows, :], SLOT * (p - 8) + 9, 2)
            v = adj[p, zs, rows, :] if p < FIELDS else eddy[zs, rows, :] if p == EDDY else relax_rate / diag[zs, rows, :]
            return roll(v, SLOT * p + 4, 2)

        def choose(p, v, c):
            if p >= 8:
                return jnp.where((slot == p - 8) & (j >= 8) & (j <= 9), v, c)
            return jnp.where((slot == p) & (j >= 1) & (j <= 6), v, c)

        c = jnp.zeros(shape, jnp.float32)
        ahead = [planes(0), planes(1), planes(2)]
        for p in range(14):
            if p + 3 < 14:
                ahead.append(planes(p + 3))
            c = choose(p, ahead[p], c)
        packed[zs, rows, :] = c

    def send(zg, t):
        zs, rows = block(zg, t)
        c = packed[zs, rows, :]
        c8 = roll(c, 8, 2)
        right = left = jnp.zeros((8, COLS), jnp.float32)
        moved = []
        for zq in range(4):
            at = 4 * zq
            moved.append([roll(c[zq], at + by, 1) for by in (-8, 0, -6, -4)])
        own[zs, rows, :] = jnp.where(j < 8, c, jnp.where(j >= 9, c8, 0.0))
        for zq in range(4):
            r0, r1, l0, l1 = moved[zq]
            here = quad[0] == zq
            right = jnp.where(here, jnp.where(jj[0] == 0, r0, r1), right)
            left = jnp.where(here, jnp.where(jj[0] == 3, l0, l1), left)
        msg_a[zg, rows, :] = jnp.where(even, right, left)
        msg_b[zg, rows, :] = jnp.where(even, left, right)

    blocks = [(zg, t) for zg in range(2) for t in range(ROWS // 8)]
    for zg, t in blocks:
        gather(zg, t)
    for zg, t in blocks:
        send(zg, t)


MIX, PAIR = 8, 16


def make_source(codes, coup, cells, weights, after, src, table):
    slot = iota((1, COLS), 1) // SLOT
    for i in range(6):
        factor = jnp.where(codes[i] == 1, 1.0, jnp.where(codes[i] == 2, -1.0, 0.0)).astype(jnp.float32)
        table[i : i + 1, :] = jnp.full((1, COLS), factor)
    for e in range(FIELDS):
        v = jnp.zeros((1, COLS), jnp.float32)
        for f in range(FIELDS):
            v = jnp.where(slot == f, coup[e, f], v)
            at = PAIR + FIELDS * e + f
            table[at : at + 1, :] = jnp.full((1, COLS), coup[e, f])
        table[MIX + e : MIX + e + 1, :] = v
    info = place()
    start_x, start_y, total_y = info[0] * ROWS, info[1] * COLS, info[4] * COLS
    r = iota((48, COLS), 0)
    row_x = jnp.where(r < EXT - 5, r, r - EXT) + start_x
    row_x = jnp.where(r < EXT, row_x, -1)
    l = iota((2 * COLS, COLS), 0)
    j = l - COLS
    col_y = jnp.where((j >= 1) & (j <= 6), j - 4, j + (COLS - 12))
    col_y = jnp.where(l < COLS, l, col_y) + start_y
    col_y = jnp.where((l < COLS) | ((j >= 1) & (j <= 6)) | ((j >= 9) & (j <= 14)), col_y, -1)
    acc = jnp.zeros((144, 2 * COLS), jnp.float32)
    for k in range(0, 16, 2):
        left, one = [], []
        for q in (k, k + 1):
            c = cells[q : q + 1, :]
            w = weights[q : q + 1, :]
            x = ((c.astype(jnp.float32) + 0.5) * (1.0 / total_y)).astype(jnp.int32)
            y = c - x * total_y
            high = w.astype(jnp.bfloat16).astype(jnp.float32)
            mid = (w - high).astype(jnp.bfloat16).astype(jnp.float32)
            low = w - high - mid
            hit = row_x == x
            left.append(jnp.concatenate([jnp.where(hit, v, 0.0).astype(jnp.bfloat16) for v in (low, mid, high)], 0))
            one.append(jnp.where(col_y == y, 1.0, 0.0).astype(jnp.bfloat16))
        acc = acc + lax.dot_general(
            jnp.concatenate(left, 1),
            jnp.concatenate(one, 1),
            (((1,), (1,)), ((), ())),
            preferred_element_type=jnp.float32,
        )
    total = acc[0:EXT, :] + acc[48 : 48 + EXT, :] + acc[96 : 96 + EXT, :]
    src[0] = total[:, :COLS]
    src[1] = total[:, COLS:]


HIGH_AT = [0, 3, 6, 9, 12, 15, 18, 21, 23]
LOW_AT = [6 + a for a in HIGH_AT]
HIGH_METRIC, LOW_METRIC = 26, 0


def pack_x(own, from_b, from_a, adj, eddy, diag, metric, strip, msg_a, msg_b, to_low, to_high):
    info = place()
    from_left, from_right = two_sides(info[1] % 2 == 0, from_a, from_b)
    even = info[0] % 2 == 0
    j = iota((ROWS, COLS), 1) % SLOT
    for z in range(LEV):
        zg, at = z // 4, 4 * (z % 4)
        low = roll(from_left[zg], -at, 1)
        high = roll(from_right[zg], 12 - at, 1)
        s = jnp.where(j < 4, low, jnp.where(j >= 12, high, own[z]))
        strip[z] = s
        sides = ((to_low, 0, 0, 0, HIGH_AT, HIGH_METRIC), (to_high, ROWS - 3, ROWS - 2, ROWS - 1, LOW_AT, LOW_METRIC))
        for msg, a, b, near, at, metric_at in sides:
            for p in range(FIELDS):
                msg[z, at[p] : at[p] + 3, :] = adj[p, z, a : a + 3, :]
                msg[z, metric_at + p : metric_at + p + 1, :] = metric[1, p, z, near : near + 1, :]
            msg[z, at[EDDY] : at[EDDY] + 3, :] = eddy[z, a : a + 3, :]
            msg[z, at[RATE] : at[RATE] + 2, :] = relax_rate / diag[z, b : b + 2, :]
            msg[z, at[STRIP] : at[STRIP] + 3, :] = s[a : a + 3, :]
    for z in range(LEV):
        low, high = to_low[z], to_high[z]
        msg_a[z] = jnp.where(even, high, low)
        msg_b[z] = jnp.where(even, low, high)


def lanes_of(v, plane):
    return jnp.take_along_axis(v, iota(v.shape, 1) % SLOT + SLOT * plane, axis=1)


class Edges:
    def __init__(self, info, table):
        self.low_x, self.high_x = info[0] == 0, info[0] == info[3] - 1
        self.low_y, self.high_y = info[1] == 0, info[1] == info[4] - 1
        self.low_z, self.high_z = info[2] == 0, info[2] == info[5] - 1
        self.factors = [table[i : i + 1, :] for i in range(6)]
        row, j = iota((8, COLS), 0), iota((EXT, COLS), 1) % SLOT
        self.row_low, self.row_high = (row == 7) & self.low_x, (row == 0) & self.high_x
        self.j = j
        self.ghost_low, self.ghost_high = (j == 3) & self.low_y, (j == 12) & self.high_y
        self.own_low, self.own_high = (j == 4) & self.low_y, (j == 11) & self.high_y

    def flux(self, v):
        t4 = v[32:40]
        t4 = jnp.where(self.row_low, self.factors[0] * roll(v[0:8], 7, 0), t4)
        t4 = jnp.where(self.row_high, self.factors[1] * roll(v[24:32], 1, 0), t4)
        return jnp.concatenate([v[0:32], t4], 0)


class Level:
    def __init__(self, center, vertical, value, rate, edge_rate, ends, lateral, store, src=None, flag=None):
        self.center, self.vertical, self.value = center, vertical, value
        self.rate, self.edge_rate, self.ends, self.lateral = rate, edge_rate, ends, lateral
        self.store, self.src, self.flag = store, src, flag


def prepare(edges, strips, ends, lateral):
    f2, f3 = edges.factors[2], edges.factors[3]

    def task(at, strip):
        def end(moved):
            v, up, down = moved
            ends[at] = jnp.where(edges.ghost_low, f2 * down, jnp.where(edges.ghost_high, f3 * up, v))
            lateral[at] = jnp.where(edges.own_low, f2 * v, up) + jnp.where(edges.own_high, f3 * v, down)

        def begin():
            v = strip()
            return v, roll(v, 1, 1), roll(v, -1, 1)

        return begin, end

    def turn(at, _):
        def begin():
            v = ends[at]
            return v, roll(v, -10, 1)

        def end(moved):
            ends[at] = jnp.where(edges.j == 3, *moved)

        return begin, end

    pipeline([task(*s) for s in strips])
    pipeline([turn(*s) for s in strips])


def sweep(levels, table):
    lane = iota((EXT, COLS), 1)
    half = FIELDS // 2

    def pair(e, f):
        at = PAIR + FIELDS * e + f
        return table[at : at + 1, :]

    def field(level, f):
        def begin():
            v = level.center(f)
            return v, roll(level.ends(), -(SLOT * f + 3), 1), roll(v, 1, 1), roll(v, -1, 1)

        def end(moved):
            v, edge, left, right = moved
            left = jnp.where(lane == 0, edge, left)
            right = jnp.where(lane == COLS - 1, edge, right)
            beside = level.vertical(f) + roll(v, -1, 0) + roll(v, 1, 0) + right + left
            coupled = pair(0, f) * level.value(0)
            for e in range(1, FIELDS):
                coupled = coupled + pair(e, f) * level.value(e)
            rest = beside - coupled
            if f == 0 and level.src is not None:
                rest = rest + level.flag * level.src[0]
            level.store(f, keep_rate * level.value(f) + level.rate() * rest)

        return begin, end

    def strip(level):
        sums = []

        def mixed(first):
            def begin():
                a = level.value(FIELDS)
                return [lanes_of(a, e) for e in range(first, first + half)]

            def end(moved):
                terms = [v * table[MIX + first + i : MIX + first + i + 1, :] for i, v in enumerate(moved)]
                sums.append(terms[0] + terms[1] + terms[2])

            return begin, end

        def end(_):
            v = level.center(FIELDS)
            rest = level.vertical(FIELDS) + roll(v, -1, 0) + roll(v, 1, 0) + level.lateral() - (sums[0] + sums[1])
            if level.src is not None:
                rest = rest + level.flag * level.src[1]
            level.store(FIELDS, keep_rate * level.value(FIELDS) + level.edge_rate() * rest)

        return [mixed(0), mixed(half), (lambda: None, end)]

    pipeline([task for level in levels for task in strip(level) + [field(level, f) for f in range(FIELDS)]])


def level_sums(z, info, field, edge_strip, strip, metric, metric_row, sums, out, zo):
    total_z = info[5] * LEV
    w = 1.0 - 0.5 * ((jnp.int32(info[2] * LEV + z).astype(jnp.float32) + 0.5) / total_z)
    totals = None
    for f in range(FIELDS):
        a = field(f)
        own = a[:ROWS]
        out[f, zo] = own
        terms = [metric[k, f, z] * own for k in range(3)] + [metric_row[f, z] * a[ROWS:]]
        totals = terms if f == 0 else [s + t for s, t in zip(totals, terms)]
    s = strip[z, :ROWS]
    j = iota((ROWS, COLS), 1) % SLOT
    m = jnp.where(j == 3, roll(s, 3, 1), jnp.where(j == 12, roll(s, -3, 1), 0.0))
    sums[0, :ROWS] += w * totals[0]
    sums[1, :ROWS] += w * totals[1]
    sums[1, ROWS:] += w * totals[3]
    sums[2, :ROWS] += w * totals[2]
    sums[3, :ROWS] += w * (m * edge_strip[:ROWS])


def halo_tile(from_low, from_high, z, p):
    at = 2 if p == RATE else 3
    start = LOW_AT[p] - (8 - at)
    above, below = from_high[z, pl.ds(HIGH_AT[p], 8), :], from_low[z, pl.ds(start, 8), :]
    return jnp.where(iota((8, COLS), 0) < 4, above, below)


def pack_z(far, table, strip, from_b, from_a, adj, eddy, diag, msg):
    info = place()
    from_low, from_high = two_sides(info[0] % 2 == 0, from_a, from_b)
    edges = Edges(info, table)
    top = (info[2] % 2 == 0) != far

    def plane(z, p):
        own = adj[p, z] if p < FIELDS else eddy[z] if p == EDDY else relax_rate / diag[z] if p == RATE else strip[z]
        return jnp.concatenate([own, halo_tile(from_low, from_high, z, p)], 0)

    near = jnp.where(top, LEV - 1, 0)
    next_ = jnp.where(top, LEV - 2, 1)
    for p in range(9):
        msg[p] = plane(near, p)
    e = plane(next_, EDDY)
    for f in range(FIELDS):
        msg[9 + f] = edges.flux(plane(next_, f) * e)
    s = plane(next_, STRIP)
    msg[15] = edges.flux(s * lanes_of(s, EDDY))


def inner_levels(
    table, adj, eddy, diag, strip, from_b, from_a, metric, src,
    f0, near1, next2, f1, rates, edge_eddy, edge_rate, out, sums, halo, metric_row, a1, a2, ends, lateral,
):
    info = place()
    from_low, from_high = two_sides(info[0] % 2 == 0, from_a, from_b)
    edges = Edges(info, table)
    row = iota((8, COLS), 0)
    for z in range(LEV):
        for p in range(9):
            halo[z, p] = halo_tile(from_low, from_high, z, p)
        for f in range(FIELDS):
            above = jnp.broadcast_to(from_high[z, HIGH_METRIC + f : HIGH_METRIC + f + 1, :], (8, COLS))
            below = jnp.broadcast_to(from_low[z, LOW_METRIC + f : LOW_METRIC + f + 1, :], (8, COLS))
            metric_row[f, z] = jnp.where(row < 4, above, below)
    hub = info[5] * LEV // 4 - info[2] * LEV
    flag = jnp.where(hub == 0, 1.0, 0.0).astype(jnp.float32)

    def value(z, p):
        own = adj[p, z] if p < FIELDS else strip[z]
        return jnp.concatenate([own, halo[z, STRIP if p == FIELDS else p]], 0)

    def eddies(z):
        return jnp.concatenate([eddy[z], halo[z, EDDY]], 0)

    for z in range(LEV):
        rates[z] = jnp.concatenate([relax_rate / diag[z], halo[z, RATE]], 0)
        s = value(z, FIELDS)
        edge_eddy[z] = lanes_of(s, EDDY)
        edge_rate[z] = lanes_of(s, RATE)
    for z in range(LEV):
        e = eddies(z)
        for f in range(FIELDS):
            f0[z, f] = edges.flux(value(z, f) * e)
        f0[z, FIELDS] = edges.flux(value(z, FIELDS) * edge_eddy[z])

    def strips_of(array, zs):
        return [(z, lambda z=z: array[z, FIELDS]) for z in zs]

    def level(z, flux, value, vertical, store, **more):
        return Level(
            lambda p: flux[z, p],
            vertical,
            lambda p: value(z, p),
            lambda: rates[z],
            lambda: edge_rate[z],
            lambda: ends[z],
            lambda: lateral[z],
            store,
            **more,
        )

    def store_first(z):
        def store(p, v):
            if z in (0, LEV - 1):
                near1[z // (LEV - 1), p] = v
            else:
                a1[z, p] = v
                f1[z, p] = edges.flux(v * (edge_eddy[z] if p == FIELDS else eddies(z)))

        return store

    def store_second(z):
        def store(p, v):
            if z in (1, LEV - 2):
                next2[z // (LEV - 2), p] = v
            else:
                a2[z, p] = v

        return store

    def around(array, z, low, high):
        if z == low:
            return lambda p: array[z + 1, p]
        if z == high:
            return lambda p: array[z - 1, p]
        return lambda p: array[z - 1, p] + array[z + 1, p]

    prepare(edges, strips_of(f0, range(LEV)), ends, lateral)
    sweep(
        [
            level(z, f0, value, around(f0, z, 0, LEV - 1), store_first(z), **({"src": src, "flag": flag} if z == 0 else {}))
            for z in range(LEV)
        ],
        table,
    )
    inside = range(1, LEV - 1)
    prepare(edges, strips_of(f1, inside), ends, lateral)
    sweep([level(z, f1, lambda z, p: a1[z, p], around(f1, z, 1, LEV - 2), store_second(z)) for z in inside], table)
    sums[...] = jnp.zeros_like(sums)
    for z in range(2, LEV - 2):
        level_sums(z, info, lambda f: a2[z, f], a2[z, FIELDS], strip, metric, metric_row, sums, out, z - 2)


def outer_levels(
    table, eddy, strip, from_b, from_a, metric, src,
    f0, near1, next2, f1, rates, edge_eddy, edge_rate, inner_out, inner_sums, halo_rows, metric_row,
    out, share, sums, fh, gh, an, gn, a2, edge_over, ends, lateral,
):
    info = place()
    edges = Edges(info, table)
    hub = info[5] * LEV // 4 - info[2] * LEV
    sums[...] = inner_sums[...]
    for f in range(FIELDS):
        for z in range(2, LEV - 2):
            out[f, z] = inner_out[f, z - 2]
    even = info[2] % 2 == 0

    def flag_of(z):
        return jnp.where(z == hub, 1.0, 0.0).astype(jnp.float32)

    def side(n, msg):
        top = even if n == 0 else jnp.logical_not(even)
        near, next_ = jnp.where(top, LEV - 1, 0), jnp.where(top, LEV - 2, 1)
        ghost = jnp.where(top, edges.high_z, edges.low_z)
        factor = jnp.where(top, edges.factors[5], edges.factors[4])
        return n, msg, jnp.where(top, 1, 0), near, next_, jnp.where(top, LEV, -1), ghost, factor

    sides = [side(0, from_a), side(1, from_b)]
    for n, msg, *_ in sides:
        edge_over[n, 0] = lanes_of(msg[STRIP], EDDY)
        edge_over[n, 1] = lanes_of(msg[STRIP], RATE)
    for n, msg, i, near, next_, over, ghost, factor in sides:
        eddy_near = jnp.concatenate([eddy[near], halo_rows[near, EDDY]], 0)
        for p in (FIELDS, *range(FIELDS)):
            v = msg[STRIP] * edge_over[n, 0] if p == FIELDS else msg[p] * msg[EDDY]
            v = jnp.where(ghost, factor * f0[near, p], edges.flux(v))
            fh[n, p] = v
            r, e = (edge_rate[near], edge_eddy[near]) if p == FIELDS else (rates[near], eddy_near)
            v = near1[i, p] + r * v
            an[n, p] = v
            gn[n, p] = edges.flux(v * e)
    prepare(edges, [(n, lambda n=n: fh[n, FIELDS]) for n in range(2)], ends, lateral)
    prepare(edges, [(2 + n, lambda n=n: gn[n, FIELDS]) for n in range(2)], ends, lateral)

    def over_level(n, msg, i, near, next_, over, ghost, factor):
        def store(p, v):
            v = edges.flux(v * (edge_over[n, 0] if p == FIELDS else msg[EDDY]))
            gh[n, p] = jnp.where(ghost, factor * gn[n, p], v)

        return Level(
            lambda p: fh[n, p],
            lambda p: msg[9 + p] + f0[near, p],
            lambda p: msg[STRIP if p == FIELDS else p],
            lambda: msg[RATE],
            lambda: edge_over[n, 1],
            lambda: ends[n],
            lambda: lateral[n],
            store,
            src,
            flag_of(over),
        )

    def near_level(n, msg, i, near, next_, over, ghost, factor):
        def store(p, v):
            a2[n, p] = v

        return Level(
            lambda p: gn[n, p],
            lambda p: gh[n, p] + f1[next_, p],
            lambda p: an[n, p],
            lambda: rates[near],
            lambda: edge_rate[near],
            lambda: ends[2 + n],
            lambda: lateral[2 + n],
            store,
            src,
            flag_of(near),
        )

    sweep([over_level(*s) for s in sides], table)
    for n, msg, i, near, next_, over, ghost, factor in sides:

        def after(p):
            return next2[i, p] + (edge_rate[next_] if p == FIELDS else rates[next_]) * gn[n, p]

        level_sums(next_, info, after, after(FIELDS), strip, metric, metric_row, sums, out, next_)
    sweep([near_level(*s) for s in sides], table)
    for n, msg, i, near, *_ in sides:
        level_sums(near, info, lambda f: a2[n, f], a2[n, FIELDS], strip, metric, metric_row, sums, out, near)

    s1 = sums[1]
    stream = roll(s1, -1, 0)[:ROWS] - roll(s1, 1, 0)[:ROWS]
    t = sums[3, :ROWS]
    s2 = sums[2, :ROWS]
    lane = iota((ROWS, COLS), 1)
    right, left = roll(s2, -1, 1), roll(s2, 1, 1)
    high = [roll(t, COLS - 1 - (SLOT * f + 12), 1) for f in range(FIELDS)]
    low = [roll(t, -(SLOT * f + 3), 1) for f in range(FIELDS)]
    right = jnp.where(lane == COLS - 1, (high[0] + high[1] + high[2]) + (high[3] + high[4] + high[5]), right)
    left = jnp.where(lane == 0, (low[0] + low[1] + low[2]) + (low[3] + low[4] + low[5]), left)
    total = sums[0, :ROWS] - 0.5 * stream - 0.5 * (right - left)
    turned = jnp.concatenate([total, jnp.zeros((COLS - ROWS, COLS), jnp.float32)], 0).T
    for k in range(share.shape[0]):
        share[k] = turned[share.shape[1] * k : share.shape[1] * (k + 1)]


def add_shares(parts, out):
    total = parts[0]
    for i in range(1, parts.shape[0]):
        total = total + parts[i]
    out[...] = total[:, :ROWS]


def call(body, outs, ins, scratch=()):
    return pl.pallas_call(
        body,
        out_shape=outs,
        in_specs=ins,
        out_specs=jax.tree.map(lambda _: VM, outs),
        scratch_shapes=list(scratch),
        compiler_params=pltpu.CompilerParams(vmem_limit_bytes=16 << 20),
        cost_estimate=pl.CostEstimate(flops=1000000, bytes_accessed=1 << 20, transcendentals=0),
    )


def local(adjoint_start, eddy_visc, diag_coef, coupling, metric_terms, sample_cells, sample_weights, face_codes):
    slices = lax.axis_size("gz")
    cells, weights = sample_cells.reshape(16, 128), sample_weights.reshape(16, 128)

    def trade(v, axis, first):
        n = lax.axis_size(axis)
        pairs = [(i, i + 1) for i in range(first, n - 1, 2)]
        return lax.ppermute(v, axis, pairs + [(b, a) for a, b in pairs])

    def buf(*shape):
        return pltpu.VMEM(shape, jnp.float32)

    level = (LEV, ROWS, COLS)
    own, msg_a, msg_b = call(
        pack_y,
        (f32(*level), f32(2, ROWS, COLS), f32(2, ROWS, COLS)),
        [VM] * 4,
        [buf(*level)],
    )(adjoint_start, eddy_visc, diag_coef, metric_terms[2:3])
    beside = trade(msg_b, "gy", 1), trade(msg_a, "gy", 0)
    strip, msg_a, msg_b = call(pack_x, (f32(*level),) * 3, [VM] * 7, [buf(*level)] * 2)(
        own, *beside, adjoint_start, eddy_visc, diag_coef, metric_terms
    )
    beside = trade(msg_b, "gx", 1), trade(msg_a, "gx", 0)
    src, table = call(
        make_source, (f32(2, EXT, COLS), f32(56, COLS)), [SM] * 2 + [VM] * 3
    )(face_codes, coupling, cells, weights, strip)
    received = (*beside, adjoint_start, eddy_visc, diag_coef)
    msg_b, msg_a = [
        call(functools.partial(pack_z, far), f32(16, EXT, COLS), [VM] * 7)(table, strip, *received)
        for far in (True, False)
    ]
    from_b = trade(msg_b, "gz", 1)
    from_a = trade(msg_a, "gz", 0)
    ext = (EXT, COLS)
    inner = call(
        inner_levels,
        (
            f32(LEV, 7, *ext),
            f32(2, 7, *ext),
            f32(2, 7, *ext),
            f32(LEV, 7, *ext),
            f32(LEV, *ext),
            f32(LEV, *ext),
            f32(LEV, *ext),
            f32(FIELDS, LEV - 4, ROWS, COLS),
            f32(4, *ext),
            f32(LEV, 9, 8, COLS),
            f32(FIELDS, LEV, 8, COLS),
        ),
        [VM] * 9,
        [buf(LEV, 7, *ext), buf(LEV, 7, *ext), buf(LEV, *ext), buf(LEV, *ext)],
    )(table, adjoint_start, eddy_visc, diag_coef, strip, *beside, metric_terms, src)
    adjoint, share = call(
        outer_levels,
        (f32(FIELDS, *level), f32(slices, COLS // slices, COLS)),
        [VM] * 18,
        [buf(4, *ext)] + [buf(2, 7, *ext)] * 5 + [buf(2, 2, *ext), buf(4, *ext), buf(4, *ext)],
    )(table, eddy_visc, strip, from_b, from_a, metric_terms, src, *inner)
    parts = lax.all_to_all(share, "gz", 0, 0, tiled=True)
    height_grad = call(add_shares, f32(COLS // slices, ROWS), [VM])(parts).T
    return (adjoint, height_grad)


def solution(mesh):
    return jax.shard_map(
        local,
        mesh=mesh,
        in_specs=(
            P(None, "gz", "gx", "gy"),
            P("gz", "gx", "gy"),
            P("gz", "gx", "gy"),
            P(),
            P(None, None, "gz", "gx", "gy"),
            P(),
            P(),
            P(),
        ),
        out_specs=(P(None, "gz", "gx", "gy"), P("gx", ("gy", "gz"))),
        check_vma=False,
    )
```

```python
import functools

import jax
import jax.numpy as jnp
from jax import lax
from jax.experimental import pallas as pl
from jax.experimental.pallas import tpu as pltpu
from jax.sharding import PartitionSpec as P

relax_rate = 0.9
keep_rate = 0.1

FIELDS = 6
LEV = 8
ROWS = 32
COLS = 128
EXT = 40
EDDY, RATE, STRIP = 6, 7, 8
SLOT = 16

VM = pl.BlockSpec(memory_space=pltpu.VMEM)
SM = pl.BlockSpec(memory_space=pltpu.SMEM)


def roll(v, shift, axis):
    return pltpu.roll(v, shift % v.shape[axis], axis)


def iota(shape, axis):
    return lax.broadcasted_iota(jnp.int32, shape, axis)


def f32(*shape):
    return jax.ShapeDtypeStruct(shape, jnp.float32)


def pipeline(tasks):
    held = None
    for begin, end in tasks:
        started = begin()
        if held is not None:
            held[0](held[1])
        held = (end, started)
    held[0](held[1])


def place():
    return [lax.axis_index(a) for a in ("gx", "gy", "gz")] + [lax.axis_size(a) for a in ("gx", "gy", "gz")]


class Either:
    def __init__(self, condition, first, second):
        self.condition, self.first, self.second = condition, first, second

    def __getitem__(self, at):
        return jnp.where(self.condition, self.first[at], self.second[at])


def two_sides(even, from_a, from_b):
    return Either(even, from_b, from_a), Either(even, from_a, from_b)


def pack_y(adj, eddy, diag, metric, own, msg_a, msg_b, packed):
    even = place()[1] % 2 == 0
    shape = (4, 8, COLS)
    lane = iota(shape, 2)
    slot, j = lane // SLOT, lane % SLOT
    quad, jj = j // 4, j % 4

    def block(zg, t):
        return pl.ds(4 * zg, 4), pl.ds(8 * t, 8)

    def gather(zg, t):
        zs, rows = block(zg, t)

        def planes(p):
            if p >= 8:
                return roll(metric[0, p - 8, zs, rows, :], SLOT * (p - 8) + 9, 2)
            v = adj[p, zs, rows, :] if p < FIELDS else eddy[zs, rows, :] if p == EDDY else relax_rate / diag[zs, rows, :]
            return roll(v, SLOT * p + 4, 2)

        def choose(p, v, c):
            if p >= 8:
                return jnp.where((slot == p - 8) & (j >= 8) & (j <= 9), v, c)
            return jnp.where((slot == p) & (j >= 1) & (j <= 6), v, c)

        c = jnp.zeros(shape, jnp.float32)
        ahead = [planes(0), planes(1), planes(2)]
        for p in range(14):
            if p + 3 < 14:
                ahead.append(planes(p + 3))
            c = choose(p, ahead[p], c)
        packed[zs, rows, :] = c

    def send(zg, t):
        zs, rows = block(zg, t)
        c = packed[zs, rows, :]
        c8 = roll(c, 8, 2)
        right = left = jnp.zeros((8, COLS), jnp.float32)
        moved = []
        for zq in range(4):
            at = 4 * zq
            moved.append([roll(c[zq], at + by, 1) for by in (-8, 0, -6, -4)])
        own[zs, rows, :] = jnp.where(j < 8, c, jnp.where(j >= 9, c8, 0.0))
        for zq in range(4):
            r0, r1, l0, l1 = moved[zq]
            here = quad[0] == zq
            right = jnp.where(here, jnp.where(jj[0] == 0, r0, r1), right)
            left = jnp.where(here, jnp.where(jj[0] == 3, l0, l1), left)
        msg_a[zg, rows, :] = jnp.where(even, right, left)
        msg_b[zg, rows, :] = jnp.where(even, left, right)

    blocks = [(zg, t) for zg in range(2) for t in range(ROWS // 8)]
    for zg, t in blocks:
        gather(zg, t)
    for zg, t in blocks:
        send(zg, t)


MIX, PAIR = 8, 16


def make_source(codes, coup, cells, weights, after, src, table):
    slot = iota((1, COLS), 1) // SLOT
    for i in range(6):
        factor = jnp.where(codes[i] == 1, 1.0, jnp.where(codes[i] == 2, -1.0, 0.0)).astype(jnp.float32)
        table[i : i + 1, :] = jnp.full((1, COLS), factor)
    for e in range(FIELDS):
        v = jnp.zeros((1, COLS), jnp.float32)
        for f in range(FIELDS):
            v = jnp.where(slot == f, coup[e, f], v)
            at = PAIR + FIELDS * e + f
            table[at : at + 1, :] = jnp.full((1, COLS), coup[e, f])
        table[MIX + e : MIX + e + 1, :] = v
    info = place()
    start_x, start_y, total_y = info[0] * ROWS, info[1] * COLS, info[4] * COLS
    r = iota((48, COLS), 0)
    row_x = jnp.where(r < EXT - 5, r, r - EXT) + start_x
    row_x = jnp.where(r < EXT, row_x, -1)
    l = iota((2 * COLS, COLS), 0)
    j = l - COLS
    col_y = jnp.where((j >= 1) & (j <= 6), j - 4, j + (COLS - 12))
    col_y = jnp.where(l < COLS, l, col_y) + start_y
    col_y = jnp.where((l < COLS) | ((j >= 1) & (j <= 6)) | ((j >= 9) & (j <= 14)), col_y, -1)
    acc = jnp.zeros((144, 2 * COLS), jnp.float32)
    for k in range(0, 16, 2):
        left, one = [], []
        for q in (k, k + 1):
            c = cells[q : q + 1, :]
            w = weights[q : q + 1, :]
            x = ((c.astype(jnp.float32) + 0.5) * (1.0 / total_y)).astype(jnp.int32)
            y = c - x * total_y
            high = w.astype(jnp.bfloat16).astype(jnp.float32)
            mid = (w - high).astype(jnp.bfloat16).astype(jnp.float32)
            low = w - high - mid
            hit = row_x == x
            left.append(jnp.concatenate([jnp.where(hit, v, 0.0).astype(jnp.bfloat16) for v in (low, mid, high)], 0))
            one.append(jnp.where(col_y == y, 1.0, 0.0).astype(jnp.bfloat16))
        acc = acc + lax.dot_general(
            jnp.concatenate(left, 1),
            jnp.concatenate(one, 1),
            (((1,), (1,)), ((), ())),
            preferred_element_type=jnp.float32,
        )
    total = acc[0:EXT, :] + acc[48 : 48 + EXT, :] + acc[96 : 96 + EXT, :]
    src[0] = total[:, :COLS]
    src[1] = total[:, COLS:]


HIGH_AT = [0, 3, 6, 9, 12, 15, 18, 21, 23]
LOW_AT = [6 + a for a in HIGH_AT]
HIGH_METRIC, LOW_METRIC = 26, 0


def pack_x(own, from_b, from_a, adj, eddy, diag, metric, strip, msg_a, msg_b, to_low, to_high):
    info = place()
    from_left, from_right = two_sides(info[1] % 2 == 0, from_a, from_b)
    even = info[0] % 2 == 0
    j = iota((ROWS, COLS), 1) % SLOT
    for z in range(LEV):
        zg, at = z // 4, 4 * (z % 4)
        low = roll(from_left[zg], -at, 1)
        high = roll(from_right[zg], 12 - at, 1)
        s = jnp.where(j < 4, low, jnp.where(j >= 12, high, own[z]))
        strip[z] = s
        sides = ((to_low, 0, 0, 0, HIGH_AT, HIGH_METRIC), (to_high, ROWS - 3, ROWS - 2, ROWS - 1, LOW_AT, LOW_METRIC))
        for msg, a, b, near, at, metric_at in sides:
            for p in range(FIELDS):
                msg[z, at[p] : at[p] + 3, :] = adj[p, z, a : a + 3, :]
                msg[z, metric_at + p : metric_at + p + 1, :] = metric[1, p, z, near : near + 1, :]
            msg[z, at[EDDY] : at[EDDY] + 3, :] = eddy[z, a : a + 3, :]
            msg[z, at[RATE] : at[RATE] + 2, :] = relax_rate / diag[z, b : b + 2, :]
            msg[z, at[STRIP] : at[STRIP] + 3, :] = s[a : a + 3, :]
    for z in range(LEV):
        low, high = to_low[z], to_high[z]
        msg_a[z] = jnp.where(even, high, low)
        msg_b[z] = jnp.where(even, low, high)


def lanes_of(v, plane):
    return jnp.take_along_axis(v, iota(v.shape, 1) % SLOT + SLOT * plane, axis=1)


class Edges:
    def __init__(self, info, table):
        self.low_x, self.high_x = info[0] == 0, info[0] == info[3] - 1
        self.low_y, self.high_y = info[1] == 0, info[1] == info[4] - 1
        self.low_z, self.high_z = info[2] == 0, info[2] == info[5] - 1
        self.factors = [table[i : i + 1, :] for i in range(6)]
        row, j = iota((8, COLS), 0), iota((EXT, COLS), 1) % SLOT
        self.row_low, self.row_high = (row == 7) & self.low_x, (row == 0) & self.high_x
        self.j = j
        self.ghost_low, self.ghost_high = (j == 3) & self.low_y, (j == 12) & self.high_y
        self.own_low, self.own_high = (j == 4) & self.low_y, (j == 11) & self.high_y

    def flux(self, v):
        t4 = v[32:40]
        t4 = jnp.where(self.row_low, self.factors[0] * roll(v[0:8], 7, 0), t4)
        t4 = jnp.where(self.row_high, self.factors[1] * roll(v[24:32], 1, 0), t4)
        return jnp.concatenate([v[0:32], t4], 0)


class Level:
    def __init__(self, center, vertical, value, rate, edge_rate, ends, lateral, store, src=None, flag=None):
        self.center, self.vertical, self.value = center, vertical, value
        self.rate, self.edge_rate, self.ends, self.lateral = rate, edge_rate, ends, lateral
        self.store, self.src, self.flag = store, src, flag


def prepare(edges, strips, ends, lateral):
    f2, f3 = edges.factors[2], edges.factors[3]

    def task(at, strip):
        def end(moved):
            v, up, down = moved
            ends[at] = jnp.where(edges.ghost_low, f2 * down, jnp.where(edges.ghost_high, f3 * up, v))
            lateral[at] = jnp.where(edges.own_low, f2 * v, up) + jnp.where(edges.own_high, f3 * v, down)

        def begin():
            v = strip()
            return v, roll(v, 1, 1), roll(v, -1, 1)

        return begin, end

    def turn(at, _):
        def begin():
            v = ends[at]
            return v, roll(v, -10, 1)

        def end(moved):
            ends[at] = jnp.where(edges.j == 3, *moved)

        return begin, end

    pipeline([task(*s) for s in strips])
    pipeline([turn(*s) for s in strips])


def sweep(levels, table):
    lane = iota((EXT, COLS), 1)
    half = FIELDS // 2

    def pair(e, f):
        at = PAIR + FIELDS * e + f
        return table[at : at + 1, :]

    def field(level, f):
        def begin():
            v = level.center(f)
            return v, roll(level.ends(), -(SLOT * f + 3), 1), roll(v, 1, 1), roll(v, -1, 1)

        def end(moved):
            v, edge, left, right = moved
            left = jnp.where(lane == 0, edge, left)
            right = jnp.where(lane == COLS - 1, edge, right)
            beside = level.vertical(f) + roll(v, -1, 0) + roll(v, 1, 0) + right + left
            coupled = pair(0, f) * level.value(0)
            for e in range(1, FIELDS):
                coupled = coupled + pair(e, f) * level.value(e)
            rest = beside - coupled
            if f == 0 and level.src is not None:
                rest = rest + level.flag * level.src[0]
            level.store(f, keep_rate * level.value(f) + level.rate() * rest)

        return begin, end

    def strip(level):
        sums = []

        def mixed(first):
            def begin():
                a = level.value(FIELDS)
                return [lanes_of(a, e) for e in range(first, first + half)]

            def end(moved):
                terms = [v * table[MIX + first + i : MIX + first + i + 1, :] for i, v in enumerate(moved)]
                sums.append(terms[0] + terms[1] + terms[2])

            return begin, end

        def end(_):
            v = level.center(FIELDS)
            rest = level.vertical(FIELDS) + roll(v, -1, 0) + roll(v, 1, 0) + level.lateral() - (sums[0] + sums[1])
            if level.src is not None:
                rest = rest + level.flag * level.src[1]
            level.store(FIELDS, keep_rate * level.value(FIELDS) + level.edge_rate() * rest)

        return [mixed(0), mixed(half), (lambda: None, end)]

    pipeline([task for level in levels for task in strip(level) + [field(level, f) for f in range(FIELDS)]])


def level_sums(z, info, field, edge_strip, strip, metric, metric_row, sums, out, zo):
    total_z = info[5] * LEV
    w = 1.0 - 0.5 * ((jnp.int32(info[2] * LEV + z).astype(jnp.float32) + 0.5) / total_z)
    totals = None
    for f in range(FIELDS):
        a = field(f)
        own = a[:ROWS]
        out[f, zo] = own
        terms = [metric[k, f, z] * own for k in range(3)] + [metric_row[f, z] * a[ROWS:]]
        totals = terms if f == 0 else [s + t for s, t in zip(totals, terms)]
    s = strip[z, :ROWS]
    j = iota((ROWS, COLS), 1) % SLOT
    m = jnp.where(j == 3, roll(s, 3, 1), jnp.where(j == 12, roll(s, -3, 1), 0.0))
    sums[0, :ROWS] += w * totals[0]
    sums[1, :ROWS] += w * totals[1]
    sums[1, ROWS:] += w * totals[3]
    sums[2, :ROWS] += w * totals[2]
    sums[3, :ROWS] += w * (m * edge_strip[:ROWS])


TILES = 15 * 32
MESSAGE = TILES + 7 * 8


def halo_tile(from_low, from_high, z, p):
    at = 2 if p == RATE else 3
    start = LOW_AT[p] - (8 - at)
    above, below = from_high[z, pl.ds(HIGH_AT[p], 8), :], from_low[z, pl.ds(start, 8), :]
    return jnp.where(iota((8, COLS), 0) < 4, above, below)


def pack_z(far, table, strip, from_b, from_a, adj, eddy, diag, msg):
    info = place()
    from_low, from_high = two_sides(info[0] % 2 == 0, from_a, from_b)
    edges = Edges(info, table)
    top = (info[2] % 2 == 0) != far

    def plane(z, p):
        own = adj[p, z] if p < FIELDS else eddy[z] if p == EDDY else relax_rate / diag[z] if p == RATE else strip[z]
        return jnp.concatenate([own, halo_tile(from_low, from_high, z, p)], 0)

    near = jnp.where(top, LEV - 1, 0)
    next_ = jnp.where(top, LEV - 2, 1)
    row, j = iota((8, COLS), 0), iota((EXT, COLS), 1) % SLOT
    s = plane(next_, STRIP)
    second = edges.flux(s * lanes_of(s, EDDY))
    held = None
    for p in range(9):
        v = plane(near, p)
        if p == STRIP:
            v = jnp.where(j == 0, roll(second, -3, 1), jnp.where(j == 15, roll(second, 3, 1), v))
        msg[32 * p : 32 * p + 32, :] = v[:ROWS]
        tile = v[ROWS:]
        if p % 2 == 1:
            moved = jnp.where(row < 4, roll(tile, 2, 0), roll(tile, -2, 0))
            tile = jnp.where((row >= 2) & (row < 6), moved, held)
        if p % 2 == 1 or p == 8:
            at = TILES + 8 * (p // 2)
            msg[at : at + 8, :] = tile
        held = tile
    e = plane(next_, EDDY)
    for f in range(FIELDS):
        v = edges.flux(plane(next_, f) * e)
        msg[32 * (9 + f) : 32 * (10 + f), :] = v[:ROWS]
        tile, k = v[ROWS:], f % 4
        if k > 0:
            tile = jnp.where(row == k, roll(tile, k, 0), jnp.where(row == 7 - k, roll(tile, -k, 0), held))
        if k == 3 or f == FIELDS - 1:
            at = TILES + 8 * (5 + f // 4)
            msg[at : at + 8, :] = tile
        held = tile


def unpack_z(msg, planes):
    row, j = iota((8, COLS), 0), iota((EXT, COLS), 1) % SLOT
    for p in range(15):
        at, k = (TILES + 8 * (p // 2), 2 * (p % 2)) if p < 9 else (TILES + 8 * (5 + (p - 9) // 4), (p - 9) % 4)
        tile = msg[at : at + 8, :]
        if k > 0:
            tile = jnp.where(row < 4, roll(tile, -k, 0), roll(tile, k, 0))
        planes[p] = jnp.concatenate([msg[32 * p : 32 * p + 32, :], tile], 0)
    s = planes[STRIP]
    planes[15] = jnp.where(j == 3, roll(s, 3, 1), jnp.where(j == 12, roll(s, -3, 1), 0.0))


def inner_levels(
    table, adj, eddy, diag, strip, from_b, from_a, metric, src,
    f0, near1, next2, f1, rates, edge_eddy, edge_rate, out, sums, halo, metric_row, a1, a2, ends, lateral,
):
    info = place()
    from_low, from_high = two_sides(info[0] % 2 == 0, from_a, from_b)
    edges = Edges(info, table)
    row = iota((8, COLS), 0)
    for z in range(LEV):
        for p in range(9):
            halo[z, p] = halo_tile(from_low, from_high, z, p)
        for f in range(FIELDS):
            above = jnp.broadcast_to(from_high[z, HIGH_METRIC + f : HIGH_METRIC + f + 1, :], (8, COLS))
            below = jnp.broadcast_to(from_low[z, LOW_METRIC + f : LOW_METRIC + f + 1, :], (8, COLS))
            metric_row[f, z] = jnp.where(row < 4, above, below)
    hub = info[5] * LEV // 4 - info[2] * LEV
    flag = jnp.where(hub == 0, 1.0, 0.0).astype(jnp.float32)

    def value(z, p):
        own = adj[p, z] if p < FIELDS else strip[z]
        return jnp.concatenate([own, halo[z, STRIP if p == FIELDS else p]], 0)

    def eddies(z):
        return jnp.concatenate([eddy[z], halo[z, EDDY]], 0)

    for z in range(LEV):
        rates[z] = jnp.concatenate([relax_rate / diag[z], halo[z, RATE]], 0)
        s = value(z, FIELDS)
        edge_eddy[z] = lanes_of(s, EDDY)
        edge_rate[z] = lanes_of(s, RATE)
    for z in range(LEV):
        e = eddies(z)
        for f in range(FIELDS):
            f0[z, f] = edges.flux(value(z, f) * e)
        f0[z, FIELDS] = edges.flux(value(z, FIELDS) * edge_eddy[z])

    def strips_of(array, zs):
        return [(z, lambda z=z: array[z, FIELDS]) for z in zs]

    def level(z, flux, value, vertical, store, **more):
        return Level(
            lambda p: flux[z, p],
            vertical,
            lambda p: value(z, p),
            lambda: rates[z],
            lambda: edge_rate[z],
            lambda: ends[z],
            lambda: lateral[z],
            store,
            **more,
        )

    def store_first(z):
        def store(p, v):
            if z in (0, LEV - 1):
                near1[z // (LEV - 1), p] = v
            else:
                a1[z, p] = v
                f1[z, p] = edges.flux(v * (edge_eddy[z] if p == FIELDS else eddies(z)))

        return store

    def store_second(z):
        def store(p, v):
            if z in (1, LEV - 2):
                next2[z // (LEV - 2), p] = v
            else:
                a2[z, p] = v

        return store

    def around(array, z, low, high):
        if z == low:
            return lambda p: array[z + 1, p]
        if z == high:
            return lambda p: array[z - 1, p]
        return lambda p: array[z - 1, p] + array[z + 1, p]

    prepare(edges, strips_of(f0, range(LEV)), ends, lateral)
    sweep(
        [
            level(z, f0, value, around(f0, z, 0, LEV - 1), store_first(z), **({"src": src, "flag": flag} if z == 0 else {}))
            for z in range(LEV)
        ],
        table,
    )
    inside = range(1, LEV - 1)
    prepare(edges, strips_of(f1, inside), ends, lateral)
    sweep([level(z, f1, lambda z, p: a1[z, p], around(f1, z, 1, LEV - 2), store_second(z)) for z in inside], table)
    sums[...] = jnp.zeros_like(sums)
    for z in range(2, LEV - 2):
        level_sums(z, info, lambda f: a2[z, f], a2[z, FIELDS], strip, metric, metric_row, sums, out, z - 2)


def outer_levels(
    table, eddy, strip, from_b, from_a, metric, src,
    f0, near1, next2, f1, rates, edge_eddy, edge_rate, inner_out, inner_sums, halo_rows, metric_row,
    out, share, sums, halo_a, halo_b, fh, gh, an, gn, a2, edge_over, ends, lateral,
):
    info = place()
    edges = Edges(info, table)
    hub = info[5] * LEV // 4 - info[2] * LEV
    sums[...] = inner_sums[...]
    for f in range(FIELDS):
        for z in range(2, LEV - 2):
            out[f, z] = inner_out[f, z - 2]
    even = info[2] % 2 == 0

    def flag_of(z):
        return jnp.where(z == hub, 1.0, 0.0).astype(jnp.float32)

    def side(n, msg):
        top = even if n == 0 else jnp.logical_not(even)
        near, next_ = jnp.where(top, LEV - 1, 0), jnp.where(top, LEV - 2, 1)
        ghost = jnp.where(top, edges.high_z, edges.low_z)
        factor = jnp.where(top, edges.factors[5], edges.factors[4])
        return n, msg, jnp.where(top, 1, 0), near, next_, jnp.where(top, LEV, -1), ghost, factor

    unpack_z(from_a, halo_a)
    unpack_z(from_b, halo_b)
    sides = [side(0, halo_a), side(1, halo_b)]
    for n, msg, *_ in sides:
        edge_over[n, 0] = lanes_of(msg[STRIP], EDDY)
        edge_over[n, 1] = lanes_of(msg[STRIP], RATE)
    for n, msg, i, near, next_, over, ghost, factor in sides:
        eddy_near = jnp.concatenate([eddy[near], halo_rows[near, EDDY]], 0)
        for p in (FIELDS, *range(FIELDS)):
            v = msg[STRIP] * edge_over[n, 0] if p == FIELDS else msg[p] * msg[EDDY]
            v = jnp.where(ghost, factor * f0[near, p], edges.flux(v))
            fh[n, p] = v
            r, e = (edge_rate[near], edge_eddy[near]) if p == FIELDS else (rates[near], eddy_near)
            v = near1[i, p] + r * v
            an[n, p] = v
            gn[n, p] = edges.flux(v * e)
    prepare(edges, [(n, lambda n=n: fh[n, FIELDS]) for n in range(2)], ends, lateral)
    prepare(edges, [(2 + n, lambda n=n: gn[n, FIELDS]) for n in range(2)], ends, lateral)

    def over_level(n, msg, i, near, next_, over, ghost, factor):
        def store(p, v):
            v = edges.flux(v * (edge_over[n, 0] if p == FIELDS else msg[EDDY]))
            gh[n, p] = jnp.where(ghost, factor * gn[n, p], v)

        return Level(
            lambda p: fh[n, p],
            lambda p: msg[9 + p] + f0[near, p],
            lambda p: msg[STRIP if p == FIELDS else p],
            lambda: msg[RATE],
            lambda: edge_over[n, 1],
            lambda: ends[n],
            lambda: lateral[n],
            store,
            src,
            flag_of(over),
        )

    def near_level(n, msg, i, near, next_, over, ghost, factor):
        def store(p, v):
            a2[n, p] = v

        return Level(
            lambda p: gn[n, p],
            lambda p: gh[n, p] + f1[next_, p],
            lambda p: an[n, p],
            lambda: rates[near],
            lambda: edge_rate[near],
            lambda: ends[2 + n],
            lambda: lateral[2 + n],
            store,
            src,
            flag_of(near),
        )

    sweep([over_level(*s) for s in sides], table)
    for n, msg, i, near, next_, over, ghost, factor in sides:

        def after(p):
            return next2[i, p] + (edge_rate[next_] if p == FIELDS else rates[next_]) * gn[n, p]

        level_sums(next_, info, after, after(FIELDS), strip, metric, metric_row, sums, out, next_)
    sweep([near_level(*s) for s in sides], table)
    for n, msg, i, near, *_ in sides:
        level_sums(near, info, lambda f: a2[n, f], a2[n, FIELDS], strip, metric, metric_row, sums, out, near)

    s1 = sums[1]
    stream = roll(s1, -1, 0)[:ROWS] - roll(s1, 1, 0)[:ROWS]
    t = sums[3, :ROWS]
    s2 = sums[2, :ROWS]
    lane = iota((ROWS, COLS), 1)
    right, left = roll(s2, -1, 1), roll(s2, 1, 1)
    high = [roll(t, COLS - 1 - (SLOT * f + 12), 1) for f in range(FIELDS)]
    low = [roll(t, -(SLOT * f + 3), 1) for f in range(FIELDS)]
    right = jnp.where(lane == COLS - 1, (high[0] + high[1] + high[2]) + (high[3] + high[4] + high[5]), right)
    left = jnp.where(lane == 0, (low[0] + low[1] + low[2]) + (low[3] + low[4] + low[5]), left)
    total = sums[0, :ROWS] - 0.5 * stream - 0.5 * (right - left)
    turned = jnp.concatenate([total, jnp.zeros((COLS - ROWS, COLS), jnp.float32)], 0).T
    for k in range(share.shape[0]):
        share[k] = turned[share.shape[1] * k : share.shape[1] * (k + 1)]


def add_shares(parts, out):
    total = parts[0]
    for i in range(1, parts.shape[0]):
        total = total + parts[i]
    out[...] = total[:, :ROWS]


def call(body, outs, ins, scratch=()):
    return pl.pallas_call(
        body,
        out_shape=outs,
        in_specs=ins,
        out_specs=jax.tree.map(lambda _: VM, outs),
        scratch_shapes=list(scratch),
        compiler_params=pltpu.CompilerParams(vmem_limit_bytes=16 << 20),
        cost_estimate=pl.CostEstimate(flops=1000000, bytes_accessed=1 << 20, transcendentals=0),
    )


def local(adjoint_start, eddy_visc, diag_coef, coupling, metric_terms, sample_cells, sample_weights, face_codes):
    slices = lax.axis_size("gz")
    cells, weights = sample_cells.reshape(16, 128), sample_weights.reshape(16, 128)

    def trade(v, axis, first):
        n = lax.axis_size(axis)
        pairs = [(i, i + 1) for i in range(first, n - 1, 2)]
        return lax.ppermute(v, axis, pairs + [(b, a) for a, b in pairs])

    def buf(*shape):
        return pltpu.VMEM(shape, jnp.float32)

    level = (LEV, ROWS, COLS)
    own, msg_a, msg_b = call(
        pack_y,
        (f32(*level), f32(2, ROWS, COLS), f32(2, ROWS, COLS)),
        [VM] * 4,
        [buf(*level)],
    )(adjoint_start, eddy_visc, diag_coef, metric_terms[2:3])
    beside = trade(msg_b, "gy", 1), trade(msg_a, "gy", 0)
    strip, msg_a, msg_b = call(pack_x, (f32(*level),) * 3, [VM] * 7, [buf(*level)] * 2)(
        own, *beside, adjoint_start, eddy_visc, diag_coef, metric_terms
    )
    beside = trade(msg_b, "gx", 1), trade(msg_a, "gx", 0)
    src, table = call(
        make_source, (f32(2, EXT, COLS), f32(56, COLS)), [SM] * 2 + [VM] * 3
    )(face_codes, coupling, cells, weights, strip)
    received = (*beside, adjoint_start, eddy_visc, diag_coef)
    msg_b, msg_a = [
        call(functools.partial(pack_z, far), f32(MESSAGE, COLS), [VM] * 7)(table, strip, *received)
        for far in (True, False)
    ]
    from_b = trade(msg_b, "gz", 1)
    from_a = trade(msg_a, "gz", 0)
    ext = (EXT, COLS)
    inner = call(
        inner_levels,
        (
            f32(LEV, 7, *ext),
            f32(2, 7, *ext),
            f32(2, 7, *ext),
            f32(LEV, 7, *ext),
            f32(LEV, *ext),
            f32(LEV, *ext),
            f32(LEV, *ext),
            f32(FIELDS, LEV - 4, ROWS, COLS),
            f32(4, *ext),
            f32(LEV, 9, 8, COLS),
            f32(FIELDS, LEV, 8, COLS),
        ),
        [VM] * 9,
        [buf(LEV, 7, *ext), buf(LEV, 7, *ext), buf(LEV, *ext), buf(LEV, *ext)],
    )(table, adjoint_start, eddy_visc, diag_coef, strip, *beside, metric_terms, src)
    adjoint, share = call(
        outer_levels,
        (f32(FIELDS, *level), f32(slices, COLS // slices, COLS)),
        [VM] * 18,
        [buf(4, *ext), buf(16, *ext), buf(16, *ext)] + [buf(2, 7, *ext)] * 5 + [buf(2, 2, *ext), buf(4, *ext), buf(4, *ext)],
    )(table, eddy_visc, strip, from_b, from_a, metric_terms, src, *inner)
    parts = lax.all_to_all(share, "gz", 0, 0, tiled=True)
    height_grad = call(add_shares, f32(COLS // slices, ROWS), [VM])(parts).T
    return (adjoint, height_grad)


def solution(mesh):
    return jax.shard_map(
        local,
        mesh=mesh,
        in_specs=(
            P(None, "gz", "gx", "gy"),
            P("gz", "gx", "gy"),
            P("gz", "gx", "gy"),
            P(),
            P(None, None, "gz", "gx", "gy"),
            P(),
            P(),
            P(),
        ),
        out_specs=(P(None, "gz", "gx", "gy"), P("gx", ("gy", "gz"))),
        check_vma=False,
    )
```

```python
import functools

import jax
import jax.numpy as jnp
from jax import lax
from jax.experimental import pallas as pl
from jax.experimental.pallas import tpu as pltpu
from jax.sharding import PartitionSpec as P

relax_rate = 0.9
keep_rate = 0.1

FIELDS = 6
LEV = 8
ROWS = 32
COLS = 128
EXT = 40
EDDY, RATE, STRIP = 6, 7, 8
SLOT = 16

VM = pl.BlockSpec(memory_space=pltpu.VMEM)
SM = pl.BlockSpec(memory_space=pltpu.SMEM)


def roll(v, shift, axis):
    return pltpu.roll(v, shift % v.shape[axis], axis)


def iota(shape, axis):
    return lax.broadcasted_iota(jnp.int32, shape, axis)


def f32(*shape):
    return jax.ShapeDtypeStruct(shape, jnp.float32)


def pipeline(tasks):
    held = None
    for begin, end in tasks:
        started = begin()
        if held is not None:
            held[0](held[1])
        held = (end, started)
    held[0](held[1])


def place():
    return [lax.axis_index(a) for a in ("gx", "gy", "gz")] + [lax.axis_size(a) for a in ("gx", "gy", "gz")]


class Either:
    def __init__(self, condition, first, second):
        self.condition, self.first, self.second = condition, first, second

    def __getitem__(self, at):
        return jnp.where(self.condition, self.first[at], self.second[at])


def two_sides(even, from_a, from_b):
    return Either(even, from_b, from_a), Either(even, from_a, from_b)


def pack_y(adj, eddy, diag, metric, own, msg_a, msg_b, packed):
    even = place()[1] % 2 == 0
    shape = (4, 8, COLS)
    lane = iota(shape, 2)
    slot, j = lane // SLOT, lane % SLOT
    quad, jj = j // 4, j % 4

    def block(zg, t):
        return pl.ds(4 * zg, 4), pl.ds(8 * t, 8)

    def gather(zg, t):
        zs, rows = block(zg, t)

        def planes(p):
            if p >= 8:
                return roll(metric[0, p - 8, zs, rows, :], SLOT * (p - 8) + 9, 2)
            v = adj[p, zs, rows, :] if p < FIELDS else eddy[zs, rows, :] if p == EDDY else relax_rate / diag[zs, rows, :]
            return roll(v, SLOT * p + 4, 2)

        def choose(p, v, c):
            if p >= 8:
                return jnp.where((slot == p - 8) & (j >= 8) & (j <= 9), v, c)
            return jnp.where((slot == p) & (j >= 1) & (j <= 6), v, c)

        c = jnp.zeros(shape, jnp.float32)
        ahead = [planes(0), planes(1), planes(2)]
        for p in range(14):
            if p + 3 < 14:
                ahead.append(planes(p + 3))
            c = choose(p, ahead[p], c)
        packed[zs, rows, :] = c

    def send(zg, t):
        zs, rows = block(zg, t)
        c = packed[zs, rows, :]
        c8 = roll(c, 8, 2)
        right = left = jnp.zeros((8, COLS), jnp.float32)
        moved = []
        for zq in range(4):
            at = 4 * zq
            moved.append([roll(c[zq], at + by, 1) for by in (-8, 0, -6, -4)])
        own[zs, rows, :] = jnp.where(j < 8, c, jnp.where(j >= 9, c8, 0.0))
        for zq in range(4):
            r0, r1, l0, l1 = moved[zq]
            here = quad[0] == zq
            right = jnp.where(here, jnp.where(jj[0] == 0, r0, r1), right)
            left = jnp.where(here, jnp.where(jj[0] == 3, l0, l1), left)
        msg_a[zg, rows, :] = jnp.where(even, right, left)
        msg_b[zg, rows, :] = jnp.where(even, left, right)

    blocks = [(zg, t) for zg in range(2) for t in range(ROWS // 8)]
    for zg, t in blocks:
        gather(zg, t)
    for zg, t in blocks:
        send(zg, t)


MIX, PAIR = 8, 16


def make_source(codes, coup, cells, weights, after, src, table):
    slot = iota((1, COLS), 1) // SLOT
    for i in range(6):
        factor = jnp.where(codes[i] == 1, 1.0, jnp.where(codes[i] == 2, -1.0, 0.0)).astype(jnp.float32)
        table[i : i + 1, :] = jnp.full((1, COLS), factor)
    for e in range(FIELDS):
        v = jnp.zeros((1, COLS), jnp.float32)
        for f in range(FIELDS):
            v = jnp.where(slot == f, coup[e, f], v)
            at = PAIR + FIELDS * e + f
            table[at : at + 1, :] = jnp.full((1, COLS), coup[e, f])
        table[MIX + e : MIX + e + 1, :] = v
    info = place()
    start_x, start_y, total_y = info[0] * ROWS, info[1] * COLS, info[4] * COLS
    r = iota((48, COLS), 0)
    row_x = jnp.where(r < EXT - 5, r, r - EXT) + start_x
    row_x = jnp.where(r < EXT, row_x, -1)
    l = iota((2 * COLS, COLS), 0)
    j = l - COLS
    col_y = jnp.where((j >= 1) & (j <= 6), j - 4, j + (COLS - 12))
    col_y = jnp.where(l < COLS, l, col_y) + start_y
    col_y = jnp.where((l < COLS) | ((j >= 1) & (j <= 6)) | ((j >= 9) & (j <= 14)), col_y, -1)
    acc = jnp.zeros((144, 2 * COLS), jnp.float32)
    for k in range(0, 16, 2):
        left, one = [], []
        for q in (k, k + 1):
            c = cells[q : q + 1, :]
            w = weights[q : q + 1, :]
            x = ((c.astype(jnp.float32) + 0.5) * (1.0 / total_y)).astype(jnp.int32)
            y = c - x * total_y
            high = w.astype(jnp.bfloat16).astype(jnp.float32)
            mid = (w - high).astype(jnp.bfloat16).astype(jnp.float32)
            low = w - high - mid
            hit = row_x == x
            left.append(jnp.concatenate([jnp.where(hit, v, 0.0).astype(jnp.bfloat16) for v in (low, mid, high)], 0))
            one.append(jnp.where(col_y == y, 1.0, 0.0).astype(jnp.bfloat16))
        acc = acc + lax.dot_general(
            jnp.concatenate(left, 1),
            jnp.concatenate(one, 1),
            (((1,), (1,)), ((), ())),
            preferred_element_type=jnp.float32,
        )
    total = acc[0:EXT, :] + acc[48 : 48 + EXT, :] + acc[96 : 96 + EXT, :]
    src[0] = total[:, :COLS]
    src[1] = total[:, COLS:]


HIGH_AT = [0, 3, 6, 9, 12, 15, 18, 21, 23]
LOW_AT = [6 + a for a in HIGH_AT]
HIGH_METRIC, LOW_METRIC = 26, 0


def pack_x(own, from_a, from_b, adj, eddy, diag, metric, strip, msg_a, msg_b, to_low, to_high):
    info = place()
    from_left, from_right = two_sides(info[1] % 2 == 0, from_a, from_b)
    even = info[0] % 2 == 0
    j = iota((ROWS, COLS), 1) % SLOT
    for z in range(LEV):
        zg, at = z // 4, 4 * (z % 4)
        low = roll(from_left[zg], -at, 1)
        high = roll(from_right[zg], 12 - at, 1)
        s = jnp.where(j < 4, low, jnp.where(j >= 12, high, own[z]))
        strip[z] = s
        sides = ((to_low, 0, 0, 0, HIGH_AT, HIGH_METRIC), (to_high, ROWS - 3, ROWS - 2, ROWS - 1, LOW_AT, LOW_METRIC))
        for msg, a, b, near, at, metric_at in sides:
            for p in range(FIELDS):
                msg[z, at[p] : at[p] + 3, :] = adj[p, z, a : a + 3, :]
                msg[z, metric_at + p : metric_at + p + 1, :] = metric[1, p, z, near : near + 1, :]
            msg[z, at[EDDY] : at[EDDY] + 3, :] = eddy[z, a : a + 3, :]
            msg[z, at[RATE] : at[RATE] + 2, :] = relax_rate / diag[z, b : b + 2, :]
            msg[z, at[STRIP] : at[STRIP] + 3, :] = s[a : a + 3, :]
    for z in range(LEV):
        low, high = to_low[z], to_high[z]
        msg_a[z] = jnp.where(even, high, low)
        msg_b[z] = jnp.where(even, low, high)


def lanes_of(v, plane):
    return jnp.take_along_axis(v, iota(v.shape, 1) % SLOT + SLOT * plane, axis=1)


class Edges:
    def __init__(self, info, table):
        self.low_x, self.high_x = info[0] == 0, info[0] == info[3] - 1
        self.low_y, self.high_y = info[1] == 0, info[1] == info[4] - 1
        self.low_z, self.high_z = info[2] == 0, info[2] == info[5] - 1
        self.factors = [table[i : i + 1, :] for i in range(6)]
        row, j = iota((8, COLS), 0), iota((EXT, COLS), 1) % SLOT
        self.row_low, self.row_high = (row == 7) & self.low_x, (row == 0) & self.high_x
        self.j = j
        self.ghost_low, self.ghost_high = (j == 3) & self.low_y, (j == 12) & self.high_y
        self.own_low, self.own_high = (j == 4) & self.low_y, (j == 11) & self.high_y

    def flux(self, v):
        t4 = v[32:40]
        t4 = jnp.where(self.row_low, self.factors[0] * roll(v[0:8], 7, 0), t4)
        t4 = jnp.where(self.row_high, self.factors[1] * roll(v[24:32], 1, 0), t4)
        return jnp.concatenate([v[0:32], t4], 0)


class Level:
    def __init__(self, center, vertical, value, rate, edge_rate, ends, lateral, store, src=None, flag=None):
        self.center, self.vertical, self.value = center, vertical, value
        self.rate, self.edge_rate, self.ends, self.lateral = rate, edge_rate, ends, lateral
        self.store, self.src, self.flag = store, src, flag


def prepare(edges, strips, ends, lateral):
    f2, f3 = edges.factors[2], edges.factors[3]

    def task(at, strip):
        def end(moved):
            v, up, down = moved
            ends[at] = jnp.where(edges.ghost_low, f2 * down, jnp.where(edges.ghost_high, f3 * up, v))
            lateral[at] = jnp.where(edges.own_low, f2 * v, up) + jnp.where(edges.own_high, f3 * v, down)

        def begin():
            v = strip()
            return v, roll(v, 1, 1), roll(v, -1, 1)

        return begin, end

    def turn(at, _):
        def begin():
            v = ends[at]
            return v, roll(v, -10, 1)

        def end(moved):
            ends[at] = jnp.where(edges.j == 3, *moved)

        return begin, end

    pipeline([task(*s) for s in strips])
    pipeline([turn(*s) for s in strips])


def sweep(levels, table):
    lane = iota((EXT, COLS), 1)
    half = FIELDS // 2

    def pair(e, f):
        at = PAIR + FIELDS * e + f
        return table[at : at + 1, :]

    def field(level, f):
        def begin():
            v = level.center(f)
            return v, roll(level.ends(), -(SLOT * f + 3), 1), roll(v, 1, 1), roll(v, -1, 1)

        def end(moved):
            v, edge, left, right = moved
            left = jnp.where(lane == 0, edge, left)
            right = jnp.where(lane == COLS - 1, edge, right)
            beside = level.vertical(f) + roll(v, -1, 0) + roll(v, 1, 0) + right + left
            coupled = pair(0, f) * level.value(0)
            for e in range(1, FIELDS):
                coupled = coupled + pair(e, f) * level.value(e)
            rest = beside - coupled
            if f == 0 and level.src is not None:
                rest = rest + level.flag * level.src[0]
            level.store(f, keep_rate * level.value(f) + level.rate() * rest)

        return begin, end

    def strip(level):
        sums = []

        def mixed(first):
            def begin():
                a = level.value(FIELDS)
                return [lanes_of(a, e) for e in range(first, first + half)]

            def end(moved):
                terms = [v * table[MIX + first + i : MIX + first + i + 1, :] for i, v in enumerate(moved)]
                sums.append(terms[0] + terms[1] + terms[2])

            return begin, end

        def end(_):
            v = level.center(FIELDS)
            rest = level.vertical(FIELDS) + roll(v, -1, 0) + roll(v, 1, 0) + level.lateral() - (sums[0] + sums[1])
            if level.src is not None:
                rest = rest + level.flag * level.src[1]
            level.store(FIELDS, keep_rate * level.value(FIELDS) + level.edge_rate() * rest)

        return [mixed(0), mixed(half), (lambda: None, end)]

    pipeline([task for level in levels for task in strip(level) + [field(level, f) for f in range(FIELDS)]])


def level_sums(z, info, field, edge_strip, strip, metric, metric_row, sums, out, zo):
    total_z = info[5] * LEV
    w = 1.0 - 0.5 * ((jnp.int32(info[2] * LEV + z).astype(jnp.float32) + 0.5) / total_z)
    totals = None
    for f in range(FIELDS):
        a = field(f)
        own = a[:ROWS]
        out[f, zo] = own
        terms = [metric[k, f, z] * own for k in range(3)] + [metric_row[f, z] * a[ROWS:]]
        totals = terms if f == 0 else [s + t for s, t in zip(totals, terms)]
    s = strip[z, :ROWS]
    j = iota((ROWS, COLS), 1) % SLOT
    m = jnp.where(j == 3, roll(s, 3, 1), jnp.where(j == 12, roll(s, -3, 1), 0.0))
    sums[0, :ROWS] += w * totals[0]
    sums[1, :ROWS] += w * totals[1]
    sums[1, ROWS:] += w * totals[3]
    sums[2, :ROWS] += w * totals[2]
    sums[3, :ROWS] += w * (m * edge_strip[:ROWS])


TILES = 15 * 32
MESSAGE = TILES + 7 * 8


def halo_tile(from_low, from_high, z, p):
    at = 2 if p == RATE else 3
    start = LOW_AT[p] - (8 - at)
    above, below = from_high[z, pl.ds(HIGH_AT[p], 8), :], from_low[z, pl.ds(start, 8), :]
    return jnp.where(iota((8, COLS), 0) < 4, above, below)


def pack_z(far, table, strip, from_b, from_a, adj, eddy, diag, msg):
    info = place()
    from_low, from_high = two_sides(info[0] % 2 == 0, from_a, from_b)
    edges = Edges(info, table)
    top = (info[2] % 2 == 0) != far

    def plane(z, p):
        own = adj[p, z] if p < FIELDS else eddy[z] if p == EDDY else relax_rate / diag[z] if p == RATE else strip[z]
        return jnp.concatenate([own, halo_tile(from_low, from_high, z, p)], 0)

    near = jnp.where(top, LEV - 1, 0)
    next_ = jnp.where(top, LEV - 2, 1)
    row, j = iota((8, COLS), 0), iota((EXT, COLS), 1) % SLOT
    s = plane(next_, STRIP)
    second = edges.flux(s * lanes_of(s, EDDY))
    held = None
    for p in range(9):
        v = plane(near, p)
        if p == STRIP:
            v = jnp.where(j == 0, roll(second, -3, 1), jnp.where(j == 15, roll(second, 3, 1), v))
        msg[32 * p : 32 * p + 32, :] = v[:ROWS]
        tile = v[ROWS:]
        if p % 2 == 1:
            moved = jnp.where(row < 4, roll(tile, 2, 0), roll(tile, -2, 0))
            tile = jnp.where((row >= 2) & (row < 6), moved, held)
        if p % 2 == 1 or p == 8:
            at = TILES + 8 * (p // 2)
            msg[at : at + 8, :] = tile
        held = tile
    e = plane(next_, EDDY)
    for f in range(FIELDS):
        v = edges.flux(plane(next_, f) * e)
        msg[32 * (9 + f) : 32 * (10 + f), :] = v[:ROWS]
        tile, k = v[ROWS:], f % 4
        if k > 0:
            tile = jnp.where(row == k, roll(tile, k, 0), jnp.where(row == 7 - k, roll(tile, -k, 0), held))
        if k == 3 or f == FIELDS - 1:
            at = TILES + 8 * (5 + f // 4)
            msg[at : at + 8, :] = tile
        held = tile


def unpack_z(msg, planes):
    row, j = iota((8, COLS), 0), iota((EXT, COLS), 1) % SLOT
    for p in range(15):
        at, k = (TILES + 8 * (p // 2), 2 * (p % 2)) if p < 9 else (TILES + 8 * (5 + (p - 9) // 4), (p - 9) % 4)
        tile = msg[at : at + 8, :]
        if k > 0:
            tile = jnp.where(row < 4, roll(tile, -k, 0), roll(tile, k, 0))
        planes[p] = jnp.concatenate([msg[32 * p : 32 * p + 32, :], tile], 0)
    s = planes[STRIP]
    planes[15] = jnp.where(j == 3, roll(s, 3, 1), jnp.where(j == 12, roll(s, -3, 1), 0.0))


def inner_levels(
    table, adj, eddy, diag, strip, from_b, from_a, metric, src,
    f0, near1, next2, f1, rates, edge_eddy, edge_rate, out, sums, halo, metric_row, a1, a2, ends, lateral,
):
    info = place()
    from_low, from_high = two_sides(info[0] % 2 == 0, from_a, from_b)
    edges = Edges(info, table)
    row = iota((8, COLS), 0)
    for z in range(LEV):
        for p in range(9):
            halo[z, p] = halo_tile(from_low, from_high, z, p)
        for f in range(FIELDS):
            above = jnp.broadcast_to(from_high[z, HIGH_METRIC + f : HIGH_METRIC + f + 1, :], (8, COLS))
            below = jnp.broadcast_to(from_low[z, LOW_METRIC + f : LOW_METRIC + f + 1, :], (8, COLS))
            metric_row[f, z] = jnp.where(row < 4, above, below)
    hub = info[5] * LEV // 4 - info[2] * LEV
    flag = jnp.where(hub == 0, 1.0, 0.0).astype(jnp.float32)

    def value(z, p):
        own = adj[p, z] if p < FIELDS else strip[z]
        return jnp.concatenate([own, halo[z, STRIP if p == FIELDS else p]], 0)

    def eddies(z):
        return jnp.concatenate([eddy[z], halo[z, EDDY]], 0)

    for z in range(LEV):
        rates[z] = jnp.concatenate([relax_rate / diag[z], halo[z, RATE]], 0)
        s = value(z, FIELDS)
        edge_eddy[z] = lanes_of(s, EDDY)
        edge_rate[z] = lanes_of(s, RATE)
    for z in range(LEV):
        e = eddies(z)
        for f in range(FIELDS):
            f0[z, f] = edges.flux(value(z, f) * e)
        f0[z, FIELDS] = edges.flux(value(z, FIELDS) * edge_eddy[z])

    def strips_of(array, zs):
        return [(z, lambda z=z: array[z, FIELDS]) for z in zs]

    def level(z, flux, value, vertical, store, **more):
        return Level(
            lambda p: flux[z, p],
            vertical,
            lambda p: value(z, p),
            lambda: rates[z],
            lambda: edge_rate[z],
            lambda: ends[z],
            lambda: lateral[z],
            store,
            **more,
        )

    def store_first(z):
        def store(p, v):
            if z in (0, LEV - 1):
                near1[z // (LEV - 1), p] = v
            else:
                a1[z, p] = v
                f1[z, p] = edges.flux(v * (edge_eddy[z] if p == FIELDS else eddies(z)))

        return store

    def store_second(z):
        def store(p, v):
            if z in (1, LEV - 2):
                next2[z // (LEV - 2), p] = v
            else:
                a2[z, p] = v

        return store

    def around(array, z, low, high):
        if z == low:
            return lambda p: array[z + 1, p]
        if z == high:
            return lambda p: array[z - 1, p]
        return lambda p: array[z - 1, p] + array[z + 1, p]

    prepare(edges, strips_of(f0, range(LEV)), ends, lateral)
    sweep(
        [
            level(z, f0, value, around(f0, z, 0, LEV - 1), store_first(z), **({"src": src, "flag": flag} if z == 0 else {}))
            for z in range(LEV)
        ],
        table,
    )
    inside = range(1, LEV - 1)
    prepare(edges, strips_of(f1, inside), ends, lateral)
    sweep([level(z, f1, lambda z, p: a1[z, p], around(f1, z, 1, LEV - 2), store_second(z)) for z in inside], table)
    sums[...] = jnp.zeros_like(sums)
    for z in range(2, LEV - 2):
        level_sums(z, info, lambda f: a2[z, f], a2[z, FIELDS], strip, metric, metric_row, sums, out, z - 2)


def outer_levels(
    table, eddy, strip, from_b, from_a, metric, src,
    f0, near1, next2, f1, rates, edge_eddy, edge_rate, inner_out, inner_sums, halo_rows, metric_row,
    out, share, sums, halo_a, halo_b, fh, gh, an, gn, a2, edge_over, ends, lateral,
):
    info = place()
    edges = Edges(info, table)
    hub = info[5] * LEV // 4 - info[2] * LEV
    sums[...] = inner_sums[...]
    for f in range(FIELDS):
        for z in range(2, LEV - 2):
            out[f, z] = inner_out[f, z - 2]
    even = info[2] % 2 == 0

    def flag_of(z):
        return jnp.where(z == hub, 1.0, 0.0).astype(jnp.float32)

    def side(n, msg):
        top = even if n == 0 else jnp.logical_not(even)
        near, next_ = jnp.where(top, LEV - 1, 0), jnp.where(top, LEV - 2, 1)
        ghost = jnp.where(top, edges.high_z, edges.low_z)
        factor = jnp.where(top, edges.factors[5], edges.factors[4])
        return n, msg, jnp.where(top, 1, 0), near, next_, jnp.where(top, LEV, -1), ghost, factor

    unpack_z(from_a, halo_a)
    unpack_z(from_b, halo_b)
    sides = [side(0, halo_a), side(1, halo_b)]
    for n, msg, *_ in sides:
        edge_over[n, 0] = lanes_of(msg[STRIP], EDDY)
        edge_over[n, 1] = lanes_of(msg[STRIP], RATE)
    for n, msg, i, near, next_, over, ghost, factor in sides:
        eddy_near = jnp.concatenate([eddy[near], halo_rows[near, EDDY]], 0)
        for p in (FIELDS, *range(FIELDS)):
            v = msg[STRIP] * edge_over[n, 0] if p == FIELDS else msg[p] * msg[EDDY]
            v = jnp.where(ghost, factor * f0[near, p], edges.flux(v))
            fh[n, p] = v
            r, e = (edge_rate[near], edge_eddy[near]) if p == FIELDS else (rates[near], eddy_near)
            v = near1[i, p] + r * v
            an[n, p] = v
            gn[n, p] = edges.flux(v * e)
    prepare(edges, [(n, lambda n=n: fh[n, FIELDS]) for n in range(2)], ends, lateral)
    prepare(edges, [(2 + n, lambda n=n: gn[n, FIELDS]) for n in range(2)], ends, lateral)

    def over_level(n, msg, i, near, next_, over, ghost, factor):
        def store(p, v):
            v = edges.flux(v * (edge_over[n, 0] if p == FIELDS else msg[EDDY]))
            gh[n, p] = jnp.where(ghost, factor * gn[n, p], v)

        return Level(
            lambda p: fh[n, p],
            lambda p: msg[9 + p] + f0[near, p],
            lambda p: msg[STRIP if p == FIELDS else p],
            lambda: msg[RATE],
            lambda: edge_over[n, 1],
            lambda: ends[n],
            lambda: lateral[n],
            store,
            src,
            flag_of(over),
        )

    def near_level(n, msg, i, near, next_, over, ghost, factor):
        def store(p, v):
            a2[n, p] = v

        return Level(
            lambda p: gn[n, p],
            lambda p: gh[n, p] + f1[next_, p],
            lambda p: an[n, p],
            lambda: rates[near],
            lambda: edge_rate[near],
            lambda: ends[2 + n],
            lambda: lateral[2 + n],
            store,
            src,
            flag_of(near),
        )

    sweep([over_level(*s) for s in sides], table)
    for n, msg, i, near, next_, over, ghost, factor in sides:

        def after(p):
            return next2[i, p] + (edge_rate[next_] if p == FIELDS else rates[next_]) * gn[n, p]

        level_sums(next_, info, after, after(FIELDS), strip, metric, metric_row, sums, out, next_)
    sweep([near_level(*s) for s in sides], table)
    for n, msg, i, near, *_ in sides:
        level_sums(near, info, lambda f: a2[n, f], a2[n, FIELDS], strip, metric, metric_row, sums, out, near)

    s1 = sums[1]
    stream = roll(s1, -1, 0)[:ROWS] - roll(s1, 1, 0)[:ROWS]
    t = sums[3, :ROWS]
    s2 = sums[2, :ROWS]
    lane = iota((ROWS, COLS), 1)
    right, left = roll(s2, -1, 1), roll(s2, 1, 1)
    high = [roll(t, COLS - 1 - (SLOT * f + 12), 1) for f in range(FIELDS)]
    low = [roll(t, -(SLOT * f + 3), 1) for f in range(FIELDS)]
    right = jnp.where(lane == COLS - 1, (high[0] + high[1] + high[2]) + (high[3] + high[4] + high[5]), right)
    left = jnp.where(lane == 0, (low[0] + low[1] + low[2]) + (low[3] + low[4] + low[5]), left)
    total = sums[0, :ROWS] - 0.5 * stream - 0.5 * (right - left)
    turned = jnp.concatenate([total, jnp.zeros((COLS - ROWS, COLS), jnp.float32)], 0).T
    for k in range(share.shape[0]):
        share[k] = turned[share.shape[1] * k : share.shape[1] * (k + 1)]


def add_shares(parts, out):
    total = parts[0]
    for i in range(1, parts.shape[0]):
        total = total + parts[i]
    out[...] = total[:, :ROWS]


def call(body, outs, ins, scratch=()):
    return pl.pallas_call(
        body,
        out_shape=outs,
        in_specs=ins,
        out_specs=jax.tree.map(lambda _: VM, outs),
        scratch_shapes=list(scratch),
        compiler_params=pltpu.CompilerParams(vmem_limit_bytes=16 << 20),
        cost_estimate=pl.CostEstimate(flops=1000000, bytes_accessed=1 << 20, transcendentals=0),
    )


def local(adjoint_start, eddy_visc, diag_coef, coupling, metric_terms, sample_cells, sample_weights, face_codes):
    slices = lax.axis_size("gz")
    cells, weights = sample_cells.reshape(16, 128), sample_weights.reshape(16, 128)

    def trade(v, axis, first):
        n = lax.axis_size(axis)
        pairs = [(i, i + 1) for i in range(first, n - 1, 2)]
        return lax.ppermute(v, axis, pairs + [(b, a) for a, b in pairs])

    def buf(*shape):
        return pltpu.VMEM(shape, jnp.float32)

    level = (LEV, ROWS, COLS)
    own, msg_a, msg_b = call(
        pack_y,
        (f32(*level), f32(2, ROWS, COLS), f32(2, ROWS, COLS)),
        [VM] * 4,
        [buf(*level)],
    )(adjoint_start, eddy_visc, diag_coef, metric_terms[2:3])
    beside = trade(msg_a, "gy", 0), trade(msg_b, "gy", 1)
    strip, msg_a, msg_b = call(pack_x, (f32(*level),) * 3, [VM] * 7, [buf(*level)] * 2)(
        own, *beside, adjoint_start, eddy_visc, diag_coef, metric_terms
    )
    beside = trade(msg_b, "gx", 1), trade(msg_a, "gx", 0)
    src, table = call(
        make_source, (f32(2, EXT, COLS), f32(56, COLS)), [SM] * 2 + [VM] * 3
    )(face_codes, coupling, cells, weights, strip)
    received = (*beside, adjoint_start, eddy_visc, diag_coef)
    msg_b, msg_a = [
        call(functools.partial(pack_z, far), f32(MESSAGE, COLS), [VM] * 7)(table, strip, *received)
        for far in (True, False)
    ]
    from_b = trade(msg_b, "gz", 1)
    from_a = trade(msg_a, "gz", 0)
    ext = (EXT, COLS)
    inner = call(
        inner_levels,
        (
            f32(LEV, 7, *ext),
            f32(2, 7, *ext),
            f32(2, 7, *ext),
            f32(LEV, 7, *ext),
            f32(LEV, *ext),
            f32(LEV, *ext),
            f32(LEV, *ext),
            f32(FIELDS, LEV - 4, ROWS, COLS),
            f32(4, *ext),
            f32(LEV, 9, 8, COLS),
            f32(FIELDS, LEV, 8, COLS),
        ),
        [VM] * 9,
        [buf(LEV, 7, *ext), buf(LEV, 7, *ext), buf(LEV, *ext), buf(LEV, *ext)],
    )(table, adjoint_start, eddy_visc, diag_coef, strip, *beside, metric_terms, src)
    adjoint, share = call(
        outer_levels,
        (f32(FIELDS, *level), f32(slices, COLS // slices, COLS)),
        [VM] * 18,
        [buf(4, *ext), buf(16, *ext), buf(16, *ext)] + [buf(2, 7, *ext)] * 5 + [buf(2, 2, *ext), buf(4, *ext), buf(4, *ext)],
    )(table, eddy_visc, strip, from_b, from_a, metric_terms, src, *inner)
    parts = lax.all_to_all(share, "gz", 0, 0, tiled=True)
    height_grad = call(add_shares, f32(COLS // slices, ROWS), [VM])(parts).T
    return (adjoint, height_grad)


def solution(mesh):
    return jax.shard_map(
        local,
        mesh=mesh,
        in_specs=(
            P(None, "gz", "gx", "gy"),
            P("gz", "gx", "gy"),
            P("gz", "gx", "gy"),
            P(),
            P(None, None, "gz", "gx", "gy"),
            P(),
            P(),
            P(),
        ),
        out_specs=(P(None, "gz", "gx", "gy"), P("gx", ("gy", "gz"))),
        check_vma=False,
    )
```

```python
import functools

import jax
import jax.numpy as jnp
from jax import lax
from jax.experimental import pallas as pl
from jax.experimental.pallas import tpu as pltpu
from jax.sharding import PartitionSpec as P

relax_rate = 0.9
keep_rate = 0.1

FIELDS = 6
LEV = 8
ROWS = 32
COLS = 128
EXT = 40
EDDY, RATE, STRIP = 6, 7, 8
SLOT = 16

VM = pl.BlockSpec(memory_space=pltpu.VMEM)
SM = pl.BlockSpec(memory_space=pltpu.SMEM)


def roll(v, shift, axis):
    return pltpu.roll(v, shift % v.shape[axis], axis)


def iota(shape, axis):
    return lax.broadcasted_iota(jnp.int32, shape, axis)


def f32(*shape):
    return jax.ShapeDtypeStruct(shape, jnp.float32)


def pipeline(tasks):
    held = None
    for begin, end in tasks:
        started = begin()
        if held is not None:
            held[0](held[1])
        held = (end, started)
    held[0](held[1])


def place():
    return [lax.axis_index(a) for a in ("gx", "gy", "gz")] + [lax.axis_size(a) for a in ("gx", "gy", "gz")]


class Either:
    def __init__(self, condition, first, second):
        self.condition, self.first, self.second = condition, first, second

    def __getitem__(self, at):
        return jnp.where(self.condition, self.first[at], self.second[at])


def two_sides(even, from_a, from_b):
    return Either(even, from_b, from_a), Either(even, from_a, from_b)


def pack_y(adj, eddy, diag, metric, own, msg_a, msg_b, packed):
    even = place()[1] % 2 == 0
    shape = (4, 8, COLS)
    lane = iota(shape, 2)
    slot, j = lane // SLOT, lane % SLOT
    quad, jj = j // 4, j % 4

    def block(zg, t):
        return pl.ds(4 * zg, 4), pl.ds(8 * t, 8)

    def gather(zg, t):
        zs, rows = block(zg, t)

        def planes(p):
            if p >= 8:
                return roll(metric[0, p - 8, zs, rows, :], SLOT * (p - 8) + 9, 2)
            v = adj[p, zs, rows, :] if p < FIELDS else eddy[zs, rows, :] if p == EDDY else relax_rate / diag[zs, rows, :]
            return roll(v, SLOT * p + 4, 2)

        def choose(p, v, c):
            if p >= 8:
                return jnp.where((slot == p - 8) & (j >= 8) & (j <= 9), v, c)
            return jnp.where((slot == p) & (j >= 1) & (j <= 6), v, c)

        c = jnp.zeros(shape, jnp.float32)
        ahead = [planes(0), planes(1), planes(2)]
        for p in range(14):
            if p + 3 < 14:
                ahead.append(planes(p + 3))
            c = choose(p, ahead[p], c)
        packed[zs, rows, :] = c

    def send(zg, t):
        zs, rows = block(zg, t)
        c = packed[zs, rows, :]
        c8 = roll(c, 8, 2)
        right = left = jnp.zeros((8, COLS), jnp.float32)
        moved = []
        for zq in range(4):
            at = 4 * zq
            moved.append([roll(c[zq], at + by, 1) for by in (-8, 0, -6, -4)])
        own[zs, rows, :] = jnp.where(j < 8, c, jnp.where(j >= 9, c8, 0.0))
        for zq in range(4):
            r0, r1, l0, l1 = moved[zq]
            here = quad[0] == zq
            right = jnp.where(here, jnp.where(jj[0] == 0, r0, r1), right)
            left = jnp.where(here, jnp.where(jj[0] == 3, l0, l1), left)
        msg_a[zg, rows, :] = jnp.where(even, right, left)
        msg_b[zg, rows, :] = jnp.where(even, left, right)

    blocks = [(zg, t) for zg in range(2) for t in range(ROWS // 8)]
    for zg, t in blocks:
        gather(zg, t)
    for zg, t in blocks:
        send(zg, t)


MIX, PAIR = 8, 16


def make_source(codes, coup, cells, weights, after, src, table):
    slot = iota((1, COLS), 1) // SLOT
    for i in range(6):
        factor = jnp.where(codes[i] == 1, 1.0, jnp.where(codes[i] == 2, -1.0, 0.0)).astype(jnp.float32)
        table[i : i + 1, :] = jnp.full((1, COLS), factor)
    for e in range(FIELDS):
        v = jnp.zeros((1, COLS), jnp.float32)
        for f in range(FIELDS):
            v = jnp.where(slot == f, coup[e, f], v)
            at = PAIR + FIELDS * e + f
            table[at : at + 1, :] = jnp.full((1, COLS), coup[e, f])
        table[MIX + e : MIX + e + 1, :] = v
    info = place()
    start_x, start_y, total_y = info[0] * ROWS, info[1] * COLS, info[4] * COLS
    r = iota((48, COLS), 0)
    row_x = jnp.where(r < EXT - 5, r, r - EXT) + start_x
    row_x = jnp.where(r < EXT, row_x, -1)
    l = iota((2 * COLS, COLS), 0)
    j = l - COLS
    col_y = jnp.where((j >= 1) & (j <= 6), j - 4, j + (COLS - 12))
    col_y = jnp.where(l < COLS, l, col_y) + start_y
    col_y = jnp.where((l < COLS) | ((j >= 1) & (j <= 6)) | ((j >= 9) & (j <= 14)), col_y, -1)
    acc = jnp.zeros((144, 2 * COLS), jnp.float32)
    for k in range(0, 16, 2):
        left, one = [], []
        for q in (k, k + 1):
            c = cells[q : q + 1, :]
            w = weights[q : q + 1, :]
            x = ((c.astype(jnp.float32) + 0.5) * (1.0 / total_y)).astype(jnp.int32)
            y = c - x * total_y
            high = w.astype(jnp.bfloat16).astype(jnp.float32)
            mid = (w - high).astype(jnp.bfloat16).astype(jnp.float32)
            low = w - high - mid
            hit = row_x == x
            left.append(jnp.concatenate([jnp.where(hit, v, 0.0).astype(jnp.bfloat16) for v in (low, mid, high)], 0))
            one.append(jnp.where(col_y == y, 1.0, 0.0).astype(jnp.bfloat16))
        acc = acc + lax.dot_general(
            jnp.concatenate(left, 1),
            jnp.concatenate(one, 1),
            (((1,), (1,)), ((), ())),
            preferred_element_type=jnp.float32,
        )
    total = acc[0:EXT, :] + acc[48 : 48 + EXT, :] + acc[96 : 96 + EXT, :]
    src[0] = total[:, :COLS]
    src[1] = total[:, COLS:]


HIGH_AT = [0, 3, 6, 9, 12, 15, 18, 21, 23]
LOW_AT = [6 + a for a in HIGH_AT]
HIGH_METRIC, LOW_METRIC = 26, 0


def pack_x(own, from_b, from_a, adj, eddy, diag, metric, strip, msg_a, msg_b, to_low, to_high):
    info = place()
    from_left, from_right = two_sides(info[1] % 2 == 0, from_a, from_b)
    even = info[0] % 2 == 0
    j = iota((ROWS, COLS), 1) % SLOT
    for z in range(LEV):
        zg, at = z // 4, 4 * (z % 4)
        low = roll(from_left[zg], -at, 1)
        high = roll(from_right[zg], 12 - at, 1)
        s = jnp.where(j < 4, low, jnp.where(j >= 12, high, own[z]))
        strip[z] = s
        sides = ((to_low, 0, 0, 0, HIGH_AT, HIGH_METRIC), (to_high, ROWS - 3, ROWS - 2, ROWS - 1, LOW_AT, LOW_METRIC))
        for msg, a, b, near, at, metric_at in sides:
            for p in range(FIELDS):
                msg[z, at[p] : at[p] + 3, :] = adj[p, z, a : a + 3, :]
                msg[z, metric_at + p : metric_at + p + 1, :] = metric[1, p, z, near : near + 1, :]
            msg[z, at[EDDY] : at[EDDY] + 3, :] = eddy[z, a : a + 3, :]
            msg[z, at[RATE] : at[RATE] + 2, :] = relax_rate / diag[z, b : b + 2, :]
            msg[z, at[STRIP] : at[STRIP] + 3, :] = s[a : a + 3, :]
    for z in range(LEV):
        low, high = to_low[z], to_high[z]
        msg_a[z] = jnp.where(even, high, low)
        msg_b[z] = jnp.where(even, low, high)


def lanes_of(v, plane):
    return jnp.take_along_axis(v, iota(v.shape, 1) % SLOT + SLOT * plane, axis=1)


class Edges:
    def __init__(self, info, table):
        self.low_x, self.high_x = info[0] == 0, info[0] == info[3] - 1
        self.low_y, self.high_y = info[1] == 0, info[1] == info[4] - 1
        self.low_z, self.high_z = info[2] == 0, info[2] == info[5] - 1
        self.factors = [table[i : i + 1, :] for i in range(6)]
        row, j = iota((8, COLS), 0), iota((EXT, COLS), 1) % SLOT
        self.row_low, self.row_high = (row == 7) & self.low_x, (row == 0) & self.high_x
        self.j = j
        self.ghost_low, self.ghost_high = (j == 3) & self.low_y, (j == 12) & self.high_y
        self.own_low, self.own_high = (j == 4) & self.low_y, (j == 11) & self.high_y

    def flux(self, v):
        t4 = v[32:40]
        t4 = jnp.where(self.row_low, self.factors[0] * roll(v[0:8], 7, 0), t4)
        t4 = jnp.where(self.row_high, self.factors[1] * roll(v[24:32], 1, 0), t4)
        return jnp.concatenate([v[0:32], t4], 0)


class Level:
    def __init__(self, center, vertical, value, rate, edge_rate, ends, lateral, store, src=None, flag=None):
        self.center, self.vertical, self.value = center, vertical, value
        self.rate, self.edge_rate, self.ends, self.lateral = rate, edge_rate, ends, lateral
        self.store, self.src, self.flag = store, src, flag


def prepare(edges, strips, ends, lateral):
    f2, f3 = edges.factors[2], edges.factors[3]

    def task(at, strip):
        def end(moved):
            v, up, down = moved
            ends[at] = jnp.where(edges.ghost_low, f2 * down, jnp.where(edges.ghost_high, f3 * up, v))
            lateral[at] = jnp.where(edges.own_low, f2 * v, up) + jnp.where(edges.own_high, f3 * v, down)

        def begin():
            v = strip()
            return v, roll(v, 1, 1), roll(v, -1, 1)

        return begin, end

    def turn(at, _):
        def begin():
            v = ends[at]
            return v, roll(v, -10, 1)

        def end(moved):
            ends[at] = jnp.where(edges.j == 3, *moved)

        return begin, end

    pipeline([task(*s) for s in strips])
    pipeline([turn(*s) for s in strips])


def sweep(levels, table):
    lane = iota((EXT, COLS), 1)
    half = FIELDS // 2

    def pair(e, f):
        at = PAIR + FIELDS * e + f
        return table[at : at + 1, :]

    def field(level, f):
        def begin():
            v = level.center(f)
            return v, roll(level.ends(), -(SLOT * f + 3), 1), roll(v, 1, 1), roll(v, -1, 1)

        def end(moved):
            v, edge, left, right = moved
            left = jnp.where(lane == 0, edge, left)
            right = jnp.where(lane == COLS - 1, edge, right)
            beside = level.vertical(f) + roll(v, -1, 0) + roll(v, 1, 0) + right + left
            coupled = pair(0, f) * level.value(0)
            for e in range(1, FIELDS):
                coupled = coupled + pair(e, f) * level.value(e)
            rest = beside - coupled
            if f == 0 and level.src is not None:
                rest = rest + level.flag * level.src[0]
            level.store(f, keep_rate * level.value(f) + level.rate() * rest)

        return begin, end

    def strip(level):
        sums = []

        def mixed(first):
            def begin():
                a = level.value(FIELDS)
                return [lanes_of(a, e) for e in range(first, first + half)]

            def end(moved):
                terms = [v * table[MIX + first + i : MIX + first + i + 1, :] for i, v in enumerate(moved)]
                sums.append(terms[0] + terms[1] + terms[2])

            return begin, end

        def end(_):
            v = level.center(FIELDS)
            rest = level.vertical(FIELDS) + roll(v, -1, 0) + roll(v, 1, 0) + level.lateral() - (sums[0] + sums[1])
            if level.src is not None:
                rest = rest + level.flag * level.src[1]
            level.store(FIELDS, keep_rate * level.value(FIELDS) + level.edge_rate() * rest)

        return [mixed(0), mixed(half), (lambda: None, end)]

    pipeline([task for level in levels for task in strip(level) + [field(level, f) for f in range(FIELDS)]])


def level_sums(z, info, field, edge_strip, strip, metric, metric_row, sums, out, zo):
    total_z = info[5] * LEV
    w = 1.0 - 0.5 * ((jnp.int32(info[2] * LEV + z).astype(jnp.float32) + 0.5) / total_z)
    totals = None
    for f in range(FIELDS):
        a = field(f)
        own = a[:ROWS]
        out[f, zo] = own
        terms = [metric[k, f, z] * own for k in range(3)] + [metric_row[f, z] * a[ROWS:]]
        totals = terms if f == 0 else [s + t for s, t in zip(totals, terms)]
    s = strip[z, :ROWS]
    j = iota((ROWS, COLS), 1) % SLOT
    m = jnp.where(j == 3, roll(s, 3, 1), jnp.where(j == 12, roll(s, -3, 1), 0.0))
    sums[0, :ROWS] += w * totals[0]
    sums[1, :ROWS] += w * totals[1]
    sums[1, ROWS:] += w * totals[3]
    sums[2, :ROWS] += w * totals[2]
    sums[3, :ROWS] += w * (m * edge_strip[:ROWS])


TILES = 15 * 32
MESSAGE = TILES + 7 * 8


def halo_tile(from_low, from_high, z, p):
    at = 2 if p == RATE else 3
    start = LOW_AT[p] - (8 - at)
    above, below = from_high[z, pl.ds(HIGH_AT[p], 8), :], from_low[z, pl.ds(start, 8), :]
    return jnp.where(iota((8, COLS), 0) < 4, above, below)


def pack_z(far, table, strip, from_b, from_a, adj, eddy, diag, msg):
    info = place()
    from_low, from_high = two_sides(info[0] % 2 == 0, from_a, from_b)
    edges = Edges(info, table)
    top = (info[2] % 2 == 0) != far

    def plane(z, p):
        own = adj[p, z] if p < FIELDS else eddy[z] if p == EDDY else relax_rate / diag[z] if p == RATE else strip[z]
        return jnp.concatenate([own, halo_tile(from_low, from_high, z, p)], 0)

    near = jnp.where(top, LEV - 1, 0)
    next_ = jnp.where(top, LEV - 2, 1)
    row, j = iota((8, COLS), 0), iota((EXT, COLS), 1) % SLOT
    s = plane(next_, STRIP)
    second = edges.flux(s * lanes_of(s, EDDY))
    held = None
    for p in range(9):
        v = plane(near, p)
        if p == STRIP:
            v = jnp.where(j == 0, roll(second, -3, 1), jnp.where(j == 15, roll(second, 3, 1), v))
        msg[32 * p : 32 * p + 32, :] = v[:ROWS]
        tile = v[ROWS:]
        if p % 2 == 1:
            moved = jnp.where(row < 4, roll(tile, 2, 0), roll(tile, -2, 0))
            tile = jnp.where((row >= 2) & (row < 6), moved, held)
        if p % 2 == 1 or p == 8:
            at = TILES + 8 * (p // 2)
            msg[at : at + 8, :] = tile
        held = tile
    e = plane(next_, EDDY)
    for f in range(FIELDS):
        v = edges.flux(plane(next_, f) * e)
        msg[32 * (9 + f) : 32 * (10 + f), :] = v[:ROWS]
        tile, k = v[ROWS:], f % 4
        if k > 0:
            tile = jnp.where(row == k, roll(tile, k, 0), jnp.where(row == 7 - k, roll(tile, -k, 0), held))
        if k == 3 or f == FIELDS - 1:
            at = TILES + 8 * (5 + f // 4)
            msg[at : at + 8, :] = tile
        held = tile


def unpack_z(msg, planes):
    row, j = iota((8, COLS), 0), iota((EXT, COLS), 1) % SLOT
    for p in range(15):
        at, k = (TILES + 8 * (p // 2), 2 * (p % 2)) if p < 9 else (TILES + 8 * (5 + (p - 9) // 4), (p - 9) % 4)
        tile = msg[at : at + 8, :]
        if k > 0:
            tile = jnp.where(row < 4, roll(tile, -k, 0), roll(tile, k, 0))
        planes[p] = jnp.concatenate([msg[32 * p : 32 * p + 32, :], tile], 0)
    s = planes[STRIP]
    planes[15] = jnp.where(j == 3, roll(s, 3, 1), jnp.where(j == 12, roll(s, -3, 1), 0.0))


def inner_levels(
    table, adj, eddy, diag, strip, from_b, from_a, metric, src,
    f0, near1, next2, f1, rates, edge_eddy, edge_rate, out, sums, halo, metric_row, a1, a2, ends, lateral,
):
    info = place()
    from_low, from_high = two_sides(info[0] % 2 == 0, from_a, from_b)
    edges = Edges(info, table)
    row = iota((8, COLS), 0)
    for z in range(LEV):
        for p in range(9):
            halo[z, p] = halo_tile(from_low, from_high, z, p)
        for f in range(FIELDS):
            above = jnp.broadcast_to(from_high[z, HIGH_METRIC + f : HIGH_METRIC + f + 1, :], (8, COLS))
            below = jnp.broadcast_to(from_low[z, LOW_METRIC + f : LOW_METRIC + f + 1, :], (8, COLS))
            metric_row[f, z] = jnp.where(row < 4, above, below)
    hub = info[5] * LEV // 4 - info[2] * LEV
    flag = jnp.where(hub == 0, 1.0, 0.0).astype(jnp.float32)

    def value(z, p):
        own = adj[p, z] if p < FIELDS else strip[z]
        return jnp.concatenate([own, halo[z, STRIP if p == FIELDS else p]], 0)

    def eddies(z):
        return jnp.concatenate([eddy[z], halo[z, EDDY]], 0)

    for z in range(LEV):
        rates[z] = jnp.concatenate([relax_rate / diag[z], halo[z, RATE]], 0)
        s = value(z, FIELDS)
        edge_eddy[z] = lanes_of(s, EDDY)
        edge_rate[z] = lanes_of(s, RATE)
    for z in range(LEV):
        e = eddies(z)
        for f in range(FIELDS):
            f0[z, f] = edges.flux(value(z, f) * e)
        f0[z, FIELDS] = edges.flux(value(z, FIELDS) * edge_eddy[z])

    def strips_of(array, zs):
        return [(z, lambda z=z: array[z, FIELDS]) for z in zs]

    def level(z, flux, value, vertical, store, **more):
        return Level(
            lambda p: flux[z, p],
            vertical,
            lambda p: value(z, p),
            lambda: rates[z],
            lambda: edge_rate[z],
            lambda: ends[z],
            lambda: lateral[z],
            store,
            **more,
        )

    def store_first(z):
        def store(p, v):
            if z in (0, LEV - 1):
                near1[z // (LEV - 1), p] = v
            else:
                a1[z, p] = v
                f1[z, p] = edges.flux(v * (edge_eddy[z] if p == FIELDS else eddies(z)))

        return store

    def store_second(z):
        def store(p, v):
            if z in (1, LEV - 2):
                next2[z // (LEV - 2), p] = v
            else:
                a2[z, p] = v

        return store

    def around(array, z, low, high):
        if z == low:
            return lambda p: array[z + 1, p]
        if z == high:
            return lambda p: array[z - 1, p]
        return lambda p: array[z - 1, p] + array[z + 1, p]

    prepare(edges, strips_of(f0, range(LEV)), ends, lateral)
    sweep(
        [
            level(z, f0, value, around(f0, z, 0, LEV - 1), store_first(z), **({"src": src, "flag": flag} if z == 0 else {}))
            for z in range(LEV)
        ],
        table,
    )
    inside = range(1, LEV - 1)
    prepare(edges, strips_of(f1, inside), ends, lateral)
    sweep([level(z, f1, lambda z, p: a1[z, p], around(f1, z, 1, LEV - 2), store_second(z)) for z in inside], table)
    sums[...] = jnp.zeros_like(sums)
    for z in range(2, LEV - 2):
        level_sums(z, info, lambda f: a2[z, f], a2[z, FIELDS], strip, metric, metric_row, sums, out, z - 2)


def outer_levels(
    table, eddy, strip, from_b, from_a, metric, src,
    f0, near1, next2, f1, rates, edge_eddy, edge_rate, inner_out, inner_sums, halo_rows, metric_row,
    out, share, levels, sems, sums, halo_a, halo_b, fh, gh, an, gn, a2, edge_over, ends, lateral,
):
    info = place()
    edges = Edges(info, table)
    hub = info[5] * LEV // 4 - info[2] * LEV
    sums[...] = inner_sums[...]
    copies = []

    def leave(ref, at, z):
        copies.append(pltpu.make_async_copy(ref, out.at[:, z], sems.at[at]))
        copies[-1].start()

    for z in range(2, LEV - 2):
        leave(inner_out.at[:, z - 2], z - 2, z)
    even = info[2] % 2 == 0

    def flag_of(z):
        return jnp.where(z == hub, 1.0, 0.0).astype(jnp.float32)

    def side(n, msg):
        top = even if n == 0 else jnp.logical_not(even)
        near, next_ = jnp.where(top, LEV - 1, 0), jnp.where(top, LEV - 2, 1)
        ghost = jnp.where(top, edges.high_z, edges.low_z)
        factor = jnp.where(top, edges.factors[5], edges.factors[4])
        return n, msg, jnp.where(top, 1, 0), near, next_, jnp.where(top, LEV, -1), ghost, factor

    unpack_z(from_a, halo_a)
    unpack_z(from_b, halo_b)
    sides = [side(0, halo_a), side(1, halo_b)]
    for n, msg, *_ in sides:
        edge_over[n, 0] = lanes_of(msg[STRIP], EDDY)
        edge_over[n, 1] = lanes_of(msg[STRIP], RATE)
    for n, msg, i, near, next_, over, ghost, factor in sides:
        eddy_near = jnp.concatenate([eddy[near], halo_rows[near, EDDY]], 0)
        for p in (FIELDS, *range(FIELDS)):
            v = msg[STRIP] * edge_over[n, 0] if p == FIELDS else msg[p] * msg[EDDY]
            v = jnp.where(ghost, factor * f0[near, p], edges.flux(v))
            fh[n, p] = v
            r, e = (edge_rate[near], edge_eddy[near]) if p == FIELDS else (rates[near], eddy_near)
            v = near1[i, p] + r * v
            an[n, p] = v
            gn[n, p] = edges.flux(v * e)
    prepare(edges, [(n, lambda n=n: fh[n, FIELDS]) for n in range(2)], ends, lateral)
    prepare(edges, [(2 + n, lambda n=n: gn[n, FIELDS]) for n in range(2)], ends, lateral)

    def over_level(n, msg, i, near, next_, over, ghost, factor):
        def store(p, v):
            v = edges.flux(v * (edge_over[n, 0] if p == FIELDS else msg[EDDY]))
            gh[n, p] = jnp.where(ghost, factor * gn[n, p], v)

        return Level(
            lambda p: fh[n, p],
            lambda p: msg[9 + p] + f0[near, p],
            lambda p: msg[STRIP if p == FIELDS else p],
            lambda: msg[RATE],
            lambda: edge_over[n, 1],
            lambda: ends[n],
            lambda: lateral[n],
            store,
            src,
            flag_of(over),
        )

    def near_level(n, msg, i, near, next_, over, ghost, factor):
        def store(p, v):
            a2[n, p] = v

        return Level(
            lambda p: gn[n, p],
            lambda p: gh[n, p] + f1[next_, p],
            lambda p: an[n, p],
            lambda: rates[near],
            lambda: edge_rate[near],
            lambda: ends[2 + n],
            lambda: lateral[2 + n],
            store,
            src,
            flag_of(near),
        )

    sweep([over_level(*s) for s in sides], table)
    for n, msg, i, near, next_, over, ghost, factor in sides:

        def after(p):
            return next2[i, p] + (edge_rate[next_] if p == FIELDS else rates[next_]) * gn[n, p]

        level_sums(next_, info, after, after(FIELDS), strip, metric, metric_row, sums, levels, 2 * n)
        leave(levels.at[:, 2 * n], 4 + 2 * n, next_)
    sweep([near_level(*s) for s in sides], table)
    for n, msg, i, near, *_ in sides:
        level_sums(near, info, lambda f: a2[n, f], a2[n, FIELDS], strip, metric, metric_row, sums, levels, 2 * n + 1)
        leave(levels.at[:, 2 * n + 1], 5 + 2 * n, near)

    s1 = sums[1]
    stream = roll(s1, -1, 0)[:ROWS] - roll(s1, 1, 0)[:ROWS]
    t = sums[3, :ROWS]
    s2 = sums[2, :ROWS]
    lane = iota((ROWS, COLS), 1)
    right, left = roll(s2, -1, 1), roll(s2, 1, 1)
    high = [roll(t, COLS - 1 - (SLOT * f + 12), 1) for f in range(FIELDS)]
    low = [roll(t, -(SLOT * f + 3), 1) for f in range(FIELDS)]
    right = jnp.where(lane == COLS - 1, (high[0] + high[1] + high[2]) + (high[3] + high[4] + high[5]), right)
    left = jnp.where(lane == 0, (low[0] + low[1] + low[2]) + (low[3] + low[4] + low[5]), left)
    total = sums[0, :ROWS] - 0.5 * stream - 0.5 * (right - left)
    turned = jnp.concatenate([total, jnp.zeros((COLS - ROWS, COLS), jnp.float32)], 0).T
    for k in range(share.shape[0]):
        share[k] = turned[share.shape[1] * k : share.shape[1] * (k + 1)]
    for copy in copies:
        copy.wait()


def add_shares(parts, out):
    total = parts[0]
    for i in range(1, parts.shape[0]):
        total = total + parts[i]
    out[...] = total[:, :ROWS]


def call(body, outs, ins, scratch=(), places=None):
    return pl.pallas_call(
        body,
        out_shape=outs,
        in_specs=ins,
        out_specs=jax.tree.map(lambda _: VM, outs) if places is None else places,
        scratch_shapes=list(scratch),
        compiler_params=pltpu.CompilerParams(vmem_limit_bytes=16 << 20),
        cost_estimate=pl.CostEstimate(flops=1000000, bytes_accessed=1 << 20, transcendentals=0),
    )


def local(adjoint_start, eddy_visc, diag_coef, coupling, metric_terms, sample_cells, sample_weights, face_codes):
    slices = lax.axis_size("gz")
    cells, weights = sample_cells.reshape(16, 128), sample_weights.reshape(16, 128)

    def trade(v, axis, first):
        n = lax.axis_size(axis)
        pairs = [(i, i + 1) for i in range(first, n - 1, 2)]
        return lax.ppermute(v, axis, pairs + [(b, a) for a, b in pairs])

    def buf(*shape):
        return pltpu.VMEM(shape, jnp.float32)

    level = (LEV, ROWS, COLS)
    own, msg_a, msg_b = call(
        pack_y,
        (f32(*level), f32(2, ROWS, COLS), f32(2, ROWS, COLS)),
        [VM] * 4,
        [buf(*level)],
    )(adjoint_start, eddy_visc, diag_coef, metric_terms[2:3])
    beside = trade(msg_b, "gy", 1), trade(msg_a, "gy", 0)
    strip, msg_a, msg_b = call(pack_x, (f32(*level),) * 3, [VM] * 7, [buf(*level)] * 2)(
        own, *beside, adjoint_start, eddy_visc, diag_coef, metric_terms
    )
    beside = trade(msg_b, "gx", 1), trade(msg_a, "gx", 0)
    src, table = call(
        make_source, (f32(2, EXT, COLS), f32(56, COLS)), [SM] * 2 + [VM] * 3
    )(face_codes, coupling, cells, weights, strip)
    received = (*beside, adjoint_start, eddy_visc, diag_coef)
    msg_b, msg_a = [
        call(functools.partial(pack_z, far), f32(MESSAGE, COLS), [VM] * 7)(table, strip, *received)
        for far in (True, False)
    ]
    from_b = trade(msg_b, "gz", 1)
    from_a = trade(msg_a, "gz", 0)
    ext = (EXT, COLS)
    inner = call(
        inner_levels,
        (
            f32(LEV, 7, *ext),
            f32(2, 7, *ext),
            f32(2, 7, *ext),
            f32(LEV, 7, *ext),
            f32(LEV, *ext),
            f32(LEV, *ext),
            f32(LEV, *ext),
            f32(FIELDS, LEV - 4, ROWS, COLS),
            f32(4, *ext),
            f32(LEV, 9, 8, COLS),
            f32(FIELDS, LEV, 8, COLS),
        ),
        [VM] * 9,
        [buf(LEV, 7, *ext), buf(LEV, 7, *ext), buf(LEV, *ext), buf(LEV, *ext)],
    )(table, adjoint_start, eddy_visc, diag_coef, strip, *beside, metric_terms, src)
    adjoint, share = call(
        outer_levels,
        (f32(FIELDS, *level), f32(slices, COLS // slices, COLS)),
        [VM] * 18,
        [buf(FIELDS, 4, ROWS, COLS), pltpu.SemaphoreType.DMA((8,)), buf(4, *ext), buf(16, *ext), buf(16, *ext)] + [buf(2, 7, *ext)] * 5 + [buf(2, 2, *ext), buf(4, *ext), buf(4, *ext)],
        (pl.BlockSpec(memory_space=pl.ANY), VM),
    )(table, eddy_visc, strip, from_b, from_a, metric_terms, src, *inner)
    parts = lax.all_to_all(share, "gz", 0, 0, tiled=True)
    height_grad = call(add_shares, f32(COLS // slices, ROWS), [VM])(parts).T
    return (adjoint, height_grad)


def solution(mesh):
    return jax.shard_map(
        local,
        mesh=mesh,
        in_specs=(
            P(None, "gz", "gx", "gy"),
            P("gz", "gx", "gy"),
            P("gz", "gx", "gy"),
            P(),
            P(None, None, "gz", "gx", "gy"),
            P(),
            P(),
            P(),
        ),
        out_specs=(P(None, "gz", "gx", "gy"), P("gx", ("gy", "gz"))),
        check_vma=False,
    )
```
